256 devices in a mesh: space: 8 (over y, x_hi), orb: 32 (over x_lo, z, core).
Axes of the slice: x: 4 (x_hi: 2, x_lo: 2; x = x_hi * 2 + x_lo), y: 4, z: 8, core: 2. Of those that a mesh axis runs over, the one named last changes fastest.
Arguments:
- orbitals: float32 [32, 16, 32, 4096], P('space', None, None, 'orb'), may hold values from -6 to 6
- potential: float32 [32, 16, 32], P('space'), may hold values from 0 to 2
Outputs:
- updated: float32 [32, 16, 32, 4096], P('space', None, None, 'orb')
The draws below stay inside these ranges and needn't reach their ends.
All inputs are finite; a program needn't handle non-finite values.
Results may differ from the reference program's by a relative error of at most 0.00007.
Values sent between devices are 32-bit elements; how exact they have to be, the bound alone decides.
No kernel may reach another device: no remote copies, remote signals or barrier semaphores. Data moves between devices by JAX's collectives and lax.ppermute only.
A program may use at most 64 MiB of HBM per device.

```python
import jax
import jax.numpy as jnp
from jax import lax

NY = 16
NZ = 32
ORB_DEV = 128
PANEL = 512
DEGREE = 4
NX = 32
ORBS = 4096
PANEL_DEV = 16
N_ORB = 32


def levels(own_key, dims, split, low, largest):
    def one(dim, parts):
        steps = jax.random.uniform(jax.random.fold_in(jax.random.fold_in(own_key, 6), dim), (parts,), jnp.float32, low / len(split), largest / len(split))
        return jnp.repeat(jnp.exp(steps), dims[dim] // parts).reshape((-1,) + (1,) * (len(dims) - dim - 1))

    loudness = one(*split[0])
    for cut in split[1:]:
        loudness = loudness * one(*cut)
    return loudness


def bell_draw(own_key, shape, spread, most, shards=(), held_as=jnp.bfloat16):
    values = spread * jax.random.normal(own_key, shape, jnp.float32)
    if shards:
        values = values * levels(own_key, shape, shards, -0.22, 0.18)
    return jnp.clip(values, -most, most).astype(held_as)


def setup_inputs(seed: int = 0) -> dict:
    keys = jax.random.split(jax.random.key(seed), 3)
    return {
        "orbitals": bell_draw(keys[0], (NX, NY, NZ, ORBS), 1.0, 6.0, ((0, 8), (3, 32)), jnp.float32),
        "potential": jnp.clip(2.0 * jax.random.uniform(keys[1], (NX, NY, NZ), jnp.float32) ** levels(keys[1], (NX, NY, NZ), ((0, 8),), -0.2, 0.2), 0.0, 2.0),
    }


STENCIL = (-205.0 / 72.0, 8.0 / 5.0, -1.0 / 5.0, 8.0 / 315.0, -1.0 / 560.0)
SHIFT_MID = 7.25
HALF_WIDTH = 4.75

def hamilton(field, potential):
    laplace = 3.0 * STENCIL[0] * field
    for axis in range(3):
        for offset in range(1, 5):
            laplace = laplace + STENCIL[offset] * (jnp.roll(field, offset, axis) + jnp.roll(field, -offset, axis))
    return -0.5 * laplace + potential[..., None] * field

def chebyshev(block, potential):
    before = block
    current = (hamilton(block, potential) - SHIFT_MID * block) / HALF_WIDTH
    for order in range(DEGREE - 1):
        following = 2.0 * (hamilton(current, potential) - SHIFT_MID * current) / HALF_WIDTH - before
        before, current = (current, following)
    return current

def reference(orbitals, potential):
    points = NX * NY * NZ
    trail = ORB_DEV - PANEL_DEV
    blocks = jnp.moveaxis(orbitals.reshape(NX, NY, NZ, N_ORB, ORB_DEV), 3, 0)
    filtered = lax.map(lambda block: chebyshev(block, potential), blocks)
    panel = jnp.moveaxis(filtered[..., :PANEL_DEV], 0, 3).reshape(points, PANEL)
    trailing = jnp.moveaxis(filtered[..., PANEL_DEV:], 0, 3).reshape(points, N_ORB * trail)
    highest = lax.Precision.HIGHEST
    gram_full = jnp.dot(panel.T, panel, precision=highest) / points
    coupling = jnp.dot(panel.T, trailing, precision=highest) / points
    lower_factor = jnp.linalg.cholesky(gram_full)
    identity = jnp.eye(PANEL, dtype=jnp.float32)
    inverse = lax.linalg.triangular_solve(lower_factor, identity, left_side=True, lower=True)
    ortho = jnp.dot(panel, inverse.T, precision=highest)
    middle = jnp.dot(inverse, coupling, precision=highest)
    project = jnp.dot(inverse.T, middle, precision=highest)
    trailing_new = trailing - jnp.dot(panel, project, precision=highest)
    joined = jnp.concatenate([ortho.reshape(points, N_ORB, PANEL_DEV), trailing_new.reshape(points, N_ORB, trail)], axis=2)
    return joined.reshape(NX, NY, NZ, N_ORB * ORB_DEV)
```

```python
import functools

import jax
import jax.numpy as jnp
from jax import lax
from jax.experimental import pallas as pl
from jax.experimental.pallas import tpu as pltpu
from jax.sharding import Mesh, PartitionSpec as P

PANEL = 512
C0, C1, C2, C3, C4 = (-205.0 / 72.0, 8.0 / 5.0, -1.0 / 5.0, 8.0 / 315.0, -1.0 / 560.0)
SHIFT_MID = 7.25
HALF_WIDTH = 4.75
POINTS = 16384.0
SPACE = ("y", "xh")
HI = lax.Precision.HIGHEST
MIB = 1024 * 1024


def dot_nn(a, b):
    return lax.dot_general(a, b, (((1,), (0,)), ((), ())), precision=HI, preferred_element_type=jnp.float32)


def dot_nt(a, b):
    return lax.dot_general(a, b, (((1,), (1,)), ((), ())), precision=HI, preferred_element_type=jnp.float32)


def dot_tn(a, b):
    return lax.dot_general(a, b, (((0,), (0,)), ((), ())), precision=HI, preferred_element_type=jnp.float32)


def swap_groups(arrays):
    arrays = list(arrays)
    group = lax.broadcasted_iota(jnp.int32, arrays[0].shape, 1) // 16
    for bit in (1, 2, 4):
        high = (group & bit) != 0
        for i in range(8):
            if i & bit:
                continue
            a, d = arrays[i], arrays[i | bit]
            arrays[i] = jnp.where(high, pltpu.roll(d, 16 * bit, 1), a)
            arrays[i | bit] = jnp.where(high, d, pltpu.roll(a, 128 - 16 * bit, 1))
    return arrays


def pack_kernel(orb_ref, pot_ref, out_ref):
    def body(step, _):
        xp, yh = step // 2, step % 2
        parts = swap_groups([orb_ref[xp, yh * 8 + yl] for yl in range(8)])
        for g in range(8):
            out_ref[g, pl.ds(step * 32, 32), :] = parts[g]
        return 0

    lax.fori_loop(0, 8, body, 0)
    packed = jnp.concatenate([pot_ref[xp] for xp in range(4)], axis=1)
    for g in range(8):
        out_ref[g, 256:272, :] = packed


def pack(orbitals, potential):
    return pl.pallas_call(
        pack_kernel,
        out_shape=jax.ShapeDtypeStruct((8, 272, 128), jnp.float32),
        compiler_params=pltpu.CompilerParams(vmem_limit_bytes=8 * MIB),
    )(orbitals, potential)


def filter_kernel(in_ref, out_ref, weight, buf_a, buf_b):
    scale = 2.0 / HALF_WIDTH
    centre = (-1.5 * C0 - SHIFT_MID) * scale
    side = [-0.5 * c * scale for c in (C1, C2, C3, C4)]
    y_of = lax.broadcasted_iota(jnp.int32, (16, 256), 0)
    lane_y = lax.broadcasted_iota(jnp.int32, (16, 256), 1) // 16
    spread = jnp.where(y_of == lane_y, 1.0, 0.0).astype(jnp.float32)
    for s in range(8):
        wide = dot_tn(in_ref[s, 256:272, :], spread) * scale + centre
        for xp in range(4):
            for yh in range(2):
                weight[4 * s + xp, yh] = wide[xp * 32 : xp * 32 + 32, yh * 128 : yh * 128 + 128]
    lane = lax.broadcasted_iota(jnp.int32, (32, 128), 1)

    def plane_of_input(x, yh):
        return in_ref[x // 4, pl.ds((x % 4) * 64 + yh * 32, 32), :]

    def apply(read, x):
        near = [read(x, yh) for yh in range(2)]
        total = [weight[x, yh] * near[yh] for yh in range(2)]
        for m in range(1, 5):
            up, down = (x + m) & 31, (x + 32 - m) & 31
            forth = [pltpu.roll(near[yh], 16 * m, 1) for yh in range(2)]
            back = [pltpu.roll(near[yh], 128 - 16 * m, 1) for yh in range(2)]
            low, top = lane < 16 * m, lane >= 128 - 16 * m
            for yh in range(2):
                along_x = read(up, yh) + read(down, yh)
                along_y = jnp.where(low, forth[1 - yh], forth[yh]) + jnp.where(top, back[1 - yh], back[yh])
                along_z = pltpu.roll(near[yh], m, 0) + pltpu.roll(near[yh], 32 - m, 0)
                total[yh] = total[yh] + side[m - 1] * (along_x + along_y + along_z)
        return total

    def first(x, _):
        total = apply(plane_of_input, x)
        for yh in range(2):
            buf_a[x, yh] = 0.5 * total[yh]
        return 0

    def second(x, _):
        total = apply(lambda p, yh: buf_a[p, yh], x)
        for yh in range(2):
            buf_b[x, yh] = total[yh] - plane_of_input(x, yh)
        return 0

    def third(x, _):
        total = apply(lambda p, yh: buf_b[p, yh], x)
        for yh in range(2):
            out_ref[x, yh] = total[yh] - buf_a[x, yh]
        return 0

    def fourth(x, _):
        total = apply(lambda p, yh: out_ref[p, yh], x)
        for yh in range(2):
            buf_a[x, yh] = total[yh] - buf_b[x, yh]
        return 0

    def move(x, _):
        out_ref[x] = buf_a[x]
        return 0

    for step in (first, second, third, fourth, move):
        lax.fori_loop(0, 32, step, 0)


def chebyshev(received):
    out = pl.pallas_call(
        filter_kernel,
        out_shape=jax.ShapeDtypeStruct((32, 2, 32, 128), jnp.float32),
        scratch_shapes=[pltpu.VMEM((32, 2, 32, 128), jnp.float32)] * 3,
        compiler_params=pltpu.CompilerParams(vmem_limit_bytes=16 * MIB),
    )(received)
    return out.reshape(8, 256, 128)


def unpack_kernel(in_ref, out_ref):
    def body(step, _):
        xp, yh = step // 2, step % 2
        parts = swap_groups([in_ref[g, pl.ds(step * 32, 32), :] for g in range(8)])
        for yl in range(8):
            out_ref[pl.ds((xp * 16 + yh * 8 + yl) * 32, 32), :] = parts[yl]
        return 0

    lax.fori_loop(0, 8, body, 0)


def unpack(back):
    return pl.pallas_call(
        unpack_kernel,
        out_shape=jax.ShapeDtypeStruct((2048, 128), jnp.float32),
        compiler_params=pltpu.CompilerParams(vmem_limit_bytes=8 * MIB),
    )(back)


def ring(count, step):
    return [(i, (i + step) % count) for i in range(count)]


def gather_panel(own):
    other = lax.ppermute(own, "xl", ring(2, 1))
    pair = jnp.concatenate([own, other], axis=0)
    found = [pair]
    right = left = pair
    for _ in range(3):
        right = lax.ppermute(right, "z", ring(8, 1))
        left = lax.ppermute(left, "z", ring(8, -1))
        found += [right, left]
    far = jnp.concatenate([lax.ppermute(right[:256], "z", ring(8, 1)), lax.ppermute(left[256:], "z", ring(8, -1))], axis=0)
    found.append(far)
    return found + [lax.ppermute(block, "c", ring(2, 1)) for block in found]


OFFSETS = (0, -1, 1, -2, 2, -3, 3, 4)


def products_kernel(place_ref, *refs):
    blocks, (field_ref, panel_ref, out_ref, order) = refs[:16], refs[16:]
    xl, z, core = place_ref[0], place_ref[1], place_ref[2]
    for other in range(2):
        for k, offset in enumerate(OFFSETS):
            for xo in range(2):
                owner = (xl ^ xo) * 16 + ((z + offset) & 7) * 2 + (core ^ other)
                order[owner] = blocks[other * 8 + k][xo * 256 : xo * 256 + 256, :]
    for group in range(4):

        def body(step, _, group=group):
            xp, yh = step // 2, step % 2
            parts = swap_groups([order[group * 8 + q, pl.ds(step * 32, 32), :] for q in range(8)])
            for yl in range(8):
                panel_ref[pl.ds((xp * 16 + yh * 8 + yl) * 32, 32), group * 128 : group * 128 + 128] = parts[yl]
            return 0

        lax.fori_loop(0, 8, body, 0)
    column = pl.multiple_of((xl * 2 + core) * 128, 128)
    out_ref[...] = jnp.zeros_like(out_ref)

    def chunk(i, _):
        rows = pl.ds(i * 512, 512)
        wide = panel_ref[rows, :]
        out_ref[0:128, :] += dot_tn(panel_ref[rows, pl.ds(column, 128)], wide)
        out_ref[128:256, :] += dot_tn(field_ref[rows, :], wide)
        return 0

    lax.fori_loop(0, 4, chunk, 0)


def products(place, blocks, field):
    return pl.pallas_call(
        products_kernel,
        in_specs=[pl.BlockSpec(memory_space=pltpu.SMEM)] + [pl.BlockSpec(memory_space=pltpu.VMEM)] * 17,
        out_shape=(jax.ShapeDtypeStruct((2048, 512), jnp.float32), jax.ShapeDtypeStruct((256, 512), jnp.float32)),
        scratch_shapes=[pltpu.VMEM((32, 256, 128), jnp.float32)],
        compiler_params=pltpu.CompilerParams(vmem_limit_bytes=28 * MIB),
    )(place, *blocks, field)


def eliminate(block):
    rows = lax.broadcasted_iota(jnp.int32, (8, 128), 0)
    lanes = lax.broadcasted_iota(jnp.int32, (8, 128), 1)
    left = [block[8 * t : 8 * t + 8, :] for t in range(16)]
    right = [jnp.where(lanes == rows + 8 * t, 1.0, 0.0).astype(jnp.float32) for t in range(16)]
    for j in range(128):
        t0, i = j // 8, j % 8
        column = jnp.broadcast_to(left[t0][:, j : j + 1], (8, 128))
        inverse = 1.0 / jnp.broadcast_to(column[i : i + 1, :], (8, 128))
        row_l = jnp.broadcast_to(left[t0][i : i + 1, :], (8, 128)) * inverse
        row_r = jnp.broadcast_to(right[t0][i : i + 1, :], (8, 128)) * inverse
        for t in range(t0, 16):
            if t == t0:
                if i == 7:
                    continue
                factor = jnp.where(rows > i, column, 0.0)
            else:
                factor = jnp.broadcast_to(left[t][:, j : j + 1], (8, 128))
            left[t] = left[t] - factor * row_l
            right[t] = right[t] - factor * row_r
    out = []
    for t in range(16):
        pivot = jnp.sum(jnp.where(lanes == rows + 8 * t, left[t], 0.0), axis=1, keepdims=True)
        root = lax.rsqrt(pivot)
        root = root * (1.5 - 0.5 * pivot * root * root)
        out.append(right[t] * root)
    return jnp.concatenate(out, axis=0)


def inverse_kernel(gram_ref, inv_ref, work):
    work[...] = gram_ref[...] * (1.0 / POINTS)
    inv_ref[...] = jnp.zeros_like(inv_ref)

    def diagonal(k, _):
        here = pl.ds(pl.multiple_of(k * 128, 128), 128)
        corner = eliminate(work[here, here])
        for kk in range(4):

            @pl.when(k == kk)
            def _(kk=kk, corner=corner):
                low, high = kk * 128, kk * 128 + 128
                if kk:
                    inv_ref[low:high, :low] = dot_nn(corner, inv_ref[low:high, :low])
                inv_ref[low:high, low:high] = corner
                if high < PANEL:
                    panel = dot_nt(work[high:, low:high], corner)
                    work[high:, high:] -= dot_nt(panel, panel)
                    inv_ref[high:, :high] -= dot_nn(panel, inv_ref[low:high, :high])

        return 0

    lax.fori_loop(0, 4, diagonal, 0)


def inverse_factor(gram):
    return pl.pallas_call(
        inverse_kernel,
        out_shape=jax.ShapeDtypeStruct((PANEL, PANEL), jnp.float32),
        scratch_shapes=[pltpu.VMEM((PANEL, PANEL), jnp.float32)],
        compiler_params=pltpu.CompilerParams(vmem_limit_bytes=16 * MIB),
    )(gram)


def update_kernel(own_ref, inv_ref, coupling_ref, panel_ref, field_ref, out_ref, mixer):
    inverse = inv_ref[...]
    middle = dot_nt(coupling_ref[...] * (1.0 / POINTS), inverse)
    mixer[...] = -dot_nn(middle, inverse)
    start = pl.multiple_of(own_ref[0] * 16, 16)
    mixer[0:16, :] = inv_ref[pl.ds(start, 16), :]

    def chunk(i, _):
        rows = pl.ds(i * 512, 512)
        keep = lax.broadcasted_iota(jnp.int32, (512, 128), 1) >= 16
        base = jnp.where(keep, field_ref[rows, :], 0.0)
        out_ref[rows, :] = base + dot_nt(panel_ref[rows, :], mixer[...])
        return 0

    lax.fori_loop(0, 4, chunk, 0)


def update(own, inverse, coupling, panel, field):
    return pl.pallas_call(
        update_kernel,
        in_specs=[pl.BlockSpec(memory_space=pltpu.SMEM)] + [pl.BlockSpec(memory_space=pltpu.VMEM)] * 4,
        out_shape=jax.ShapeDtypeStruct((2048, 128), jnp.float32),
        scratch_shapes=[pltpu.VMEM((128, PANEL), jnp.float32)],
        compiler_params=pltpu.CompilerParams(vmem_limit_bytes=28 * MIB),
    )(own, inverse, coupling, panel, field)


def per_device(orbitals, potential):
    xl, z, core = lax.axis_index("xl"), lax.axis_index("z"), lax.axis_index("c")
    place = jnp.stack([xl, z, core]).astype(jnp.int32)
    received = lax.all_to_all(pack(orbitals, potential), SPACE, 0, 0, tiled=True)
    back = lax.all_to_all(chebyshev(received), SPACE, 0, 0, tiled=True)
    field = unpack(back)
    panel, terms = products(place, gather_panel(back[0]), field)
    terms = terms.reshape(2, 8, 16, PANEL).swapaxes(0, 1)
    mine = jnp.sum(lax.all_to_all(terms, SPACE, 0, 0, tiled=True), axis=0)
    full = lax.all_to_all(jnp.broadcast_to(mine, (8, 2, 16, PANEL)), SPACE, 0, 0, tiled=True)
    piece, coupling = full[:, 0].reshape(128, PANEL), full[:, 1].reshape(128, PANEL)
    by_core = lax.ppermute(piece, "c", ring(2, 1))
    low = jnp.where(core == 0, piece, by_core)
    high = jnp.where(core == 0, by_core, piece)
    half = jnp.concatenate([low, high], axis=0)
    by_x = lax.ppermute(half, "xl", ring(2, 1))
    gram = jnp.concatenate([jnp.where(xl == 0, half, by_x), jnp.where(xl == 0, by_x, half)], axis=0)
    inverse = inverse_factor(gram)
    own = (xl * 16 + z * 2 + core).astype(jnp.int32).reshape(1)
    return update(own, inverse, coupling, panel, field).reshape(4, 16, 32, 128)


def solution(mesh):
    fine = Mesh(mesh.devices.reshape(4, 2, 2, 8, 2), ("y", "xh", "xl", "z", "c"))
    return jax.shard_map(
        per_device,
        mesh=fine,
        in_specs=(P(SPACE, None, None, ("xl", "z", "c")), P(SPACE, None, None)),
        out_specs=P(SPACE, None, None, ("xl", "z", "c")),
        check_vma=False,
    )
```

```python
import functools

import jax
import jax.numpy as jnp
from jax import lax
from jax.experimental import pallas as pl
from jax.experimental.pallas import tpu as pltpu
from jax.sharding import Mesh, PartitionSpec as P

PANEL = 512
C0, C1, C2, C3, C4 = (-205.0 / 72.0, 8.0 / 5.0, -1.0 / 5.0, 8.0 / 315.0, -1.0 / 560.0)
SHIFT_MID = 7.25
HALF_WIDTH = 4.75
POINTS = 16384.0
SPACE = ("y", "xh")
HI = lax.Precision.HIGHEST
MIB = 1024 * 1024


def dot_nn(a, b):
    return lax.dot_general(a, b, (((1,), (0,)), ((), ())), precision=HI, preferred_element_type=jnp.float32)


def dot_nt(a, b):
    return lax.dot_general(a, b, (((1,), (1,)), ((), ())), precision=HI, preferred_element_type=jnp.float32)


def dot_tn(a, b):
    return lax.dot_general(a, b, (((0,), (0,)), ((), ())), precision=HI, preferred_element_type=jnp.float32)


def swap_groups(arrays):
    arrays = list(arrays)
    group = lax.broadcasted_iota(jnp.int32, arrays[0].shape, 1) // 16
    for bit in (1, 2, 4):
        high = (group & bit) != 0
        for i in range(8):
            if i & bit:
                continue
            a, d = arrays[i], arrays[i | bit]
            arrays[i] = jnp.where(high, pltpu.roll(d, 16 * bit, 1), a)
            arrays[i | bit] = jnp.where(high, d, pltpu.roll(a, 128 - 16 * bit, 1))
    return arrays


def pack_kernel(orb_ref, pot_ref, out_ref):
    def body(step, _):
        xp, yh = step // 2, step % 2
        parts = swap_groups([orb_ref[xp, yh * 8 + yl] for yl in range(8)])
        for g in range(8):
            out_ref[g, pl.ds(step * 32, 32), :] = parts[g]
        return 0

    lax.fori_loop(0, 8, body, 0)
    packed = jnp.concatenate([pot_ref[xp] for xp in range(4)], axis=1)
    for g in range(8):
        out_ref[g, 256:272, :] = packed


def pack(orbitals, potential):
    return pl.pallas_call(
        pack_kernel,
        out_shape=jax.ShapeDtypeStruct((8, 272, 128), jnp.float32),
        compiler_params=pltpu.CompilerParams(vmem_limit_bytes=8 * MIB),
    )(orbitals, potential)


def roll_y(pair, places, lane):
    shift = 16 * places % 128
    turned = [pltpu.roll(half, shift, 1) for half in pair]
    wraps = lane < shift if places > 0 else lane >= shift
    return [jnp.where(wraps, turned[1], turned[0]), jnp.where(wraps, turned[0], turned[1])]


def filter_kernel(in_ref, out_ref, weight, buf_a, buf_b):
    scale = 2.0 / HALF_WIDTH
    centre = (-1.5 * C0 - SHIFT_MID) * scale
    side = [-0.5 * c * scale for c in (C1, C2, C3, C4)]
    y_of = lax.broadcasted_iota(jnp.int32, (16, 256), 0)
    lane_y = lax.broadcasted_iota(jnp.int32, (16, 256), 1) // 16
    spread = jnp.where(y_of == lane_y, 1.0, 0.0).astype(jnp.float32)
    for s in range(8):
        wide = dot_tn(in_ref[s, 256:272, :], spread) * scale + centre
        for xp in range(4):
            for yh in range(2):
                weight[8 * s + 2 * xp + yh] = wide[xp * 32 : xp * 32 + 32, yh * 128 : yh * 128 + 128]
    lane = lax.broadcasted_iota(jnp.int32, (32, 128), 1)

    def put(ref, plane, value):
        ref[plane, 8:40, :] = value
        ref[plane, 4:8, :] = value[28:32, :]
        ref[plane, 40:44, :] = value[0:4, :]

    def take(plane, _):
        put(buf_b, plane, in_ref[plane // 8, pl.ds((plane % 8) * 32, 32), :])
        return 0

    def apply(ref, x):
        near = [ref[2 * x + yh, 8:40, :] for yh in range(2)]
        total = [weight[2 * x + yh] * near[yh] for yh in range(2)]
        for m in range(1, 5):
            up, down = 2 * ((x + m) & 31), 2 * ((x + 32 - m) & 31)
            for yh in range(2):
                along_x = ref[up + yh, 8:40, :] + ref[down + yh, 8:40, :]
                along_z = ref[2 * x + yh, 8 - m : 40 - m, :] + ref[2 * x + yh, 8 + m : 40 + m, :]
                total[yh] = total[yh] + side[m - 1] * (along_x + along_z)
        forth, back = roll_y(near, 1, lane), roll_y(near, -1, lane)
        ahead = [side[1] * back[yh] + side[2] * near[yh] + side[3] * forth[yh] for yh in range(2)]
        behind = [side[1] * forth[yh] + side[2] * near[yh] + side[3] * back[yh] for yh in range(2)]
        ahead, behind = roll_y(ahead, 3, lane), roll_y(behind, -3, lane)
        return [total[yh] + (side[0] * (forth[yh] + back[yh]) + (ahead[yh] + behind[yh])) for yh in range(2)]

    def first(x, _):
        for yh, total in enumerate(apply(buf_b, x)):
            put(buf_a, 2 * x + yh, 0.5 * total)
        return 0

    def second(x, _):
        for yh, total in enumerate(apply(buf_a, x)):
            put(buf_b, 2 * x + yh, total - buf_b[2 * x + yh, 8:40, :])
        return 0

    def third(x, _):
        for yh, total in enumerate(apply(buf_b, x)):
            put(buf_a, 2 * x + yh, total - buf_a[2 * x + yh, 8:40, :])
        return 0

    def fourth(x, _):
        for yh, total in enumerate(apply(buf_a, x)):
            out_ref[2 * x + yh] = total - buf_b[2 * x + yh, 8:40, :]
        return 0

    lax.fori_loop(0, 64, take, 0, unroll=4)
    for step in (first, second, third, fourth):
        lax.fori_loop(0, 32, step, 0, unroll=4)


def chebyshev(received):
    out = pl.pallas_call(
        filter_kernel,
        out_shape=jax.ShapeDtypeStruct((64, 32, 128), jnp.float32),
        scratch_shapes=[pltpu.VMEM((64, 32, 128), jnp.float32)] + [pltpu.VMEM((64, 48, 128), jnp.float32)] * 2,
        compiler_params=pltpu.CompilerParams(vmem_limit_bytes=16 * MIB),
    )(received)
    return out.reshape(8, 256, 128)


def unpack_kernel(in_ref, out_ref):
    def body(step, _):
        xp, yh = step // 2, step % 2
        parts = swap_groups([in_ref[g, pl.ds(step * 32, 32), :] for g in range(8)])
        for yl in range(8):
            out_ref[pl.ds((xp * 16 + yh * 8 + yl) * 32, 32), :] = parts[yl]
        return 0

    lax.fori_loop(0, 8, body, 0)


def unpack(back):
    return pl.pallas_call(
        unpack_kernel,
        out_shape=jax.ShapeDtypeStruct((2048, 128), jnp.float32),
        compiler_params=pltpu.CompilerParams(vmem_limit_bytes=8 * MIB),
    )(back)


def ring(count, step):
    return [(i, (i + step) % count) for i in range(count)]


def gather_panel(own):
    other = lax.ppermute(own, "xl", ring(2, 1))
    pair = jnp.concatenate([own, other], axis=0)
    found = [pair]
    right = left = pair
    for _ in range(3):
        right = lax.ppermute(right, "z", ring(8, 1))
        left = lax.ppermute(left, "z", ring(8, -1))
        found += [right, left]
    far = jnp.concatenate([lax.ppermute(right[:256], "z", ring(8, 1)), lax.ppermute(left[256:], "z", ring(8, -1))], axis=0)
    found.append(far)
    return found + [lax.ppermute(block, "c", ring(2, 1)) for block in found]


OFFSETS = (0, -1, 1, -2, 2, -3, 3, 4)


def products_kernel(place_ref, *refs):
    blocks, (field_ref, panel_ref, out_ref, order) = refs[:16], refs[16:]
    xl, z, core = place_ref[0], place_ref[1], place_ref[2]
    for other in range(2):
        for k, offset in enumerate(OFFSETS):
            for xo in range(2):
                owner = (xl ^ xo) * 16 + ((z + offset) & 7) * 2 + (core ^ other)
                order[owner] = blocks[other * 8 + k][xo * 256 : xo * 256 + 256, :]
    for group in range(4):

        def body(step, _, group=group):
            xp, yh = step // 2, step % 2
            parts = swap_groups([order[group * 8 + q, pl.ds(step * 32, 32), :] for q in range(8)])
            for yl in range(8):
                panel_ref[pl.ds((xp * 16 + yh * 8 + yl) * 32, 32), group * 128 : group * 128 + 128] = parts[yl]
            return 0

        lax.fori_loop(0, 8, body, 0)
    column = pl.multiple_of((xl * 2 + core) * 128, 128)
    out_ref[...] = jnp.zeros_like(out_ref)

    def chunk(i, _):
        rows = pl.ds(i * 512, 512)
        wide = panel_ref[rows, :]
        out_ref[0:128, :] += dot_tn(panel_ref[rows, pl.ds(column, 128)], wide)
        out_ref[128:256, :] += dot_tn(field_ref[rows, :], wide)
        return 0

    lax.fori_loop(0, 4, chunk, 0)


def products(place, blocks, field):
    return pl.pallas_call(
        products_kernel,
        in_specs=[pl.BlockSpec(memory_space=pltpu.SMEM)] + [pl.BlockSpec(memory_space=pltpu.VMEM)] * 17,
        out_shape=(jax.ShapeDtypeStruct((2048, 512), jnp.float32), jax.ShapeDtypeStruct((256, 512), jnp.float32)),
        scratch_shapes=[pltpu.VMEM((32, 256, 128), jnp.float32)],
        compiler_params=pltpu.CompilerParams(vmem_limit_bytes=28 * MIB),
    )(place, *blocks, field)


def total_of(terms):
    while len(terms) > 1:
        terms = [terms[i] + terms[i + 1] for i in range(0, len(terms), 2)]
    return terms[0]


def eliminate(block):
    rows = lax.broadcasted_iota(jnp.int32, (8, 128), 0)
    lanes = lax.broadcasted_iota(jnp.int32, (8, 128), 1)

    def spread_row(tile, i):
        return jnp.broadcast_to(tile[i : i + 1, :], (8, 128))

    def spread_lane(tile, j):
        return jnp.broadcast_to(tile[:, j : j + 1], (8, 128))

    left = [block[8 * t : 8 * t + 8, :] for t in range(16)]
    right = [jnp.where(lanes == rows + 8 * t, 1.0, 0.0).astype(jnp.float32) for t in range(16)]
    out = []
    for t0 in range(16):
        columns = [spread_lane(left[t0], 8 * t0 + j) for j in range(8)]
        corner = [[spread_row(columns[j], i) for j in range(i + 1)] for i in range(8)]
        row_l = [spread_row(left[t0], i) for i in range(8)]
        row_r = [spread_row(right[t0], i) for i in range(8)]
        inverse, factor = [None] * 8, [[None] * 8 for _ in range(8)]
        for j in range(8):
            inverse[j] = 1.0 / corner[j][j]
            for i in range(j + 1, 8):
                factor[i][j] = corner[i][j] * inverse[j]
            for i in range(j + 1, 8):
                for k in range(j + 1, i + 1):
                    corner[i][k] = corner[i][k] - factor[i][j] * corner[k][j]
                row_l[i] = row_l[i] - factor[i][j] * row_l[j]
                row_r[i] = row_r[i] - factor[i][j] * row_r[j]
        own, pivot = row_r[0], corner[0][0]
        for i in range(1, 8):
            own, pivot = jnp.where(rows == i, row_r[i], own), jnp.where(rows == i, corner[i][i], pivot)
        root = lax.rsqrt(pivot)
        root = root * (1.5 - 0.5 * pivot * root * root)
        out.append(own * root)
        if t0 == 15:
            break
        solved_l, solved_r = [None] * 8, [None] * 8
        for k in range(7, -1, -1):
            u, v = row_l[k] * inverse[k], row_r[k] * inverse[k]
            for i in range(7, k, -1):
                u, v = u - factor[i][k] * solved_l[i], v - factor[i][k] * solved_r[i]
            solved_l[k], solved_r[k] = u, v
        for t in range(t0 + 1, 16):
            weights = [spread_lane(left[t], 8 * t0 + j) for j in range(8)]
            left[t] = left[t] - total_of([weights[j] * solved_l[j] for j in range(8)])
            right[t] = right[t] - total_of([weights[j] * solved_r[j] for j in range(8)])
    return jnp.concatenate(out, axis=0)


def inverse_kernel(gram_ref, inv_ref, work):
    work[...] = gram_ref[...] * (1.0 / POINTS)
    inv_ref[...] = jnp.zeros_like(inv_ref)

    def diagonal(k, _):
        here = pl.ds(pl.multiple_of(k * 128, 128), 128)
        corner = eliminate(work[here, here])
        for kk in range(4):

            @pl.when(k == kk)
            def _(kk=kk, corner=corner):
                low, high = kk * 128, kk * 128 + 128
                if kk:
                    inv_ref[low:high, :low] = dot_nn(corner, inv_ref[low:high, :low])
                inv_ref[low:high, low:high] = corner
                if high < PANEL:
                    panel = dot_nt(work[high:, low:high], corner)
                    work[high:, high:] -= dot_nt(panel, panel)
                    inv_ref[high:, :high] -= dot_nn(panel, inv_ref[low:high, :high])

        return 0

    lax.fori_loop(0, 4, diagonal, 0)


def inverse_factor(gram):
    return pl.pallas_call(
        inverse_kernel,
        out_shape=jax.ShapeDtypeStruct((PANEL, PANEL), jnp.float32),
        scratch_shapes=[pltpu.VMEM((PANEL, PANEL), jnp.float32)],
        compiler_params=pltpu.CompilerParams(vmem_limit_bytes=16 * MIB),
    )(gram)


def update_kernel(own_ref, inv_ref, coupling_ref, panel_ref, field_ref, out_ref, mixer):
    inverse = inv_ref[...]
    middle = dot_nt(coupling_ref[...] * (1.0 / POINTS), inverse)
    mixer[...] = -dot_nn(middle, inverse)
    start = pl.multiple_of(own_ref[0] * 16, 16)
    mixer[0:16, :] = inv_ref[pl.ds(start, 16), :]

    def chunk(i, _):
        rows = pl.ds(i * 512, 512)
        keep = lax.broadcasted_iota(jnp.int32, (512, 128), 1) >= 16
        base = jnp.where(keep, field_ref[rows, :], 0.0)
        out_ref[rows, :] = base + dot_nt(panel_ref[rows, :], mixer[...])
        return 0

    lax.fori_loop(0, 4, chunk, 0)


def update(own, inverse, coupling, panel, field):
    return pl.pallas_call(
        update_kernel,
        in_specs=[pl.BlockSpec(memory_space=pltpu.SMEM)] + [pl.BlockSpec(memory_space=pltpu.VMEM)] * 4,
        out_shape=jax.ShapeDtypeStruct((2048, 128), jnp.float32),
        scratch_shapes=[pltpu.VMEM((128, PANEL), jnp.float32)],
        compiler_params=pltpu.CompilerParams(vmem_limit_bytes=28 * MIB),
    )(own, inverse, coupling, panel, field)


def per_device(orbitals, potential):
    xl, z, core = lax.axis_index("xl"), lax.axis_index("z"), lax.axis_index("c")
    place = jnp.stack([xl, z, core]).astype(jnp.int32)
    received = lax.all_to_all(pack(orbitals, potential), SPACE, 0, 0, tiled=True)
    back = lax.all_to_all(chebyshev(received), SPACE, 0, 0, tiled=True)
    field = unpack(back)
    panel, terms = products(place, gather_panel(back[0]), field)
    terms = terms.reshape(2, 8, 16, PANEL).swapaxes(0, 1)
    mine = jnp.sum(lax.all_to_all(terms, SPACE, 0, 0, tiled=True), axis=0)
    full = lax.all_to_all(jnp.broadcast_to(mine, (8, 2, 16, PANEL)), SPACE, 0, 0, tiled=True)
    piece, coupling = full[:, 0].reshape(128, PANEL), full[:, 1].reshape(128, PANEL)
    by_core = lax.ppermute(piece, "c", ring(2, 1))
    low = jnp.where(core == 0, piece, by_core)
    high = jnp.where(core == 0, by_core, piece)
    half = jnp.concatenate([low, high], axis=0)
    by_x = lax.ppermute(half, "xl", ring(2, 1))
    gram = jnp.concatenate([jnp.where(xl == 0, half, by_x), jnp.where(xl == 0, by_x, half)], axis=0)
    inverse = inverse_factor(gram)
    own = (xl * 16 + z * 2 + core).astype(jnp.int32).reshape(1)
    return update(own, inverse, coupling, panel, field).reshape(4, 16, 32, 128)


def solution(mesh):
    fine = Mesh(mesh.devices.reshape(4, 2, 2, 8, 2), ("y", "xh", "xl", "z", "c"))
    return jax.shard_map(
        per_device,
        mesh=fine,
        in_specs=(P(SPACE, None, None, ("xl", "z", "c")), P(SPACE, None, None)),
        out_specs=P(SPACE, None, None, ("xl", "z", "c")),
        check_vma=False,
    )
```

```python
import functools

import jax
import jax.numpy as jnp
from jax import lax
from jax.experimental import pallas as pl
from jax.experimental.pallas import tpu as pltpu
from jax.sharding import Mesh, PartitionSpec as P

PANEL = 512
C0, C1, C2, C3, C4 = (-205.0 / 72.0, 8.0 / 5.0, -1.0 / 5.0, 8.0 / 315.0, -1.0 / 560.0)
SHIFT_MID = 7.25
HALF_WIDTH = 4.75
POINTS = 16384.0
SPACE = ("y", "xh")
HI = lax.Precision.HIGHEST
MIB = 1024 * 1024


def dot_nn(a, b):
    return lax.dot_general(a, b, (((1,), (0,)), ((), ())), precision=HI, preferred_element_type=jnp.float32)


def dot_nt(a, b):
    return lax.dot_general(a, b, (((1,), (1,)), ((), ())), precision=HI, preferred_element_type=jnp.float32)


def dot_tn(a, b):
    return lax.dot_general(a, b, (((0,), (0,)), ((), ())), precision=HI, preferred_element_type=jnp.float32)


def swap_groups(arrays):
    arrays = list(arrays)
    group = lax.broadcasted_iota(jnp.int32, arrays[0].shape, 1) // 16
    for bit in (1, 2, 4):
        high = (group & bit) != 0
        for i in range(8):
            if i & bit:
                continue
            a, d = arrays[i], arrays[i | bit]
            arrays[i] = jnp.where(high, pltpu.roll(d, 16 * bit, 1), a)
            arrays[i | bit] = jnp.where(high, d, pltpu.roll(a, 128 - 16 * bit, 1))
    return arrays


def pack_kernel(orb_ref, pot_ref, out_ref):
    def body(step, _):
        xp, yh = step // 2, step % 2
        parts = swap_groups([orb_ref[xp, yh * 8 + yl] for yl in range(8)])
        for g in range(8):
            out_ref[g, pl.ds(step * 32, 32), :] = parts[g]
        return 0

    lax.fori_loop(0, 8, body, 0, unroll=2)
    packed = jnp.concatenate([pot_ref[xp] for xp in range(4)], axis=1)
    for g in range(8):
        out_ref[g, 256:272, :] = packed


def pack(orbitals, potential):
    return pl.pallas_call(
        pack_kernel,
        out_shape=jax.ShapeDtypeStruct((8, 272, 128), jnp.float32),
        compiler_params=pltpu.CompilerParams(vmem_limit_bytes=8 * MIB),
    )(orbitals, potential)


def roll_y(pair, places, lane):
    shift = 16 * places % 128
    turned = [pltpu.roll(half, shift, 1) for half in pair]
    wraps = lane < shift if places > 0 else lane >= shift
    return [jnp.where(wraps, turned[1], turned[0]), jnp.where(wraps, turned[0], turned[1])]


def filter_kernel(in_ref, out_ref, weight, buf_a, buf_b):
    scale = 2.0 / HALF_WIDTH
    centre = (-1.5 * C0 - SHIFT_MID) * scale
    side = [-0.5 * c * scale for c in (C1, C2, C3, C4)]
    y_of = lax.broadcasted_iota(jnp.int32, (16, 256), 0)
    lane_y = lax.broadcasted_iota(jnp.int32, (16, 256), 1) // 16
    spread = jnp.where(y_of == lane_y, 1.0, 0.0).astype(jnp.float32)
    for s in range(8):
        wide = dot_tn(in_ref[s, 256:272, :], spread) * scale + centre
        for xp in range(4):
            for yh in range(2):
                weight[8 * s + 2 * xp + yh] = wide[xp * 32 : xp * 32 + 32, yh * 128 : yh * 128 + 128]
    lane = lax.broadcasted_iota(jnp.int32, (32, 128), 1)

    def put(ref, plane, value):
        ref[plane, 8:40, :] = value
        ref[plane, 4:8, :] = value[28:32, :]
        ref[plane, 40:44, :] = value[0:4, :]

    def take(plane, _):
        put(buf_b, plane, in_ref[plane // 8, pl.ds((plane % 8) * 32, 32), :])
        return 0

    def apply(ref, x):
        near = [ref[2 * x + yh, 8:40, :] for yh in range(2)]
        total = [weight[2 * x + yh] * near[yh] for yh in range(2)]
        for m in range(1, 5):
            up, down = 2 * ((x + m) & 31), 2 * ((x + 32 - m) & 31)
            for yh in range(2):
                along_x = ref[up + yh, 8:40, :] + ref[down + yh, 8:40, :]
                along_z = ref[2 * x + yh, 8 - m : 40 - m, :] + ref[2 * x + yh, 8 + m : 40 + m, :]
                total[yh] = total[yh] + side[m - 1] * (along_x + along_z)
        forth, back = roll_y(near, 1, lane), roll_y(near, -1, lane)
        ahead = [side[1] * back[yh] + side[2] * near[yh] + side[3] * forth[yh] for yh in range(2)]
        behind = [side[1] * forth[yh] + side[2] * near[yh] + side[3] * back[yh] for yh in range(2)]
        ahead, behind = roll_y(ahead, 3, lane), roll_y(behind, -3, lane)
        return [total[yh] + (side[0] * (forth[yh] + back[yh]) + (ahead[yh] + behind[yh])) for yh in range(2)]

    def first(x, _):
        for yh, total in enumerate(apply(buf_b, x)):
            put(buf_a, 2 * x + yh, 0.5 * total)
        return 0

    def second(x, _):
        for yh, total in enumerate(apply(buf_a, x)):
            put(buf_b, 2 * x + yh, total - buf_b[2 * x + yh, 8:40, :])
        return 0

    def third(x, _):
        for yh, total in enumerate(apply(buf_b, x)):
            put(buf_a, 2 * x + yh, total - buf_a[2 * x + yh, 8:40, :])
        return 0

    def fourth(x, _):
        for yh, total in enumerate(apply(buf_a, x)):
            out_ref[2 * x + yh] = total - buf_b[2 * x + yh, 8:40, :]
        return 0

    lax.fori_loop(0, 64, take, 0, unroll=4)
    for step in (first, second, third, fourth):
        lax.fori_loop(0, 32, step, 0, unroll=4)


def chebyshev(received):
    out = pl.pallas_call(
        filter_kernel,
        out_shape=jax.ShapeDtypeStruct((64, 32, 128), jnp.float32),
        scratch_shapes=[pltpu.VMEM((64, 32, 128), jnp.float32)] + [pltpu.VMEM((64, 48, 128), jnp.float32)] * 2,
        compiler_params=pltpu.CompilerParams(vmem_limit_bytes=16 * MIB),
    )(received)
    return out.reshape(8, 256, 128)


def unpack_kernel(in_ref, out_ref):
    def body(step, _):
        parts = swap_groups([in_ref[g, pl.ds(step * 32, 32), :] for g in range(8)])
        for yl in range(8):
            out_ref[pl.ds(yl * 256 + step * 32, 32), :] = parts[yl]
        return 0

    lax.fori_loop(0, 8, body, 0, unroll=2)


def unpack(back):
    return pl.pallas_call(
        unpack_kernel,
        out_shape=jax.ShapeDtypeStruct((2048, 128), jnp.float32),
        compiler_params=pltpu.CompilerParams(vmem_limit_bytes=8 * MIB),
        cost_estimate=pl.CostEstimate(flops=4_000_000, bytes_accessed=4 * MIB, transcendentals=0),
    )(back)


def own_panel_kernel(in_ref, out_ref):
    turned = in_ref[0].T
    for yl in range(8):
        out_ref[:, yl * 256 : yl * 256 + 256] = turned[yl * 16 : yl * 16 + 16, :]


def own_panel(back):
    return pl.pallas_call(
        own_panel_kernel,
        grid=(1,),
        in_specs=[pl.BlockSpec((1, 256, 128), lambda i: (0, 0, 0))],
        out_specs=pl.BlockSpec((16, 2048), lambda i: (0, 0)),
        out_shape=jax.ShapeDtypeStruct((16, 2048), jnp.float32),
        compiler_params=pltpu.CompilerParams(vmem_limit_bytes=4 * MIB),
    )(back)


def ring(count, step):
    return [(i, (i + step) % count) for i in range(count)]


def gather_panel(own):
    other = lax.ppermute(own, "xl", ring(2, 1))
    pair = jnp.concatenate([own, other], axis=0)
    found = [pair]
    right = left = pair
    for _ in range(3):
        right = lax.ppermute(right, "z", ring(8, 1))
        left = lax.ppermute(left, "z", ring(8, -1))
        found += [right, left]
    far = jnp.concatenate([lax.ppermute(right[:16], "z", ring(8, 1)), lax.ppermute(left[16:], "z", ring(8, -1))], axis=0)
    found.append(far)
    return found + [lax.ppermute(block, "c", ring(2, 1)) for block in found]


OFFSETS = (0, -1, 1, -2, 2, -3, 3, 4)


def products_kernel(place_ref, *refs):
    blocks, (field_ref, panel_ref, out_ref, gram, coupling) = refs[:16], refs[16:]
    xl, z, core = place_ref[0], place_ref[1], place_ref[2]
    for other in range(2):
        for k, offset in enumerate(OFFSETS):
            for xo in range(2):
                owner = (xl ^ xo) * 16 + ((z + offset) & 7) * 2 + (core ^ other)
                rows = pl.ds(pl.multiple_of(owner * 16, 16), 16)
                panel_ref[rows, :] = blocks[other * 8 + k][xo * 16 : xo * 16 + 16, :]
    mine = pl.ds(pl.multiple_of((xl * 2 + core) * 128, 128), 128)
    gram[...] = jnp.zeros_like(gram)
    coupling[...] = jnp.zeros_like(coupling)

    def chunk(i, _):
        points = pl.ds(pl.multiple_of(i * 512, 512), 512)
        wide = panel_ref[:, points]
        gram[...] += dot_nt(panel_ref[mine, points], wide)
        coupling[...] += dot_nn(wide, field_ref[points, :])
        return 0

    lax.fori_loop(0, 4, chunk, 0)
    for s in range(8):
        for j in range(4):
            out_ref[s, j * 16 : j * 16 + 16, :] = gram[s * 16 : s * 16 + 16, j * 128 : j * 128 + 128]
        out_ref[s, 64:128, :] = coupling[s * 64 : s * 64 + 64, :]


def products(place, blocks, field):
    return pl.pallas_call(
        products_kernel,
        in_specs=[pl.BlockSpec(memory_space=pltpu.SMEM)] + [pl.BlockSpec(memory_space=pltpu.VMEM)] * 17,
        out_shape=(jax.ShapeDtypeStruct((512, 2048), jnp.float32), jax.ShapeDtypeStruct((8, 128, 128), jnp.float32)),
        scratch_shapes=[pltpu.VMEM((128, 512), jnp.float32), pltpu.VMEM((512, 128), jnp.float32)],
        compiler_params=pltpu.CompilerParams(vmem_limit_bytes=28 * MIB),
    )(place, *blocks, field)


def total_of(terms):
    while len(terms) > 1:
        terms = [terms[i] + terms[i + 1] for i in range(0, len(terms), 2)]
    return terms[0]


def eliminate(block):
    rows = lax.broadcasted_iota(jnp.int32, (8, 128), 0)
    lanes = lax.broadcasted_iota(jnp.int32, (8, 128), 1)

    def spread_row(tile, i):
        return jnp.broadcast_to(tile[i : i + 1, :], (8, 128))

    def spread_lane(tile, j):
        return jnp.broadcast_to(tile[:, j : j + 1], (8, 128))

    left = [block[8 * t : 8 * t + 8, :] for t in range(16)]
    right = [jnp.where(lanes == rows + 8 * t, 1.0, 0.0).astype(jnp.float32) for t in range(16)]
    out = []
    for t0 in range(16):
        columns = [spread_lane(left[t0], 8 * t0 + j) for j in range(8)]
        corner = [[spread_row(columns[j], i) for j in range(i + 1)] for i in range(8)]
        row_l = [spread_row(left[t0], i) for i in range(8)]
        row_r = [spread_row(right[t0], i) for i in range(8)]
        inverse, factor = [None] * 8, [[None] * 8 for _ in range(8)]
        for j in range(8):
            inverse[j] = 1.0 / corner[j][j]
            for i in range(j + 1, 8):
                factor[i][j] = corner[i][j] * inverse[j]
            for i in range(j + 1, 8):
                for k in range(j + 1, i + 1):
                    corner[i][k] = corner[i][k] - factor[i][j] * corner[k][j]
                row_l[i] = row_l[i] - factor[i][j] * row_l[j]
                row_r[i] = row_r[i] - factor[i][j] * row_r[j]
        own, pivot = row_r[0], corner[0][0]
        for i in range(1, 8):
            own, pivot = jnp.where(rows == i, row_r[i], own), jnp.where(rows == i, corner[i][i], pivot)
        root = lax.rsqrt(pivot)
        root = root * (1.5 - 0.5 * pivot * root * root)
        out.append(own * root)
        if t0 == 15:
            break
        solved_l, solved_r = [None] * 8, [None] * 8
        for k in range(7, -1, -1):
            u, v = row_l[k] * inverse[k], row_r[k] * inverse[k]
            for i in range(7, k, -1):
                u, v = u - factor[i][k] * solved_l[i], v - factor[i][k] * solved_r[i]
            solved_l[k], solved_r[k] = u, v
        for t in range(t0 + 1, 16):
            weights = [spread_lane(left[t], 8 * t0 + j) for j in range(8)]
            left[t] = left[t] - total_of([weights[j] * solved_l[j] for j in range(8)])
            right[t] = right[t] - total_of([weights[j] * solved_r[j] for j in range(8)])
    return jnp.concatenate(out, axis=0)


def inverse_kernel(place_ref, own_ref, by_x_ref, by_core_ref, by_both_ref, inv_ref, work):
    xl, core = place_ref[0], place_ref[2]
    for flip, ref in enumerate((own_ref, by_core_ref, by_x_ref, by_both_ref)):
        piece = (xl ^ (flip // 2)) * 2 + (core ^ (flip % 2))
        for s in range(8):
            rows = pl.ds(pl.multiple_of(piece * 128 + s * 16, 16), 16)
            for j in range(4):
                work[rows, j * 128 : j * 128 + 128] = ref[s, j * 16 : j * 16 + 16, :] * (1.0 / POINTS)
    inv_ref[...] = jnp.zeros_like(inv_ref)

    def diagonal(k, _):
        here = pl.ds(pl.multiple_of(k * 128, 128), 128)
        corner = eliminate(work[here, here])
        for kk in range(4):

            @pl.when(k == kk)
            def _(kk=kk, corner=corner):
                low, high = kk * 128, kk * 128 + 128
                if kk:
                    inv_ref[low:high, :low] = dot_nn(corner, inv_ref[low:high, :low])
                inv_ref[low:high, low:high] = corner
                if high < PANEL:
                    panel = dot_nt(work[high:, low:high], corner)
                    work[high:, high:] -= dot_nt(panel, panel)
                    inv_ref[high:, :high] -= dot_nn(panel, inv_ref[low:high, :high])

        return 0

    lax.fori_loop(0, 4, diagonal, 0)


def inverse_factor(place, pieces):
    return pl.pallas_call(
        inverse_kernel,
        in_specs=[pl.BlockSpec(memory_space=pltpu.SMEM)] + [pl.BlockSpec(memory_space=pltpu.VMEM)] * 4,
        out_shape=jax.ShapeDtypeStruct((PANEL, PANEL), jnp.float32),
        scratch_shapes=[pltpu.VMEM((PANEL, PANEL), jnp.float32)],
        compiler_params=pltpu.CompilerParams(vmem_limit_bytes=16 * MIB),
    )(place, *pieces)


def update_kernel(place_ref, inv_ref, sums_ref, panel_ref, field_ref, out_ref, coupling, mixer):
    for s in range(8):
        coupling[s * 64 : s * 64 + 64, :] = sums_ref[s, 64:128, :] * (1.0 / POINTS)
    inverse = inv_ref[...]
    middle = dot_nt(coupling[...].T, inverse)
    mixer[...] = -dot_nn(middle, inverse)
    own = place_ref[0] * 16 + place_ref[1] * 2 + place_ref[2]
    mixer[0:16, :] = inv_ref[pl.ds(pl.multiple_of(own * 16, 16), 16), :]
    keep = lax.broadcasted_iota(jnp.int32, (256, 128), 1) >= 16

    def chunk(yl, _):
        points = pl.ds(pl.multiple_of(yl * 256, 256), 256)
        moved = dot_nn(mixer[...], panel_ref[:, points]).T
        moved = moved + jnp.where(keep, field_ref[points, :], 0.0)
        for xp in range(4):
            for yh in range(2):
                out_ref[xp, yh * 8 + yl] = moved[xp * 64 + yh * 32 : xp * 64 + yh * 32 + 32, :]
        return 0

    lax.fori_loop(0, 8, chunk, 0)


def update(place, inverse, sums, panel, field):
    return pl.pallas_call(
        update_kernel,
        in_specs=[pl.BlockSpec(memory_space=pltpu.SMEM)] + [pl.BlockSpec(memory_space=pltpu.VMEM)] * 4,
        out_shape=jax.ShapeDtypeStruct((4, 16, 32, 128), jnp.float32),
        scratch_shapes=[pltpu.VMEM((PANEL, 128), jnp.float32), pltpu.VMEM((128, PANEL), jnp.float32)],
        compiler_params=pltpu.CompilerParams(vmem_limit_bytes=28 * MIB),
    )(place, inverse, sums, panel, field)


def per_device(orbitals, potential):
    xl, z, core = lax.axis_index("xl"), lax.axis_index("z"), lax.axis_index("c")
    place = jnp.stack([xl, z, core]).astype(jnp.int32)
    received = lax.all_to_all(pack(orbitals, potential), SPACE, 0, 0, tiled=True)
    back = lax.all_to_all(chebyshev(received), SPACE, 0, 0, tiled=True)
    field = unpack(back)
    panel, terms = products(place, gather_panel(own_panel(back)), field)
    mine = jnp.sum(lax.all_to_all(terms, SPACE, 0, 0, tiled=True), axis=0)
    sums = lax.all_to_all(jnp.broadcast_to(mine, (8, 128, 128)), SPACE, 0, 0, tiled=True)
    piece = sums[:, :64]
    by_core = lax.ppermute(piece, "c", ring(2, 1))
    by_x = lax.ppermute(piece, "xl", ring(2, 1))
    by_both = lax.ppermute(by_x, "c", ring(2, 1))
    inverse = inverse_factor(place, (piece, by_x, by_core, by_both))
    return update(place, inverse, sums, panel, field)


def solution(mesh):
    fine = Mesh(mesh.devices.reshape(4, 2, 2, 8, 2), ("y", "xh", "xl", "z", "c"))
    return jax.shard_map(
        per_device,
        mesh=fine,
        in_specs=(P(SPACE, None, None, ("xl", "z", "c")), P(SPACE, None, None)),
        out_specs=P(SPACE, None, None, ("xl", "z", "c")),
        check_vma=False,
    )
```

```python
import functools

import jax
import jax.numpy as jnp
from jax import lax
from jax.experimental import pallas as pl
from jax.experimental.pallas import tpu as pltpu
from jax.sharding import Mesh, PartitionSpec as P

PANEL = 512
C0, C1, C2, C3, C4 = (-205.0 / 72.0, 8.0 / 5.0, -1.0 / 5.0, 8.0 / 315.0, -1.0 / 560.0)
SHIFT_MID = 7.25
HALF_WIDTH = 4.75
POINTS = 16384.0
SPACE = ("y", "xh")
HI = lax.Precision.HIGHEST
MIB = 1024 * 1024
BIG = 56


def dot_nn(a, b):
    return lax.dot_general(a, b, (((1,), (0,)), ((), ())), precision=HI, preferred_element_type=jnp.float32)


def dot_nt(a, b):
    return lax.dot_general(a, b, (((1,), (1,)), ((), ())), precision=HI, preferred_element_type=jnp.float32)


def dot_tn(a, b):
    return lax.dot_general(a, b, (((0,), (0,)), ((), ())), precision=HI, preferred_element_type=jnp.float32)


def swap_groups(arrays):
    arrays = list(arrays)
    group = lax.broadcasted_iota(jnp.int32, arrays[0].shape, 1) // 16
    for bit in (1, 2, 4):
        high = (group & bit) != 0
        for i in range(8):
            if i & bit:
                continue
            a, d = arrays[i], arrays[i | bit]
            arrays[i] = jnp.where(high, pltpu.roll(d, 16 * bit, 1), a)
            arrays[i | bit] = jnp.where(high, d, pltpu.roll(a, 128 - 16 * bit, 1))
    return arrays


def pack_kernel(orb_ref, pot_ref, out_ref):
    xp = pl.program_id(0)
    for yh in range(2):
        parts = swap_groups([orb_ref[0, yh * 8 + yl] for yl in range(8)])
        for g in range(8):
            out_ref[g, pl.ds(pl.multiple_of(xp * 64 + yh * 32, 32), 32), :] = parts[g]

    @pl.when(xp == 3)
    def _():
        packed = jnp.concatenate([pot_ref[p] for p in range(4)], axis=1)
        for g in range(8):
            out_ref[g, 256:272, :] = packed


def pack(orbitals, potential):
    return pl.pallas_call(
        pack_kernel,
        grid=(4,),
        in_specs=[pl.BlockSpec((1, 16, 32, 128), lambda i: (i, 0, 0, 0)), pl.BlockSpec((4, 16, 32), lambda i: (0, 0, 0))],
        out_specs=pl.BlockSpec((8, 272, 128), lambda i: (0, 0, 0)),
        out_shape=jax.ShapeDtypeStruct((8, 272, 128), jnp.float32),
        compiler_params=pltpu.CompilerParams(vmem_limit_bytes=BIG * MIB),
    )(orbitals, potential)


def roll_y(pair, places, lane):
    shift = 16 * places % 128
    turned = [pltpu.roll(half, shift, 1) for half in pair]
    wraps = lane < shift if places > 0 else lane >= shift
    return [jnp.where(wraps, turned[1], turned[0]), jnp.where(wraps, turned[0], turned[1])]


def filter_kernel(in_ref, out_ref, weight, buf_a, buf_b):
    scale = 2.0 / HALF_WIDTH
    centre = (-1.5 * C0 - SHIFT_MID) * scale
    side = [-0.5 * c * scale for c in (C1, C2, C3, C4)]
    y_of = lax.broadcasted_iota(jnp.int32, (16, 256), 0)
    lane_y = lax.broadcasted_iota(jnp.int32, (16, 256), 1) // 16
    spread = jnp.where(y_of == lane_y, 1.0, 0.0).astype(jnp.float32)
    for s in range(8):
        wide = dot_tn(in_ref[s, 256:272, :], spread) * scale + centre
        for xp in range(4):
            for yh in range(2):
                weight[8 * s + 2 * xp + yh] = wide[xp * 32 : xp * 32 + 32, yh * 128 : yh * 128 + 128]
    lane = lax.broadcasted_iota(jnp.int32, (32, 128), 1)

    def put(ref, plane, value):
        ref[plane, 8:40, :] = value
        ref[plane, 4:8, :] = value[28:32, :]
        ref[plane, 40:44, :] = value[0:4, :]

    def take(plane, _):
        put(buf_b, plane, in_ref[plane // 8, pl.ds((plane % 8) * 32, 32), :])
        return 0

    def apply(ref, x):
        near = [ref[2 * x + yh, 8:40, :] for yh in range(2)]
        total = [weight[2 * x + yh] * near[yh] for yh in range(2)]
        for m in range(1, 5):
            up, down = 2 * ((x + m) & 31), 2 * ((x + 32 - m) & 31)
            for yh in range(2):
                along_x = ref[up + yh, 8:40, :] + ref[down + yh, 8:40, :]
                along_z = ref[2 * x + yh, 8 - m : 40 - m, :] + ref[2 * x + yh, 8 + m : 40 + m, :]
                total[yh] = total[yh] + side[m - 1] * (along_x + along_z)
        forth, back = roll_y(near, 1, lane), roll_y(near, -1, lane)
        ahead = [side[1] * back[yh] + side[2] * near[yh] + side[3] * forth[yh] for yh in range(2)]
        behind = [side[1] * forth[yh] + side[2] * near[yh] + side[3] * back[yh] for yh in range(2)]
        ahead, behind = roll_y(ahead, 3, lane), roll_y(behind, -3, lane)
        return [total[yh] + (side[0] * (forth[yh] + back[yh]) + (ahead[yh] + behind[yh])) for yh in range(2)]

    def first(x, _):
        for yh, total in enumerate(apply(buf_b, x)):
            put(buf_a, 2 * x + yh, 0.5 * total)
        return 0

    def second(x, _):
        for yh, total in enumerate(apply(buf_a, x)):
            put(buf_b, 2 * x + yh, total - buf_b[2 * x + yh, 8:40, :])
        return 0

    def third(x, _):
        for yh, total in enumerate(apply(buf_b, x)):
            put(buf_a, 2 * x + yh, total - buf_a[2 * x + yh, 8:40, :])
        return 0

    def fourth(x, _):
        for yh, total in enumerate(apply(buf_a, x)):
            out_ref[2 * x + yh] = total - buf_b[2 * x + yh, 8:40, :]
        return 0

    lax.fori_loop(0, 64, take, 0, unroll=4)
    for step in (first, second, third, fourth):
        lax.fori_loop(0, 32, step, 0, unroll=4)


def chebyshev(received):
    out = pl.pallas_call(
        filter_kernel,
        out_shape=jax.ShapeDtypeStruct((64, 32, 128), jnp.float32),
        scratch_shapes=[pltpu.VMEM((64, 32, 128), jnp.float32)] + [pltpu.VMEM((64, 48, 128), jnp.float32)] * 2,
        compiler_params=pltpu.CompilerParams(vmem_limit_bytes=16 * MIB),
    )(received)
    return out.reshape(8, 256, 128)


def turn_kernel(in_ref, out_ref):
    turned = in_ref[0].T
    for yl in range(8):
        out_ref[:, yl * 256 : yl * 256 + 256] = turned[yl * 16 : yl * 16 + 16, :]


def turn(back, groups):
    return pl.pallas_call(
        turn_kernel,
        grid=(groups,),
        in_specs=[pl.BlockSpec((1, 256, 128), lambda i: (i, 0, 0))],
        out_specs=pl.BlockSpec((16, 2048), lambda i: (i, 0)),
        out_shape=jax.ShapeDtypeStruct((16 * groups, 2048), jnp.float32),
        compiler_params=pltpu.CompilerParams(vmem_limit_bytes=4 * MIB),
        cost_estimate=pl.CostEstimate(flops=groups * 500_000, bytes_accessed=groups * MIB // 4, transcendentals=0),
    )(back)


def ring(count, step):
    return [(i, (i + step) % count) for i in range(count)]


def gather_panel(own, field):
    other = lax.ppermute(own, "xl", ring(2, 1))
    right = left = pair = jnp.concatenate([own, other], axis=0)
    found, swapped, waiting = [pair], [], [pair]
    for step in range(4):
        swaps = [lax.ppermute(block, "c", ring(2, 1)) for block in waiting]
        if step < 3:
            right = lax.ppermute(right, "z", ring(8, 1))
            left = lax.ppermute(left, "z", ring(8, -1))
            waiting = [right, left]
            found += waiting
        else:
            far_r = lax.ppermute(right[:16], "z", ring(8, 1))
            far_l = lax.ppermute(left[16:], "z", ring(8, -1))
            found.append(jnp.concatenate([far_r, far_l], axis=0))
        right, left, swaps, field = lax.optimization_barrier((right, left, swaps, field))
        swapped += swaps
    return found + swapped + [lax.ppermute(found[-1], "c", ring(2, 1))], field


OFFSETS = (0, -1, 1, -2, 2, -3, 3, 4)


def products_kernel(place_ref, *refs):
    blocks, (field_ref, home_ref, out_ref, panel_ref, acc, sems) = refs[:16], refs[16:]
    xl, z, core = place_ref[0], place_ref[1], place_ref[2]
    copies = []
    for other in range(2):
        for k, offset in enumerate(OFFSETS):
            for xo in range(2):
                owner = (xl ^ xo) * 16 + ((z + offset) & 7) * 2 + (core ^ other)
                rows = pl.ds(pl.multiple_of(owner * 16, 16), 16)
                source = blocks[other * 8 + k].at[pl.ds(xo * 16, 16), :]
                copies.append(pltpu.make_async_copy(source, panel_ref.at[rows, :], sems.at[len(copies)]))
                copies[-1].start()
    mine = pl.ds(pl.multiple_of((xl * 2 + core) * 128, 128), 128)
    acc[...] = jnp.zeros_like(acc)
    for copy in copies:
        copy.wait()
    home = pltpu.make_async_copy(panel_ref, home_ref, sems.at[32])
    home.start()

    def chunk(i, _):
        points = pl.ds(pl.multiple_of(i * 512, 512), 512)
        rows = jnp.concatenate([panel_ref[mine, points], field_ref[:, points]], axis=0)
        acc[...] += dot_nt(rows, panel_ref[:, points])
        return 0

    lax.fori_loop(0, 4, chunk, 0)
    for s in range(8):
        out_ref[s, 0:16, :] = acc[s * 16 : s * 16 + 16, :]
        out_ref[s, 16:32, :] = acc[128 + s * 16 : 128 + s * 16 + 16, :]
    home.wait()


def products(place, blocks, field):
    return pl.pallas_call(
        products_kernel,
        in_specs=[pl.BlockSpec(memory_space=pltpu.SMEM)]
        + [pl.BlockSpec(memory_space=pl.ANY)] * 16
        + [pl.BlockSpec(memory_space=pltpu.VMEM)],
        out_shape=(jax.ShapeDtypeStruct((512, 2048), jnp.float32), jax.ShapeDtypeStruct((8, 32, 512), jnp.float32)),
        out_specs=(pl.BlockSpec(memory_space=pl.ANY), pl.BlockSpec(memory_space=pltpu.VMEM)),
        scratch_shapes=[
            pltpu.VMEM((512, 2048), jnp.float32),
            pltpu.VMEM((256, 512), jnp.float32),
            pltpu.SemaphoreType.DMA((33,)),
        ],
        compiler_params=pltpu.CompilerParams(vmem_limit_bytes=BIG * MIB),
    )(place, *blocks, field)


def total_of(terms):
    while len(terms) > 1:
        terms = [terms[i] + terms[i + 1] for i in range(0, len(terms), 2)]
    return terms[0]


def eliminate(block):
    rows = lax.broadcasted_iota(jnp.int32, (8, 128), 0)
    lanes = lax.broadcasted_iota(jnp.int32, (8, 128), 1)

    def spread_row(tile, i):
        return jnp.broadcast_to(tile[i : i + 1, :], (8, 128))

    def spread_lane(tile, j):
        return jnp.broadcast_to(tile[:, j : j + 1], (8, 128))

    left = [block[8 * t : 8 * t + 8, :] for t in range(16)]
    right = [jnp.where(lanes == rows + 8 * t, 1.0, 0.0).astype(jnp.float32) for t in range(16)]
    out = []
    for t0 in range(16):
        columns = [spread_lane(left[t0], 8 * t0 + j) for j in range(8)]
        corner = [[spread_row(columns[j], i) for j in range(i + 1)] for i in range(8)]
        row_l = [spread_row(left[t0], i) for i in range(8)]
        row_r = [spread_row(right[t0], i) for i in range(8)]
        inverse, factor = [None] * 8, [[None] * 8 for _ in range(8)]
        for j in range(8):
            inverse[j] = 1.0 / corner[j][j]
            for i in range(j + 1, 8):
                factor[i][j] = corner[i][j] * inverse[j]
            for i in range(j + 1, 8):
                for k in range(j + 1, i + 1):
                    corner[i][k] = corner[i][k] - factor[i][j] * corner[k][j]
                row_l[i] = row_l[i] - factor[i][j] * row_l[j]
                row_r[i] = row_r[i] - factor[i][j] * row_r[j]
        own, pivot = row_r[0], corner[0][0]
        for i in range(1, 8):
            own, pivot = jnp.where(rows == i, row_r[i], own), jnp.where(rows == i, corner[i][i], pivot)
        root = lax.rsqrt(pivot)
        root = root * (1.5 - 0.5 * pivot * root * root)
        out.append(own * root)
        if t0 == 15:
            break
        solved_l, solved_r = [None] * 8, [None] * 8
        for k in range(7, -1, -1):
            u, v = row_l[k] * inverse[k], row_r[k] * inverse[k]
            for i in range(7, k, -1):
                u, v = u - factor[i][k] * solved_l[i], v - factor[i][k] * solved_r[i]
            solved_l[k], solved_r[k] = u, v
        for t in range(t0 + 1, 16):
            weights = [spread_lane(left[t], 8 * t0 + j) for j in range(8)]
            left[t] = left[t] - total_of([weights[j] * solved_l[j] for j in range(8)])
            right[t] = right[t] - total_of([weights[j] * solved_r[j] for j in range(8)])
    return jnp.concatenate(out, axis=0)


def inverse_kernel(place_ref, own_ref, by_x_ref, by_core_ref, by_both_ref, inv_ref, work):
    xl, core = place_ref[0], place_ref[2]
    for flip, ref in enumerate((own_ref, by_core_ref, by_x_ref, by_both_ref)):
        piece = (xl ^ (flip // 2)) * 2 + (core ^ (flip % 2))
        for s in range(8):
            rows = pl.ds(pl.multiple_of(piece * 128 + s * 16, 16), 16)
            work[rows, :] = ref[s] * (1.0 / POINTS)
    inv_ref[...] = jnp.zeros_like(inv_ref)

    def diagonal(k, _):
        here = pl.ds(pl.multiple_of(k * 128, 128), 128)
        corner = eliminate(work[here, here])
        for kk in range(4):

            @pl.when(k == kk)
            def _(kk=kk, corner=corner):
                low, high = kk * 128, kk * 128 + 128
                if kk:
                    inv_ref[low:high, :low] = dot_nn(corner, inv_ref[low:high, :low])
                inv_ref[low:high, low:high] = corner
                if high < PANEL:
                    panel = dot_nt(work[high:, low:high], corner)
                    work[high:, high:] -= dot_nt(panel, panel)
                    inv_ref[high:, :high] -= dot_nn(panel, inv_ref[low:high, :high])

        return 0

    lax.fori_loop(0, 4, diagonal, 0)


def inverse_factor(place, pieces):
    return pl.pallas_call(
        inverse_kernel,
        in_specs=[pl.BlockSpec(memory_space=pltpu.SMEM)] + [pl.BlockSpec(memory_space=pltpu.VMEM)] * 4,
        out_shape=jax.ShapeDtypeStruct((PANEL, PANEL), jnp.float32),
        scratch_shapes=[pltpu.VMEM((PANEL, PANEL), jnp.float32)],
        compiler_params=pltpu.CompilerParams(vmem_limit_bytes=16 * MIB),
    )(place, *pieces)


def update_kernel(place_ref, inv_ref, sums_ref, panel_ref, field_ref, out_ref, coupling, mixer):
    @pl.when(pl.program_id(0) == 0)
    def _():
        for s in range(8):
            coupling[s * 16 : s * 16 + 16, :] = sums_ref[s, 16:32, :] * (1.0 / POINTS)
        inverse = inv_ref[...]
        mixer[...] = -dot_nn(dot_nt(coupling[...], inverse), inverse)
        own = place_ref[0] * 16 + place_ref[1] * 2 + place_ref[2]
        mixer[0:16, :] = inv_ref[pl.ds(pl.multiple_of(own * 16, 16), 16), :]

    keep = lax.broadcasted_iota(jnp.int32, (128, 256), 0) >= 16
    moved = (dot_nn(mixer[...], panel_ref[...]) + jnp.where(keep, field_ref[...], 0.0)).T
    for xp in range(4):
        for yh in range(2):
            out_ref[xp, yh, 0] = moved[xp * 64 + yh * 32 : xp * 64 + yh * 32 + 32, :]


def update(place, inverse, sums, panel, field):
    out = pl.pallas_call(
        update_kernel,
        grid=(8,),
        in_specs=[
            pl.BlockSpec(memory_space=pltpu.SMEM),
            pl.BlockSpec((PANEL, PANEL), lambda i: (0, 0)),
            pl.BlockSpec((8, 32, PANEL), lambda i: (0, 0, 0)),
            pl.BlockSpec((PANEL, 256), lambda i: (0, i)),
            pl.BlockSpec((128, 256), lambda i: (0, i)),
        ],
        out_specs=pl.BlockSpec((4, 2, 1, 32, 128), lambda i: (0, 0, i, 0, 0)),
        out_shape=jax.ShapeDtypeStruct((4, 2, 8, 32, 128), jnp.float32),
        scratch_shapes=[pltpu.VMEM((128, PANEL), jnp.float32)] * 2,
        compiler_params=pltpu.CompilerParams(vmem_limit_bytes=16 * MIB),
    )(place, inverse, sums, panel, field)
    return out.reshape(4, 16, 32, 128)


def per_device(orbitals, potential):
    xl, z, core = lax.axis_index("xl"), lax.axis_index("z"), lax.axis_index("c")
    place = jnp.stack([xl, z, core]).astype(jnp.int32)
    received = lax.all_to_all(pack(orbitals, potential), SPACE, 0, 0, tiled=True)
    back = lax.all_to_all(chebyshev(received), SPACE, 0, 0, tiled=True)
    blocks, field = gather_panel(turn(back, 1), turn(back, 8))
    panel, terms = products(place, blocks, field)
    mine = jnp.sum(lax.all_to_all(terms, SPACE, 0, 0, tiled=True), axis=0)
    sums = lax.all_to_all(jnp.broadcast_to(mine, (8, 32, PANEL)), SPACE, 0, 0, tiled=True)
    piece = sums[:, :16]
    by_core = lax.ppermute(piece, "c", ring(2, 1))
    by_x = lax.ppermute(piece, "xl", ring(2, 1))
    by_both = lax.ppermute(by_x, "c", ring(2, 1))
    inverse = inverse_factor(place, (piece, by_x, by_core, by_both))
    return update(place, inverse, sums, panel, field)


def solution(mesh):
    fine = Mesh(mesh.devices.reshape(4, 2, 2, 8, 2), ("y", "xh", "xl", "z", "c"))
    return jax.shard_map(
        per_device,
        mesh=fine,
        in_specs=(P(SPACE, None, None, ("xl", "z", "c")), P(SPACE, None, None)),
        out_specs=P(SPACE, None, None, ("xl", "z", "c")),
        check_vma=False,
    )
```

```python
import functools

import jax
import jax.numpy as jnp
from jax import lax
from jax.experimental import pallas as pl
from jax.experimental.pallas import tpu as pltpu
from jax.sharding import Mesh, PartitionSpec as P

PANEL = 512
C0, C1, C2, C3, C4 = (-205.0 / 72.0, 8.0 / 5.0, -1.0 / 5.0, 8.0 / 315.0, -1.0 / 560.0)
SHIFT_MID = 7.25
HALF_WIDTH = 4.75
POINTS = 16384.0
SPACE = ("y", "xh")
HI = lax.Precision.HIGHEST
MIB = 1024 * 1024
BIG = 56


def dot_nn(a, b):
    return lax.dot_general(a, b, (((1,), (0,)), ((), ())), precision=HI, preferred_element_type=jnp.float32)


def dot_nt(a, b):
    return lax.dot_general(a, b, (((1,), (1,)), ((), ())), precision=HI, preferred_element_type=jnp.float32)


def dot_tn(a, b):
    return lax.dot_general(a, b, (((0,), (0,)), ((), ())), precision=HI, preferred_element_type=jnp.float32)


def swap_groups(arrays):
    arrays = list(arrays)
    group = lax.broadcasted_iota(jnp.int32, arrays[0].shape, 1) // 16
    for bit in (1, 2, 4):
        high = (group & bit) != 0
        for i in range(8):
            if i & bit:
                continue
            a, d = arrays[i], arrays[i | bit]
            arrays[i] = jnp.where(high, pltpu.roll(d, 16 * bit, 1), a)
            arrays[i | bit] = jnp.where(high, d, pltpu.roll(a, 128 - 16 * bit, 1))
    return arrays


def pack_kernel(orb_ref, pot_ref, out_ref):
    xp = pl.program_id(0)
    for yh in range(2):
        parts = swap_groups([orb_ref[0, yh * 8 + yl] for yl in range(8)])
        for g in range(8):
            out_ref[g, pl.ds(pl.multiple_of(xp * 64 + yh * 32, 32), 32), :] = parts[g]

    @pl.when(xp == 3)
    def _():
        packed = jnp.concatenate([pot_ref[p] for p in range(4)], axis=1)
        for g in range(8):
            out_ref[g, 256:272, :] = packed


def pack(orbitals, potential):
    return pl.pallas_call(
        pack_kernel,
        grid=(4,),
        in_specs=[pl.BlockSpec((1, 16, 32, 128), lambda i: (i, 0, 0, 0)), pl.BlockSpec((4, 16, 32), lambda i: (0, 0, 0))],
        out_specs=pl.BlockSpec((8, 272, 128), lambda i: (0, 0, 0)),
        out_shape=jax.ShapeDtypeStruct((8, 272, 128), jnp.float32),
        compiler_params=pltpu.CompilerParams(vmem_limit_bytes=BIG * MIB),
    )(orbitals, potential)


def roll_y(pair, places, lane):
    shift = 16 * places % 128
    turned = [pltpu.roll(half, shift, 1) for half in pair]
    wraps = lane < shift if places > 0 else lane >= shift
    return [jnp.where(wraps, turned[1], turned[0]), jnp.where(wraps, turned[0], turned[1])]


def filter_kernel(in_ref, out_ref, weight, buf_a, buf_b):
    scale = 2.0 / HALF_WIDTH
    centre = (-1.5 * C0 - SHIFT_MID) * scale
    side = [-0.5 * c * scale for c in (C1, C2, C3, C4)]
    y_of = lax.broadcasted_iota(jnp.int32, (16, 256), 0)
    lane_y = lax.broadcasted_iota(jnp.int32, (16, 256), 1) // 16
    spread = jnp.where(y_of == lane_y, 1.0, 0.0).astype(jnp.float32)
    for s in range(8):
        wide = dot_tn(in_ref[s, 256:272, :], spread) * scale + centre
        for xp in range(4):
            for yh in range(2):
                weight[8 * s + 2 * xp + yh] = wide[xp * 32 : xp * 32 + 32, yh * 128 : yh * 128 + 128]
    lane = lax.broadcasted_iota(jnp.int32, (32, 128), 1)

    def put(ref, plane, value):
        ref[plane, 8:40, :] = value
        ref[plane, 4:8, :] = value[28:32, :]
        ref[plane, 40:44, :] = value[0:4, :]

    def take(plane, _):
        put(buf_b, plane, in_ref[plane // 8, pl.ds((plane % 8) * 32, 32), :])
        return 0

    def apply(ref, x):
        near = [ref[2 * x + yh, 8:40, :] for yh in range(2)]
        total = [weight[2 * x + yh] * near[yh] for yh in range(2)]
        for m in range(1, 5):
            up, down = 2 * ((x + m) & 31), 2 * ((x + 32 - m) & 31)
            for yh in range(2):
                along_x = ref[up + yh, 8:40, :] + ref[down + yh, 8:40, :]
                along_z = ref[2 * x + yh, 8 - m : 40 - m, :] + ref[2 * x + yh, 8 + m : 40 + m, :]
                total[yh] = total[yh] + side[m - 1] * (along_x + along_z)
        forth, back = roll_y(near, 1, lane), roll_y(near, -1, lane)
        ahead = [side[1] * back[yh] + side[2] * near[yh] + side[3] * forth[yh] for yh in range(2)]
        behind = [side[1] * forth[yh] + side[2] * near[yh] + side[3] * back[yh] for yh in range(2)]
        ahead, behind = roll_y(ahead, 3, lane), roll_y(behind, -3, lane)
        return [total[yh] + (side[0] * (forth[yh] + back[yh]) + (ahead[yh] + behind[yh])) for yh in range(2)]

    def first(x, _):
        for yh, total in enumerate(apply(buf_b, x)):
            put(buf_a, 2 * x + yh, 0.5 * total)
        return 0

    def second(x, _):
        for yh, total in enumerate(apply(buf_a, x)):
            put(buf_b, 2 * x + yh, total - buf_b[2 * x + yh, 8:40, :])
        return 0

    def third(x, _):
        for yh, total in enumerate(apply(buf_b, x)):
            put(buf_a, 2 * x + yh, total - buf_a[2 * x + yh, 8:40, :])
        return 0

    def fourth(x, _):
        for yh, total in enumerate(apply(buf_a, x)):
            out_ref[2 * x + yh] = total - buf_b[2 * x + yh, 8:40, :]
        return 0

    lax.fori_loop(0, 64, take, 0, unroll=4)
    for step in (first, second, third, fourth):
        lax.fori_loop(0, 32, step, 0, unroll=4)


def chebyshev(received):
    out = pl.pallas_call(
        filter_kernel,
        out_shape=jax.ShapeDtypeStruct((64, 32, 128), jnp.float32),
        scratch_shapes=[pltpu.VMEM((64, 32, 128), jnp.float32)] + [pltpu.VMEM((64, 48, 128), jnp.float32)] * 2,
        compiler_params=pltpu.CompilerParams(vmem_limit_bytes=16 * MIB),
    )(received)
    return out.reshape(8, 256, 128)


def turn_kernel(in_ref, out_ref):
    turned = in_ref[0].T
    for yl in range(8):
        out_ref[:, yl * 256 : yl * 256 + 256] = turned[yl * 16 : yl * 16 + 16, :]


def turn(back, groups):
    return pl.pallas_call(
        turn_kernel,
        grid=(groups,),
        in_specs=[pl.BlockSpec((1, 256, 128), lambda i: (i, 0, 0))],
        out_specs=pl.BlockSpec((16, 2048), lambda i: (i, 0)),
        out_shape=jax.ShapeDtypeStruct((16 * groups, 2048), jnp.float32),
        compiler_params=pltpu.CompilerParams(vmem_limit_bytes=4 * MIB),
        cost_estimate=pl.CostEstimate(flops=groups * 500_000, bytes_accessed=groups * MIB // 4, transcendentals=0),
    )(back)


def ring(count, step):
    return [(i, (i + step) % count) for i in range(count)]


def gather_panel(own, field):
    def step(right, left, swaps, more=()):
        moved = (
            lax.ppermute(right, "z", ring(8, 1)),
            lax.ppermute(left, "z", ring(8, -1)),
            [lax.ppermute(block, "c", ring(2, 1)) for block in swaps],
            *(lax.ppermute(block, "xl", ring(2, 1)) for block in more),
        )
        return lax.optimization_barrier(moved)

    right1, left1, swap0, other = step(own, own, [own], [own])
    both_r = jnp.concatenate([right1, other], axis=0)
    both_l = jnp.concatenate([other, left1], axis=0)
    right2, left2, swap1 = step(both_r, both_l, [both_r, left1])
    right2, left2, field = lax.optimization_barrier((right2, left2, field))
    right3, left3, swap2 = step(right2, left2, [right2, left2])
    right4, left4, swap3 = step(right3[8:], left3[:24], [right3, left3])
    right5, left5, swap4 = step(right4[16:], left4[:8], [right4, left4])
    last = jnp.concatenate([right5, left5], axis=0)
    swap5 = [lax.ppermute(last, "c", ring(2, 1))]
    here = [own, both_r, left1, right2, left2, right3, left3, right4, left4, last]
    return here + swap0 + swap1 + swap2 + swap3 + swap4 + swap5, field


PARTS = (
    ((0, 16, 0, 0, 0),),
    ((0, 16, 0, -1, 0), (16, 16, 1, 0, 0)),
    ((0, 16, 0, 1, 0),),
    ((0, 16, 0, -2, 0), (16, 16, 1, -1, 0)),
    ((0, 16, 1, 1, 0), (16, 16, 0, 2, 0)),
    ((0, 16, 0, -3, 0), (16, 16, 1, -2, 0)),
    ((0, 16, 1, 2, 0), (16, 16, 0, 3, 0)),
    ((0, 8, 0, 4, 8), (8, 16, 1, -3, 0)),
    ((0, 16, 1, 3, 0), (16, 8, 0, 4, 0)),
    ((0, 8, 1, 4, 8), (8, 8, 1, 4, 0)),
)
BLOCKS = 2 * len(PARTS)
COPIES = 2 * sum(len(parts) for parts in PARTS)


def products_kernel(place_ref, *refs):
    blocks, (field_ref, home_ref, out_ref, panel_ref, acc, sems) = refs[:BLOCKS], refs[BLOCKS:]
    xl, z, core = place_ref[0], place_ref[1], place_ref[2]
    copies = []
    for flip in range(2):
        for k, parts in enumerate(PARTS):
            for first, count, xo, offset, into in parts:
                owner = (xl ^ xo) * 16 + ((z + offset) & 7) * 2 + (core ^ flip)
                rows = pl.ds(pl.multiple_of(owner * 16 + into, 8), count)
                source = blocks[flip * len(PARTS) + k].at[pl.ds(first, count), :]
                copies.append(pltpu.make_async_copy(source, panel_ref.at[rows, :], sems.at[len(copies)]))
                copies[-1].start()
    mine = pl.ds(pl.multiple_of((xl * 2 + core) * 128, 128), 128)
    acc[...] = jnp.zeros_like(acc)
    for copy in copies:
        copy.wait()
    home = pltpu.make_async_copy(panel_ref, home_ref, sems.at[COPIES])
    home.start()

    def chunk(i, _):
        points = pl.ds(pl.multiple_of(i * 512, 512), 512)
        rows = jnp.concatenate([panel_ref[mine, points], field_ref[:, points]], axis=0)
        acc[...] += dot_nt(rows, panel_ref[:, points])
        return 0

    lax.fori_loop(0, 4, chunk, 0)
    for s in range(8):
        out_ref[s, 0:16, :] = acc[s * 16 : s * 16 + 16, :]
        out_ref[s, 16:32, :] = acc[128 + s * 16 : 128 + s * 16 + 16, :]
    home.wait()


def products(place, blocks, field):
    return pl.pallas_call(
        products_kernel,
        in_specs=[pl.BlockSpec(memory_space=pltpu.SMEM)]
        + [pl.BlockSpec(memory_space=pl.ANY)] * BLOCKS
        + [pl.BlockSpec(memory_space=pltpu.VMEM)],
        out_shape=(jax.ShapeDtypeStruct((512, 2048), jnp.float32), jax.ShapeDtypeStruct((8, 32, 512), jnp.float32)),
        out_specs=(pl.BlockSpec(memory_space=pl.ANY), pl.BlockSpec(memory_space=pltpu.VMEM)),
        scratch_shapes=[
            pltpu.VMEM((512, 2048), jnp.float32),
            pltpu.VMEM((256, 512), jnp.float32),
            pltpu.SemaphoreType.DMA((COPIES + 1,)),
        ],
        compiler_params=pltpu.CompilerParams(vmem_limit_bytes=BIG * MIB),
    )(place, *blocks, field)


def total_of(terms):
    while len(terms) > 1:
        terms = [terms[i] + terms[i + 1] for i in range(0, len(terms), 2)]
    return terms[0]


def eliminate(block):
    rows = lax.broadcasted_iota(jnp.int32, (8, 128), 0)
    lanes = lax.broadcasted_iota(jnp.int32, (8, 128), 1)

    def spread_row(tile, i):
        return jnp.broadcast_to(tile[i : i + 1, :], (8, 128))

    def spread_lane(tile, j):
        return jnp.broadcast_to(tile[:, j : j + 1], (8, 128))

    left = [block[8 * t : 8 * t + 8, :] for t in range(16)]
    right = [jnp.where(lanes == rows + 8 * t, 1.0, 0.0).astype(jnp.float32) for t in range(16)]
    out = []
    for t0 in range(16):
        columns = [spread_lane(left[t0], 8 * t0 + j) for j in range(8)]
        corner = [[spread_row(columns[j], i) for j in range(i + 1)] for i in range(8)]
        row_l = [spread_row(left[t0], i) for i in range(8)]
        row_r = [spread_row(right[t0], i) for i in range(8)]
        inverse, factor = [None] * 8, [[None] * 8 for _ in range(8)]
        for j in range(8):
            inverse[j] = 1.0 / corner[j][j]
            for i in range(j + 1, 8):
                factor[i][j] = corner[i][j] * inverse[j]
            for i in range(j + 1, 8):
                for k in range(j + 1, i + 1):
                    corner[i][k] = corner[i][k] - factor[i][j] * corner[k][j]
                row_l[i] = row_l[i] - factor[i][j] * row_l[j]
                row_r[i] = row_r[i] - factor[i][j] * row_r[j]
        own, pivot = row_r[0], corner[0][0]
        for i in range(1, 8):
            own, pivot = jnp.where(rows == i, row_r[i], own), jnp.where(rows == i, corner[i][i], pivot)
        root = lax.rsqrt(pivot)
        root = root * (1.5 - 0.5 * pivot * root * root)
        out.append(own * root)
        if t0 == 15:
            break
        solved_l, solved_r = [None] * 8, [None] * 8
        for k in range(7, -1, -1):
            u, v = row_l[k] * inverse[k], row_r[k] * inverse[k]
            for i in range(7, k, -1):
                u, v = u - factor[i][k] * solved_l[i], v - factor[i][k] * solved_r[i]
            solved_l[k], solved_r[k] = u, v
        for t in range(t0 + 1, 16):
            weights = [spread_lane(left[t], 8 * t0 + j) for j in range(8)]
            left[t] = left[t] - total_of([weights[j] * solved_l[j] for j in range(8)])
            right[t] = right[t] - total_of([weights[j] * solved_r[j] for j in range(8)])
    return jnp.concatenate(out, axis=0)


def invert(pieces, xl, core, work, inv_ref):
    for flip, ref in enumerate(pieces):
        piece = (xl ^ (flip // 2)) * 2 + (core ^ (flip % 2))
        for s in range(8):
            rows = pl.ds(pl.multiple_of(piece * 128 + s * 16, 16), 16)
            work[rows, :] = ref[s] * (1.0 / POINTS)
    inv_ref[...] = jnp.zeros_like(inv_ref)

    def diagonal(k, _):
        here = pl.ds(pl.multiple_of(k * 128, 128), 128)
        corner = eliminate(work[here, here])
        for kk in range(4):

            @pl.when(k == kk)
            def _(kk=kk, corner=corner):
                low, high = kk * 128, kk * 128 + 128
                if kk:
                    inv_ref[low:high, :low] = dot_nn(corner, inv_ref[low:high, :low])
                inv_ref[low:high, low:high] = corner
                if high < PANEL:
                    panel = dot_nt(work[high:, low:high], corner)
                    work[high:, high:] -= dot_nt(panel, panel)
                    inv_ref[high:, :high] -= dot_nn(panel, inv_ref[low:high, :high])

        return 0

    lax.fori_loop(0, 4, diagonal, 0)


def update_kernel(place_ref, own_ref, by_core_ref, by_x_ref, by_both_ref, sums_ref, panel_ref, field_ref, out_ref, *scratch):
    work, inverse, coupling, mixer = scratch
    xl, z, core = place_ref[0], place_ref[1], place_ref[2]

    @pl.when(pl.program_id(0) == 0)
    def _():
        invert((own_ref, by_core_ref, by_x_ref, by_both_ref), xl, core, work, inverse)
        for s in range(8):
            coupling[s * 16 : s * 16 + 16, :] = sums_ref[s, 16:32, :] * (1.0 / POINTS)
        factor = inverse[...]
        mixer[...] = -dot_nn(dot_nt(coupling[...], factor), factor)
        own = xl * 16 + z * 2 + core
        mixer[0:16, :] = inverse[pl.ds(pl.multiple_of(own * 16, 16), 16), :]

    keep = lax.broadcasted_iota(jnp.int32, (128, 256), 0) >= 16
    moved = (dot_nn(mixer[...], panel_ref[...]) + jnp.where(keep, field_ref[...], 0.0)).T
    for xp in range(4):
        for yh in range(2):
            out_ref[xp, yh, 0] = moved[xp * 64 + yh * 32 : xp * 64 + yh * 32 + 32, :]


def update(place, pieces, sums, panel, field):
    whole = pl.BlockSpec((8, 16, PANEL), lambda i: (0, 0, 0))
    out = pl.pallas_call(
        update_kernel,
        grid=(8,),
        in_specs=[
            pl.BlockSpec(memory_space=pltpu.SMEM),
            *[whole] * 4,
            pl.BlockSpec((8, 32, PANEL), lambda i: (0, 0, 0)),
            pl.BlockSpec((PANEL, 256), lambda i: (0, i)),
            pl.BlockSpec((128, 256), lambda i: (0, i)),
        ],
        out_specs=pl.BlockSpec((4, 2, 1, 32, 128), lambda i: (0, 0, i, 0, 0)),
        out_shape=jax.ShapeDtypeStruct((4, 2, 8, 32, 128), jnp.float32),
        scratch_shapes=[pltpu.VMEM((PANEL, PANEL), jnp.float32)] * 2 + [pltpu.VMEM((128, PANEL), jnp.float32)] * 2,
        compiler_params=pltpu.CompilerParams(vmem_limit_bytes=52 * MIB),
    )(place, *pieces, sums, panel, field)
    return out.reshape(4, 16, 32, 128)


def per_device(orbitals, potential):
    xl, z, core = lax.axis_index("xl"), lax.axis_index("z"), lax.axis_index("c")
    place = jnp.stack([xl, z, core]).astype(jnp.int32)
    received = lax.all_to_all(pack(orbitals, potential), SPACE, 0, 0, tiled=True)
    back = lax.all_to_all(chebyshev(received), SPACE, 0, 0, tiled=True)
    blocks, field = gather_panel(turn(back, 1), turn(back, 8))
    panel, terms = products(place, blocks, field)
    mine = jnp.sum(lax.all_to_all(terms, SPACE, 0, 0, tiled=True), axis=0)
    sums = lax.all_to_all(jnp.broadcast_to(mine, (8, 32, PANEL)), SPACE, 0, 0, tiled=True)
    piece = sums[:, :16]
    by_core = lax.ppermute(piece, "c", ring(2, 1))
    by_x = lax.ppermute(piece, "xl", ring(2, 1))
    by_both = lax.ppermute(by_x, "c", ring(2, 1))
    return update(place, (piece, by_core, by_x, by_both), sums, panel, field)


def solution(mesh):
    fine = Mesh(mesh.devices.reshape(4, 2, 2, 8, 2), ("y", "xh", "xl", "z", "c"))
    return jax.shard_map(
        per_device,
        mesh=fine,
        in_specs=(P(SPACE, None, None, ("xl", "z", "c")), P(SPACE, None, None)),
        out_specs=P(SPACE, None, None, ("xl", "z", "c")),
        check_vma=False,
    )
```

```python
import functools

import jax
import jax.numpy as jnp
from jax import lax
from jax.experimental import pallas as pl
from jax.experimental.pallas import tpu as pltpu
from jax.sharding import Mesh, PartitionSpec as P

PANEL = 512
C0, C1, C2, C3, C4 = (-205.0 / 72.0, 8.0 / 5.0, -1.0 / 5.0, 8.0 / 315.0, -1.0 / 560.0)
SHIFT_MID = 7.25
HALF_WIDTH = 4.75
POINTS = 16384.0
SPACE = ("y", "xh")
HI = lax.Precision.HIGHEST
MIB = 1024 * 1024
BIG = 56


def dot_nn(a, b):
    return lax.dot_general(a, b, (((1,), (0,)), ((), ())), precision=HI, preferred_element_type=jnp.float32)


def dot_nt(a, b):
    return lax.dot_general(a, b, (((1,), (1,)), ((), ())), precision=HI, preferred_element_type=jnp.float32)


def dot_tn(a, b):
    return lax.dot_general(a, b, (((0,), (0,)), ((), ())), precision=HI, preferred_element_type=jnp.float32)


def swap_groups(arrays):
    arrays = list(arrays)
    group = lax.broadcasted_iota(jnp.int32, arrays[0].shape, 1) // 16
    for bit in (1, 2, 4):
        high = (group & bit) != 0
        for i in range(8):
            if i & bit:
                continue
            a, d = arrays[i], arrays[i | bit]
            arrays[i] = jnp.where(high, pltpu.roll(d, 16 * bit, 1), a)
            arrays[i | bit] = jnp.where(high, d, pltpu.roll(a, 128 - 16 * bit, 1))
    return arrays


def pack_kernel(orb_ref, pot_ref, out_ref):
    xp = pl.program_id(0)
    for yh in range(2):
        parts = swap_groups([orb_ref[0, yh * 8 + yl] for yl in range(8)])
        for g in range(8):
            out_ref[g, pl.ds(pl.multiple_of(xp * 64 + yh * 32, 32), 32), :] = parts[g]

    @pl.when(xp == 3)
    def _():
        packed = jnp.concatenate([pot_ref[p] for p in range(4)], axis=1)
        for g in range(8):
            out_ref[g, 256:272, :] = packed


def pack(orbitals, potential):
    return pl.pallas_call(
        pack_kernel,
        grid=(4,),
        in_specs=[pl.BlockSpec((1, 16, 32, 128), lambda i: (i, 0, 0, 0)), pl.BlockSpec((4, 16, 32), lambda i: (0, 0, 0))],
        out_specs=pl.BlockSpec((8, 272, 128), lambda i: (0, 0, 0)),
        out_shape=jax.ShapeDtypeStruct((8, 272, 128), jnp.float32),
        compiler_params=pltpu.CompilerParams(vmem_limit_bytes=BIG * MIB),
    )(orbitals, potential)


def roll_y(pair, places, lane):
    shift = 16 * places % 128
    turned = [pltpu.roll(half, shift, 1) for half in pair]
    wraps = lane < shift if places > 0 else lane >= shift
    return [jnp.where(wraps, turned[1], turned[0]), jnp.where(wraps, turned[0], turned[1])]


def filter_kernel(in_ref, out_ref, weight, buf_a, buf_b):
    scale = 2.0 / HALF_WIDTH
    centre = (-1.5 * C0 - SHIFT_MID) * scale
    side = [-0.5 * c * scale for c in (C1, C2, C3, C4)]
    y_of = lax.broadcasted_iota(jnp.int32, (16, 256), 0)
    lane_y = lax.broadcasted_iota(jnp.int32, (16, 256), 1) // 16
    spread = jnp.where(y_of == lane_y, 1.0, 0.0).astype(jnp.float32)
    for s in range(8):
        wide = dot_tn(in_ref[s, 256:272, :], spread) * scale + centre
        for xp in range(4):
            for yh in range(2):
                weight[8 * s + 2 * xp + yh] = wide[xp * 32 : xp * 32 + 32, yh * 128 : yh * 128 + 128]
    lane = lax.broadcasted_iota(jnp.int32, (32, 128), 1)

    def put(ref, plane, value):
        ref[plane, 8:40, :] = value
        ref[plane, 4:8, :] = value[28:32, :]
        ref[plane, 40:44, :] = value[0:4, :]

    def take(plane, _):
        put(buf_b, plane, in_ref[plane // 8, pl.ds((plane % 8) * 32, 32), :])
        return 0

    def apply(ref, x):
        near = [ref[2 * x + yh, 8:40, :] for yh in range(2)]
        total = [weight[2 * x + yh] * near[yh] for yh in range(2)]
        for m in range(1, 5):
            up, down = 2 * ((x + m) & 31), 2 * ((x + 32 - m) & 31)
            for yh in range(2):
                along_x = ref[up + yh, 8:40, :] + ref[down + yh, 8:40, :]
                along_z = ref[2 * x + yh, 8 - m : 40 - m, :] + ref[2 * x + yh, 8 + m : 40 + m, :]
                total[yh] = total[yh] + side[m - 1] * (along_x + along_z)
        forth, back = roll_y(near, 1, lane), roll_y(near, -1, lane)
        ahead = [side[1] * back[yh] + side[2] * near[yh] + side[3] * forth[yh] for yh in range(2)]
        behind = [side[1] * forth[yh] + side[2] * near[yh] + side[3] * back[yh] for yh in range(2)]
        ahead, behind = roll_y(ahead, 3, lane), roll_y(behind, -3, lane)
        return [total[yh] + (side[0] * (forth[yh] + back[yh]) + (ahead[yh] + behind[yh])) for yh in range(2)]

    def first(x, _):
        for yh, total in enumerate(apply(buf_b, x)):
            put(buf_a, 2 * x + yh, 0.5 * total)
        return 0

    def second(x, _):
        for yh, total in enumerate(apply(buf_a, x)):
            put(buf_b, 2 * x + yh, total - buf_b[2 * x + yh, 8:40, :])
        return 0

    def third(x, _):
        for yh, total in enumerate(apply(buf_b, x)):
            put(buf_a, 2 * x + yh, total - buf_a[2 * x + yh, 8:40, :])
        return 0

    def fourth(x, _):
        for yh, total in enumerate(apply(buf_a, x)):
            out_ref[2 * x + yh] = total - buf_b[2 * x + yh, 8:40, :]
        return 0

    lax.fori_loop(0, 64, take, 0, unroll=4)
    for step in (first, second, third, fourth):
        lax.fori_loop(0, 32, step, 0, unroll=4)


def chebyshev(received):
    out = pl.pallas_call(
        filter_kernel,
        out_shape=jax.ShapeDtypeStruct((64, 32, 128), jnp.float32),
        scratch_shapes=[pltpu.VMEM((64, 32, 128), jnp.float32)] + [pltpu.VMEM((64, 48, 128), jnp.float32)] * 2,
        compiler_params=pltpu.CompilerParams(vmem_limit_bytes=16 * MIB),
    )(received)
    return out.reshape(8, 256, 128)


def turn_kernel(in_ref, out_ref):
    turned = in_ref[0].T
    for yl in range(8):
        out_ref[:, yl * 256 : yl * 256 + 256] = turned[yl * 16 : yl * 16 + 16, :]


def turn(back, groups):
    return pl.pallas_call(
        turn_kernel,
        grid=(groups,),
        in_specs=[pl.BlockSpec((1, 256, 128), lambda i: (i, 0, 0))],
        out_specs=pl.BlockSpec((16, 2048), lambda i: (i, 0)),
        out_shape=jax.ShapeDtypeStruct((16 * groups, 2048), jnp.float32),
        compiler_params=pltpu.CompilerParams(vmem_limit_bytes=4 * MIB),
        cost_estimate=pl.CostEstimate(flops=groups * 500_000, bytes_accessed=groups * MIB // 4, transcendentals=0),
    )(back)


def ring(count, step):
    return [(i, (i + step) % count) for i in range(count)]


def gather_panel(own, field):
    other, field = lax.optimization_barrier((lax.ppermute(own, "xl", ring(2, 1)), field))
    right = left = pair = jnp.concatenate([own, other], axis=0)
    found, swapped, waiting = [pair], [], []
    for step in range(4):
        swaps = [lax.ppermute(block, "c", ring(2, 1)) for block in waiting]
        if step < 3:
            right = lax.ppermute(right, "z", ring(8, 1))
            left = lax.ppermute(left, "z", ring(8, -1))
            waiting = [right, left] if step else [pair, right, left]
            found += [right, left]
        else:
            far_r = lax.ppermute(right[:16], "z", ring(8, 1))
            far_l = lax.ppermute(left[16:], "z", ring(8, -1))
            found.append(jnp.concatenate([far_r, far_l], axis=0))
        right, left, swaps = lax.optimization_barrier((right, left, swaps))
        swapped += swaps
    return found + swapped + [lax.ppermute(found[-1], "c", ring(2, 1))], field


OFFSETS = (0, -1, 1, -2, 2, -3, 3, 4)


def products_kernel(place_ref, *refs):
    blocks, (field_ref, home_ref, out_ref, panel_ref, acc, sems) = refs[:16], refs[16:]
    xl, z, core = place_ref[0], place_ref[1], place_ref[2]
    copies = []
    for half in range(2):
        points = pl.ds(half * 1024, 1024)
        for flip in range(2):
            for k, offset in enumerate(OFFSETS):
                for xo in range(2):
                    owner = (xl ^ xo) * 16 + ((z + offset) & 7) * 2 + (core ^ flip)
                    rows = pl.ds(pl.multiple_of(owner * 16, 16), 16)
                    source = blocks[flip * 8 + k].at[pl.ds(xo * 16, 16), points]
                    copies.append(pltpu.make_async_copy(source, panel_ref.at[rows, points], sems.at[len(copies)]))
                    copies[-1].start()
    long = pl.ds(pl.multiple_of((3 - core) * 128, 128), 128)
    short = pl.ds(pl.multiple_of(core * 128, 128), 128)
    acc[...] = jnp.zeros_like(acc)

    def chunk(i, _):
        points = pl.ds(pl.multiple_of(i * 512, 512), 512)
        rows = jnp.concatenate([panel_ref[long, points], panel_ref[short, points], field_ref[:, points]], axis=0)
        acc[...] += dot_nt(rows, panel_ref[:, points])
        return 0

    for half in range(2):
        for copy in copies[half * 32 : half * 32 + 32]:
            copy.wait()
        if half:
            home = pltpu.make_async_copy(panel_ref, home_ref, sems.at[64])
            home.start()
        lax.fori_loop(half * 2, half * 2 + 2, chunk, 0)
    for s in range(8):
        rows = slice(s * 16, s * 16 + 16)
        lower = slice(128 + s * 16, 128 + s * 16 + 16)
        out_ref[s, :, 0:384] = acc[rows, 0:384]
        out_ref[s, :, 384:512] = jnp.where(core == 0, acc[rows, 384:512], acc[lower, 128:256])
        out_ref[s, :, 512:640] = acc[lower, 0:128]
        out_ref[s, :, 640:1152] = acc[256 + s * 16 : 256 + s * 16 + 16, :]
    home.wait()


def products(place, blocks, field):
    return pl.pallas_call(
        products_kernel,
        in_specs=[pl.BlockSpec(memory_space=pltpu.SMEM)]
        + [pl.BlockSpec(memory_space=pl.ANY)] * 16
        + [pl.BlockSpec(memory_space=pltpu.VMEM)],
        out_shape=(jax.ShapeDtypeStruct((512, 2048), jnp.float32), jax.ShapeDtypeStruct((8, 16, 1152), jnp.float32)),
        out_specs=(pl.BlockSpec(memory_space=pl.ANY), pl.BlockSpec(memory_space=pltpu.VMEM)),
        scratch_shapes=[
            pltpu.VMEM((512, 2048), jnp.float32),
            pltpu.VMEM((384, 512), jnp.float32),
            pltpu.SemaphoreType.DMA((65,)),
        ],
        compiler_params=pltpu.CompilerParams(vmem_limit_bytes=BIG * MIB),
    )(place, *blocks, field)


def total_of(terms):
    while len(terms) > 1:
        terms = [terms[i] + terms[i + 1] for i in range(0, len(terms), 2)]
    return terms[0]


def eliminate(block):
    rows = lax.broadcasted_iota(jnp.int32, (8, 128), 0)
    lanes = lax.broadcasted_iota(jnp.int32, (8, 128), 1)

    def spread_row(tile, i):
        return jnp.broadcast_to(tile[i : i + 1, :], (8, 128))

    def spread_lane(tile, j):
        return jnp.broadcast_to(tile[:, j : j + 1], (8, 128))

    left = [block[8 * t : 8 * t + 8, :] for t in range(16)]
    right = [jnp.where(lanes == rows + 8 * t, 1.0, 0.0).astype(jnp.float32) for t in range(16)]
    out = []
    for t0 in range(16):
        columns = [spread_lane(left[t0], 8 * t0 + j) for j in range(8)]
        corner = [[spread_row(columns[j], i) for j in range(i + 1)] for i in range(8)]
        row_l = [spread_row(left[t0], i) for i in range(8)]
        row_r = [spread_row(right[t0], i) for i in range(8)]
        inverse, factor = [None] * 8, [[None] * 8 for _ in range(8)]
        for j in range(8):
            inverse[j] = 1.0 / corner[j][j]
            for i in range(j + 1, 8):
                factor[i][j] = corner[i][j] * inverse[j]
            for i in range(j + 1, 8):
                for k in range(j + 1, i + 1):
                    corner[i][k] = corner[i][k] - factor[i][j] * corner[k][j]
                row_l[i] = row_l[i] - factor[i][j] * row_l[j]
                row_r[i] = row_r[i] - factor[i][j] * row_r[j]
        own, pivot = row_r[0], corner[0][0]
        for i in range(1, 8):
            own, pivot = jnp.where(rows == i, row_r[i], own), jnp.where(rows == i, corner[i][i], pivot)
        root = lax.rsqrt(pivot)
        root = root * (1.5 - 0.5 * pivot * root * root)
        out.append(own * root)
        if t0 == 15:
            break
        solved_l, solved_r = [None] * 8, [None] * 8
        for k in range(7, -1, -1):
            u, v = row_l[k] * inverse[k], row_r[k] * inverse[k]
            for i in range(7, k, -1):
                u, v = u - factor[i][k] * solved_l[i], v - factor[i][k] * solved_r[i]
            solved_l[k], solved_r[k] = u, v
        for t in range(t0 + 1, 16):
            weights = [spread_lane(left[t], 8 * t0 + j) for j in range(8)]
            left[t] = left[t] - total_of([weights[j] * solved_l[j] for j in range(8)])
            right[t] = right[t] - total_of([weights[j] * solved_r[j] for j in range(8)])
    return jnp.concatenate(out, axis=0)


def invert(pieces, core, work, inv_ref):
    for flip, ref in enumerate(pieces):
        owner = core ^ flip
        for s in range(8):
            tile = ref[s] * (1.0 / POINTS)
            work[pl.ds(pl.multiple_of((3 - owner) * 128 + s * 16, 16), 16), 0:384] = tile[:, 0:384]
            square = pl.multiple_of((3 - 2 * owner) * 128, 128)
            work[pl.ds(pl.multiple_of(square + s * 16, 16), 16), pl.ds(square, 128)] = tile[:, 384:512]
            work[pl.ds(pl.multiple_of(owner * 128 + s * 16, 16), 16), 0:128] = tile[:, 512:640]
    inv_ref[...] = jnp.zeros_like(inv_ref)

    def diagonal(k, _):
        here = pl.ds(pl.multiple_of(k * 128, 128), 128)
        corner = eliminate(work[here, here])
        for kk in range(4):

            @pl.when(k == kk)
            def _(kk=kk, corner=corner):
                low, high = kk * 128, kk * 128 + 128
                if kk:
                    inv_ref[low:high, :low] = dot_nn(corner, inv_ref[low:high, :low])
                inv_ref[low:high, low:high] = corner
                if high < PANEL:
                    panel = dot_nt(work[high:, low:high], corner)
                    work[high:, high:] -= dot_nt(panel, panel)
                    inv_ref[high:, :high] -= dot_nn(panel, inv_ref[low:high, :high])

        return 0

    lax.fori_loop(0, 4, diagonal, 0)


def update_kernel(place_ref, sums_ref, by_core_ref, panel_ref, field_ref, out_ref, *scratch):
    work, inverse, coupling, mixer = scratch
    xl, z, core = place_ref[0], place_ref[1], place_ref[2]

    @pl.when(pl.program_id(0) == 0)
    def _():
        invert((sums_ref, by_core_ref), core, work, inverse)
        for s in range(8):
            coupling[s * 16 : s * 16 + 16, :] = sums_ref[s, :, 640:1152] * (1.0 / POINTS)
        factor = inverse[...]
        mixer[...] = -dot_nn(dot_nt(coupling[...], factor), factor)
        own = xl * 16 + z * 2 + core
        mixer[0:16, :] = inverse[pl.ds(pl.multiple_of(own * 16, 16), 16), :]

    keep = lax.broadcasted_iota(jnp.int32, (128, 256), 0) >= 16
    moved = (dot_nn(mixer[...], panel_ref[...]) + jnp.where(keep, field_ref[...], 0.0)).T
    for xp in range(4):
        for yh in range(2):
            out_ref[xp, yh, 0] = moved[xp * 64 + yh * 32 : xp * 64 + yh * 32 + 32, :]


def update(place, sums, by_core, panel, field):
    out = pl.pallas_call(
        update_kernel,
        grid=(8,),
        in_specs=[
            pl.BlockSpec(memory_space=pltpu.SMEM),
            pl.BlockSpec((8, 16, 1152), lambda i: (0, 0, 0)),
            pl.BlockSpec((8, 16, 640), lambda i: (0, 0, 0)),
            pl.BlockSpec((PANEL, 256), lambda i: (0, i)),
            pl.BlockSpec((128, 256), lambda i: (0, i)),
        ],
        out_specs=pl.BlockSpec((4, 2, 1, 32, 128), lambda i: (0, 0, i, 0, 0)),
        out_shape=jax.ShapeDtypeStruct((4, 2, 8, 32, 128), jnp.float32),
        scratch_shapes=[pltpu.VMEM((PANEL, PANEL), jnp.float32)] * 2 + [pltpu.VMEM((128, PANEL), jnp.float32)] * 2,
        compiler_params=pltpu.CompilerParams(vmem_limit_bytes=52 * MIB),
    )(place, sums, by_core, panel, field)
    return out.reshape(4, 16, 32, 128)


def per_device(orbitals, potential):
    xl, z, core = lax.axis_index("xl"), lax.axis_index("z"), lax.axis_index("c")
    place = jnp.stack([xl, z, core]).astype(jnp.int32)
    received = lax.all_to_all(pack(orbitals, potential), SPACE, 0, 0, tiled=True)
    back = lax.all_to_all(chebyshev(received), SPACE, 0, 0, tiled=True)
    blocks, field = gather_panel(turn(back, 1), turn(back, 8))
    panel, terms = products(place, blocks, field)
    mine = jnp.sum(lax.all_to_all(terms, SPACE, 0, 0, tiled=True), axis=0)
    sums = lax.all_to_all(jnp.broadcast_to(mine, (8, 16, 1152)), SPACE, 0, 0, tiled=True)
    by_core = lax.ppermute(sums[:, :, :640], "c", ring(2, 1))
    return update(place, sums, by_core, panel, field)


def solution(mesh):
    fine = Mesh(mesh.devices.reshape(4, 2, 2, 8, 2), ("y", "xh", "xl", "z", "c"))
    return jax.shard_map(
        per_device,
        mesh=fine,
        in_specs=(P(SPACE, None, None, ("xl", "z", "c")), P(SPACE, None, None)),
        out_specs=P(SPACE, None, None, ("xl", "z", "c")),
        check_vma=False,
    )
```

```python
import functools

import jax
import jax.numpy as jnp
from jax import lax
from jax.experimental import pallas as pl
from jax.experimental.pallas import tpu as pltpu
from jax.sharding import Mesh, PartitionSpec as P

PANEL = 512
C0, C1, C2, C3, C4 = (-205.0 / 72.0, 8.0 / 5.0, -1.0 / 5.0, 8.0 / 315.0, -1.0 / 560.0)
SHIFT_MID = 7.25
HALF_WIDTH = 4.75
POINTS = 16384.0
SPACE = ("y", "xh")
HI = lax.Precision.HIGHEST
MIB = 1024 * 1024
BIG = 56


def dot_nn(a, b):
    return lax.dot_general(a, b, (((1,), (0,)), ((), ())), precision=HI, preferred_element_type=jnp.float32)


def dot_nt(a, b):
    return lax.dot_general(a, b, (((1,), (1,)), ((), ())), precision=HI, preferred_element_type=jnp.float32)


def dot_tn(a, b):
    return lax.dot_general(a, b, (((0,), (0,)), ((), ())), precision=HI, preferred_element_type=jnp.float32)


def swap_groups(arrays):
    arrays = list(arrays)
    group = lax.broadcasted_iota(jnp.int32, arrays[0].shape, 1) // 16
    for bit in (1, 2, 4):
        high = (group & bit) != 0
        for i in range(8):
            if i & bit:
                continue
            a, d = arrays[i], arrays[i | bit]
            arrays[i] = jnp.where(high, pltpu.roll(d, 16 * bit, 1), a)
            arrays[i | bit] = jnp.where(high, d, pltpu.roll(a, 128 - 16 * bit, 1))
    return arrays


def pack_kernel(orb_ref, pot_ref, out_ref):
    xp = pl.program_id(0)
    for yh in range(2):
        parts = swap_groups([orb_ref[0, yh * 8 + yl] for yl in range(8)])
        for g in range(8):
            out_ref[g, pl.ds(pl.multiple_of(xp * 64 + yh * 32, 32), 32), :] = parts[g]

    @pl.when(xp == 3)
    def _():
        packed = jnp.concatenate([pot_ref[p] for p in range(4)], axis=1)
        for g in range(8):
            out_ref[g, 256:272, :] = packed


def pack(orbitals, potential):
    return pl.pallas_call(
        pack_kernel,
        grid=(4,),
        in_specs=[pl.BlockSpec((1, 16, 32, 128), lambda i: (i, 0, 0, 0)), pl.BlockSpec((4, 16, 32), lambda i: (0, 0, 0))],
        out_specs=pl.BlockSpec((8, 272, 128), lambda i: (0, 0, 0)),
        out_shape=jax.ShapeDtypeStruct((8, 272, 128), jnp.float32),
        compiler_params=pltpu.CompilerParams(vmem_limit_bytes=BIG * MIB),
    )(orbitals, potential)


def roll_y(pair, places, lane):
    shift = 16 * places % 128
    turned = [pltpu.roll(half, shift, 1) for half in pair]
    wraps = lane < shift if places > 0 else lane >= shift
    return [jnp.where(wraps, turned[1], turned[0]), jnp.where(wraps, turned[0], turned[1])]


def filter_kernel(in_ref, out_ref, weight, buf_a, buf_b):
    scale = 2.0 / HALF_WIDTH
    centre = (-1.5 * C0 - SHIFT_MID) * scale
    side = [-0.5 * c * scale for c in (C1, C2, C3, C4)]
    y_of = lax.broadcasted_iota(jnp.int32, (16, 256), 0)
    lane_y = lax.broadcasted_iota(jnp.int32, (16, 256), 1) // 16
    spread = jnp.where(y_of == lane_y, 1.0, 0.0).astype(jnp.float32)
    for s in range(8):
        wide = dot_tn(in_ref[s, 256:272, :], spread) * scale + centre
        for xp in range(4):
            for yh in range(2):
                weight[8 * s + 2 * xp + yh] = wide[xp * 32 : xp * 32 + 32, yh * 128 : yh * 128 + 128]
    lane = lax.broadcasted_iota(jnp.int32, (32, 128), 1)

    def put(ref, plane, value):
        ref[plane, 8:40, :] = value
        ref[plane, 4:8, :] = value[28:32, :]
        ref[plane, 40:44, :] = value[0:4, :]

    def take(plane, _):
        put(buf_b, plane, in_ref[plane // 8, pl.ds((plane % 8) * 32, 32), :])
        return 0

    def apply(ref, x):
        near = [ref[2 * x + yh, 8:40, :] for yh in range(2)]
        total = [weight[2 * x + yh] * near[yh] for yh in range(2)]
        for m in range(1, 5):
            up, down = 2 * ((x + m) & 31), 2 * ((x + 32 - m) & 31)
            for yh in range(2):
                along_x = ref[up + yh, 8:40, :] + ref[down + yh, 8:40, :]
                along_z = ref[2 * x + yh, 8 - m : 40 - m, :] + ref[2 * x + yh, 8 + m : 40 + m, :]
                total[yh] = total[yh] + side[m - 1] * (along_x + along_z)
        forth, back = roll_y(near, 1, lane), roll_y(near, -1, lane)
        ahead = [side[1] * back[yh] + side[2] * near[yh] + side[3] * forth[yh] for yh in range(2)]
        behind = [side[1] * forth[yh] + side[2] * near[yh] + side[3] * back[yh] for yh in range(2)]
        ahead, behind = roll_y(ahead, 3, lane), roll_y(behind, -3, lane)
        return [total[yh] + (side[0] * (forth[yh] + back[yh]) + (ahead[yh] + behind[yh])) for yh in range(2)]

    def first(x, _):
        for yh, total in enumerate(apply(buf_b, x)):
            put(buf_a, 2 * x + yh, 0.5 * total)
        return 0

    def second(x, _):
        for yh, total in enumerate(apply(buf_a, x)):
            put(buf_b, 2 * x + yh, total - buf_b[2 * x + yh, 8:40, :])
        return 0

    def third(x, _):
        for yh, total in enumerate(apply(buf_b, x)):
            put(buf_a, 2 * x + yh, total - buf_a[2 * x + yh, 8:40, :])
        return 0

    def fourth(x, _):
        for yh, total in enumerate(apply(buf_a, x)):
            out_ref[2 * x + yh] = total - buf_b[2 * x + yh, 8:40, :]
        return 0

    lax.fori_loop(0, 64, take, 0, unroll=4)
    for step in (first, second, third, fourth):
        lax.fori_loop(0, 32, step, 0, unroll=4)


def chebyshev(received):
    out = pl.pallas_call(
        filter_kernel,
        out_shape=jax.ShapeDtypeStruct((64, 32, 128), jnp.float32),
        scratch_shapes=[pltpu.VMEM((64, 32, 128), jnp.float32)] + [pltpu.VMEM((64, 48, 128), jnp.float32)] * 2,
        compiler_params=pltpu.CompilerParams(vmem_limit_bytes=16 * MIB),
    )(received)
    return out.reshape(8, 256, 128)


def turn_kernel(in_ref, out_ref):
    turned = in_ref[0].T
    for yl in range(8):
        out_ref[:, yl * 256 : yl * 256 + 256] = turned[yl * 16 : yl * 16 + 16, :]


def turn(back, groups):
    return pl.pallas_call(
        turn_kernel,
        grid=(groups,),
        in_specs=[pl.BlockSpec((1, 256, 128), lambda i: (i, 0, 0))],
        out_specs=pl.BlockSpec((16, 2048), lambda i: (i, 0)),
        out_shape=jax.ShapeDtypeStruct((16 * groups, 2048), jnp.float32),
        compiler_params=pltpu.CompilerParams(vmem_limit_bytes=4 * MIB),
        cost_estimate=pl.CostEstimate(flops=groups * 500_000, bytes_accessed=groups * MIB // 4, transcendentals=0),
    )(back)


def ring(count, step):
    return [(i, (i + step) % count) for i in range(count)]


def gather_panel(own, field, xl):
    def right(block):
        return lax.ppermute(block, "z", ring(8, 1))

    def left(block):
        return lax.ppermute(block, "z", ring(8, -1))

    def swap(block):
        return lax.ppermute(block, "c", ring(2, 1))

    then = lax.optimization_barrier
    other, field = then((lax.ppermute(own, "xl", ring(2, 1)), field))
    pair = jnp.concatenate([jnp.where(xl == 0, own, other), jnp.where(xl == 0, other, own)], axis=0)
    right1, left1 = right(pair), left(pair)
    next_r, pair_s = then((right1, swap(pair)))
    right2, left2 = right(next_r), left(left1)
    next_r, right1_s = then((right2, swap(right1)))
    next_l, left1_s = then((left2, swap(left1)))
    right3, left3 = right(next_r), left(next_l)
    next_r, right2_s = then((right3, swap(right2)))
    next_l, left2_s = then((left3, swap(left2)))
    far = jnp.concatenate([right(next_r[:16]), left(next_l[16:])], axis=0)
    here = [pair, right1, left1, right2, left2, right3, left3, far]
    return here + [pair_s, right1_s, left1_s, right2_s, left2_s, swap(right3), swap(left3), swap(far)], field


OFFSETS = (0, -1, 1, -2, 2, -3, 3, 4)


def products_kernel(place_ref, *refs):
    blocks, (field_ref, home_ref, out_ref, panel_ref, acc, sems) = refs[:16], refs[16:]
    z, core = place_ref[1], place_ref[2]
    copies = []
    for half in range(2):
        points = pl.ds(half * 1024, 1024)
        for flip in range(2):
            for k, offset in enumerate(OFFSETS):
                first = (((z + offset) & 7) * 2 + (core ^ flip)) * 16
                target = panel_ref.at[:, pl.ds(pl.multiple_of(first, 16), 16), points]
                copies.append(pltpu.make_async_copy(blocks[flip * 8 + k].at[:, :, points], target, sems.at[len(copies)]))
                copies[-1].start()
    long = pl.ds(pl.multiple_of((1 - core) * 128, 128), 128)
    short = pl.ds(pl.multiple_of(core * 128, 128), 128)
    acc[...] = jnp.zeros_like(acc)

    def chunk(i, _):
        points = pl.ds(pl.multiple_of(i * 512, 512), 512)
        rows = jnp.concatenate([panel_ref[1, long, points], panel_ref[0, short, points], field_ref[:, points]], axis=0)
        acc[...] += dot_nt(rows, panel_ref[:, :, points].reshape(PANEL, 512))
        return 0

    for half in range(2):
        for copy in copies[half * 16 : half * 16 + 16]:
            copy.wait()
        if half:
            home = pltpu.make_async_copy(panel_ref, home_ref, sems.at[32])
            home.start()
        lax.fori_loop(half * 2, half * 2 + 2, chunk, 0)
    for s in range(8):
        rows = slice(s * 16, s * 16 + 16)
        lower = slice(128 + s * 16, 128 + s * 16 + 16)
        out_ref[s, :, 0:384] = acc[rows, 0:384]
        out_ref[s, :, 384:512] = jnp.where(core == 0, acc[rows, 384:512], acc[lower, 128:256])
        out_ref[s, :, 512:640] = acc[lower, 0:128]
        out_ref[s, :, 640:1152] = acc[256 + s * 16 : 256 + s * 16 + 16, :]
    home.wait()


def products(place, blocks, field):
    panel, terms = pl.pallas_call(
        products_kernel,
        in_specs=[pl.BlockSpec(memory_space=pltpu.SMEM)]
        + [pl.BlockSpec(memory_space=pl.ANY)] * 16
        + [pl.BlockSpec(memory_space=pltpu.VMEM)],
        out_shape=(jax.ShapeDtypeStruct((2, 256, 2048), jnp.float32), jax.ShapeDtypeStruct((8, 16, 1152), jnp.float32)),
        out_specs=(pl.BlockSpec(memory_space=pl.ANY), pl.BlockSpec(memory_space=pltpu.VMEM)),
        scratch_shapes=[
            pltpu.VMEM((2, 256, 2048), jnp.float32),
            pltpu.VMEM((384, 512), jnp.float32),
            pltpu.SemaphoreType.DMA((33,)),
        ],
        compiler_params=pltpu.CompilerParams(vmem_limit_bytes=BIG * MIB),
    )(place, *(block.reshape(2, 16, 2048) for block in blocks), field)
    return panel.reshape(PANEL, 2048), terms


def total_of(terms):
    while len(terms) > 1:
        terms = [terms[i] + terms[i + 1] for i in range(0, len(terms), 2)]
    return terms[0]


def eliminate(block):
    rows = lax.broadcasted_iota(jnp.int32, (8, 128), 0)
    lanes = lax.broadcasted_iota(jnp.int32, (8, 128), 1)

    def spread_row(tile, i):
        return jnp.broadcast_to(tile[i : i + 1, :], (8, 128))

    def spread_lane(tile, j):
        return jnp.broadcast_to(tile[:, j : j + 1], (8, 128))

    left = [block[8 * t : 8 * t + 8, :] for t in range(16)]
    right = [jnp.where(lanes == rows + 8 * t, 1.0, 0.0).astype(jnp.float32) for t in range(16)]
    out = []
    for t0 in range(16):
        columns = [spread_lane(left[t0], 8 * t0 + j) for j in range(8)]
        corner = [[spread_row(columns[j], i) for j in range(i + 1)] for i in range(8)]
        row_l = [spread_row(left[t0], i) for i in range(8)]
        row_r = [spread_row(right[t0], i) for i in range(8)]
        inverse, factor = [None] * 8, [[None] * 8 for _ in range(8)]
        for j in range(8):
            inverse[j] = 1.0 / corner[j][j]
            for i in range(j + 1, 8):
                factor[i][j] = corner[i][j] * inverse[j]
            for i in range(j + 1, 8):
                for k in range(j + 1, i + 1):
                    corner[i][k] = corner[i][k] - factor[i][j] * corner[k][j]
                row_l[i] = row_l[i] - factor[i][j] * row_l[j]
                row_r[i] = row_r[i] - factor[i][j] * row_r[j]
        own, pivot = row_r[0], corner[0][0]
        for i in range(1, 8):
            own, pivot = jnp.where(rows == i, row_r[i], own), jnp.where(rows == i, corner[i][i], pivot)
        root = lax.rsqrt(pivot)
        root = root * (1.5 - 0.5 * pivot * root * root)
        out.append(own * root)
        if t0 == 15:
            break
        solved_l, solved_r = [None] * 8, [None] * 8
        for k in range(7, -1, -1):
            u, v = row_l[k] * inverse[k], row_r[k] * inverse[k]
            for i in range(7, k, -1):
                u, v = u - factor[i][k] * solved_l[i], v - factor[i][k] * solved_r[i]
            solved_l[k], solved_r[k] = u, v
        for t in range(t0 + 1, 16):
            weights = [spread_lane(left[t], 8 * t0 + j) for j in range(8)]
            left[t] = left[t] - total_of([weights[j] * solved_l[j] for j in range(8)])
            right[t] = right[t] - total_of([weights[j] * solved_r[j] for j in range(8)])
    return jnp.concatenate(out, axis=0)


def invert(pieces, core, work, inv_ref):
    for flip, ref in enumerate(pieces):
        owner = core ^ flip
        for s in range(8):
            tile = ref[s] * (1.0 / POINTS)
            work[pl.ds(pl.multiple_of((3 - owner) * 128 + s * 16, 16), 16), 0:384] = tile[:, 0:384]
            square = pl.multiple_of((3 - 2 * owner) * 128, 128)
            work[pl.ds(pl.multiple_of(square + s * 16, 16), 16), pl.ds(square, 128)] = tile[:, 384:512]
            work[pl.ds(pl.multiple_of(owner * 128 + s * 16, 16), 16), 0:128] = tile[:, 512:640]
    inv_ref[...] = jnp.zeros_like(inv_ref)

    def diagonal(k, _):
        here = pl.ds(pl.multiple_of(k * 128, 128), 128)
        corner = eliminate(work[here, here])
        for kk in range(4):

            @pl.when(k == kk)
            def _(kk=kk, corner=corner):
                low, high = kk * 128, kk * 128 + 128
                if kk:
                    inv_ref[low:high, :low] = dot_nn(corner, inv_ref[low:high, :low])
                inv_ref[low:high, low:high] = corner
                if high < PANEL:
                    panel = dot_nt(work[high:, low:high], corner)
                    work[high:, high:] -= dot_nt(panel, panel)
                    inv_ref[high:, :high] -= dot_nn(panel, inv_ref[low:high, :high])

        return 0

    lax.fori_loop(0, 4, diagonal, 0)


def update_kernel(place_ref, sums_ref, by_core_ref, panel_ref, field_ref, out_ref, *scratch):
    work, inverse, coupling, mixer = scratch
    xl, z, core = place_ref[0], place_ref[1], place_ref[2]

    @pl.when(pl.program_id(0) == 0)
    def _():
        invert((sums_ref, by_core_ref), core, work, inverse)
        for s in range(8):
            coupling[s * 16 : s * 16 + 16, :] = sums_ref[s, :, 640:1152] * (1.0 / POINTS)
        factor = inverse[...]
        mixer[...] = -dot_nn(dot_nt(coupling[...], factor), factor)
        own = xl * 16 + z * 2 + core
        mixer[0:16, :] = inverse[pl.ds(pl.multiple_of(own * 16, 16), 16), :]

    keep = lax.broadcasted_iota(jnp.int32, (128, 256), 0) >= 16
    moved = (dot_nn(mixer[...], panel_ref[...]) + jnp.where(keep, field_ref[...], 0.0)).T
    for xp in range(4):
        for yh in range(2):
            out_ref[xp, yh, 0] = moved[xp * 64 + yh * 32 : xp * 64 + yh * 32 + 32, :]


def update(place, sums, by_core, panel, field):
    out = pl.pallas_call(
        update_kernel,
        grid=(8,),
        in_specs=[
            pl.BlockSpec(memory_space=pltpu.SMEM),
            pl.BlockSpec((8, 16, 1152), lambda i: (0, 0, 0)),
            pl.BlockSpec((8, 16, 640), lambda i: (0, 0, 0)),
            pl.BlockSpec((PANEL, 256), lambda i: (0, i)),
            pl.BlockSpec((128, 256), lambda i: (0, i)),
        ],
        out_specs=pl.BlockSpec((4, 2, 1, 32, 128), lambda i: (0, 0, i, 0, 0)),
        out_shape=jax.ShapeDtypeStruct((4, 2, 8, 32, 128), jnp.float32),
        scratch_shapes=[pltpu.VMEM((PANEL, PANEL), jnp.float32)] * 2 + [pltpu.VMEM((128, PANEL), jnp.float32)] * 2,
        compiler_params=pltpu.CompilerParams(vmem_limit_bytes=52 * MIB),
    )(place, sums, by_core, panel, field)
    return out.reshape(4, 16, 32, 128)


def per_device(orbitals, potential):
    xl, z, core = lax.axis_index("xl"), lax.axis_index("z"), lax.axis_index("c")
    place = jnp.stack([xl, z, core]).astype(jnp.int32)
    received = lax.all_to_all(pack(orbitals, potential), SPACE, 0, 0, tiled=True)
    back = lax.all_to_all(chebyshev(received), SPACE, 0, 0, tiled=True)
    blocks, field = gather_panel(turn(back, 1), turn(back, 8), xl)
    panel, terms = products(place, blocks, field)
    mine = jnp.sum(lax.all_to_all(terms, SPACE, 0, 0, tiled=True), axis=0)
    sums = lax.all_to_all(jnp.broadcast_to(mine, (8, 16, 1152)), SPACE, 0, 0, tiled=True)
    by_core = lax.ppermute(sums[:, :, :640], "c", ring(2, 1))
    return update(place, sums, by_core, panel, field)


def solution(mesh):
    fine = Mesh(mesh.devices.reshape(4, 2, 2, 8, 2), ("y", "xh", "xl", "z", "c"))
    return jax.shard_map(
        per_device,
        mesh=fine,
        in_specs=(P(SPACE, None, None, ("xl", "z", "c")), P(SPACE, None, None)),
        out_specs=P(SPACE, None, None, ("xl", "z", "c")),
        check_vma=False,
    )
```

```python
import functools

import jax
import jax.numpy as jnp
from jax import lax
from jax.experimental import pallas as pl
from jax.experimental.pallas import tpu as pltpu
from jax.sharding import Mesh, PartitionSpec as P

PANEL = 512
C0, C1, C2, C3, C4 = (-205.0 / 72.0, 8.0 / 5.0, -1.0 / 5.0, 8.0 / 315.0, -1.0 / 560.0)
SHIFT_MID = 7.25
HALF_WIDTH = 4.75
POINTS = 16384.0
SPACE = ("y", "xh")
HI = lax.Precision.HIGHEST
MIB = 1024 * 1024
BIG = 56


def dot_nn(a, b):
    return lax.dot_general(a, b, (((1,), (0,)), ((), ())), precision=HI, preferred_element_type=jnp.float32)


def dot_nt(a, b):
    return lax.dot_general(a, b, (((1,), (1,)), ((), ())), precision=HI, preferred_element_type=jnp.float32)


def dot_tn(a, b):
    return lax.dot_general(a, b, (((0,), (0,)), ((), ())), precision=HI, preferred_element_type=jnp.float32)


def swap_groups(arrays):
    arrays = list(arrays)
    group = lax.broadcasted_iota(jnp.int32, arrays[0].shape, 1) // 16
    for bit in (1, 2, 4):
        high = (group & bit) != 0
        for i in range(8):
            if i & bit:
                continue
            a, d = arrays[i], arrays[i | bit]
            arrays[i] = jnp.where(high, pltpu.roll(d, 16 * bit, 1), a)
            arrays[i | bit] = jnp.where(high, d, pltpu.roll(a, 128 - 16 * bit, 1))
    return arrays


def pack_kernel(orb_ref, pot_ref, out_ref, orb, pot, sems):
    copies = [pltpu.make_async_copy(orb_ref.at[xp], orb.at[xp], sems.at[xp]) for xp in range(4)]
    copies.append(pltpu.make_async_copy(pot_ref, pot, sems.at[4]))
    for copy in copies:
        copy.start()
    for xp in range(4):
        copies[xp].wait()
        for yh in range(2):
            parts = swap_groups([orb[xp, yh * 8 + yl] for yl in range(8)])
            for g in range(8):
                out_ref[g, xp * 64 + yh * 32 : xp * 64 + yh * 32 + 32, :] = parts[g]
    copies[4].wait()
    packed = jnp.concatenate([pot[p] for p in range(4)], axis=1)
    for g in range(8):
        out_ref[g, 256:272, :] = packed


def pack(orbitals, potential):
    return pl.pallas_call(
        pack_kernel,
        in_specs=[pl.BlockSpec(memory_space=pl.ANY)] * 2,
        out_specs=pl.BlockSpec(memory_space=pltpu.VMEM),
        out_shape=jax.ShapeDtypeStruct((8, 272, 128), jnp.float32),
        scratch_shapes=[
            pltpu.VMEM((4, 16, 32, 128), jnp.float32),
            pltpu.VMEM((4, 16, 32), jnp.float32),
            pltpu.SemaphoreType.DMA((5,)),
        ],
        compiler_params=pltpu.CompilerParams(vmem_limit_bytes=BIG * MIB),
    )(orbitals, potential)


def roll_y(pair, places, lane):
    shift = 16 * places % 128
    turned = [pltpu.roll(half, shift, 1) for half in pair]
    wraps = lane < shift if places > 0 else lane >= shift
    return [jnp.where(wraps, turned[1], turned[0]), jnp.where(wraps, turned[0], turned[1])]


def filter_kernel(in_ref, out_ref, weight, buf_a, buf_b):
    scale = 2.0 / HALF_WIDTH
    centre = (-1.5 * C0 - SHIFT_MID) * scale
    side = [-0.5 * c * scale for c in (C1, C2, C3, C4)]
    y_of = lax.broadcasted_iota(jnp.int32, (16, 256), 0)
    lane_y = lax.broadcasted_iota(jnp.int32, (16, 256), 1) // 16
    spread = jnp.where(y_of == lane_y, 1.0, 0.0).astype(jnp.float32)
    for s in range(8):
        wide = dot_tn(in_ref[s, 256:272, :], spread) * scale + centre
        for xp in range(4):
            for yh in range(2):
                weight[8 * s + 2 * xp + yh] = wide[xp * 32 : xp * 32 + 32, yh * 128 : yh * 128 + 128]
    lane = lax.broadcasted_iota(jnp.int32, (32, 128), 1)

    def put(ref, plane, value):
        ref[plane, 8:40, :] = value
        ref[plane, 4:8, :] = value[28:32, :]
        ref[plane, 40:44, :] = value[0:4, :]

    def take(plane, _):
        put(buf_b, plane, in_ref[plane // 8, pl.ds((plane % 8) * 32, 32), :])
        return 0

    def apply(ref, x):
        near = [ref[2 * x + yh, 8:40, :] for yh in range(2)]
        total = [weight[2 * x + yh] * near[yh] for yh in range(2)]
        for m in range(1, 5):
            up, down = 2 * ((x + m) & 31), 2 * ((x + 32 - m) & 31)
            for yh in range(2):
                along_x = ref[up + yh, 8:40, :] + ref[down + yh, 8:40, :]
                along_z = ref[2 * x + yh, 8 - m : 40 - m, :] + ref[2 * x + yh, 8 + m : 40 + m, :]
                total[yh] = total[yh] + side[m - 1] * (along_x + along_z)
        forth, back = roll_y(near, 1, lane), roll_y(near, -1, lane)
        ahead = [side[1] * back[yh] + side[2] * near[yh] + side[3] * forth[yh] for yh in range(2)]
        behind = [side[1] * forth[yh] + side[2] * near[yh] + side[3] * back[yh] for yh in range(2)]
        ahead, behind = roll_y(ahead, 3, lane), roll_y(behind, -3, lane)
        return [total[yh] + (side[0] * (forth[yh] + back[yh]) + (ahead[yh] + behind[yh])) for yh in range(2)]

    def first(x, _):
        for yh, total in enumerate(apply(buf_b, x)):
            put(buf_a, 2 * x + yh, 0.5 * total)
        return 0

    def second(x, _):
        for yh, total in enumerate(apply(buf_a, x)):
            put(buf_b, 2 * x + yh, total - buf_b[2 * x + yh, 8:40, :])
        return 0

    def third(x, _):
        for yh, total in enumerate(apply(buf_b, x)):
            put(buf_a, 2 * x + yh, total - buf_a[2 * x + yh, 8:40, :])
        return 0

    def fourth(x, _):
        for yh, total in enumerate(apply(buf_a, x)):
            out_ref[2 * x + yh] = total - buf_b[2 * x + yh, 8:40, :]
        return 0

    lax.fori_loop(0, 64, take, 0, unroll=4)
    for step in (first, second, third, fourth):
        lax.fori_loop(0, 32, step, 0, unroll=4)


def chebyshev(received):
    out = pl.pallas_call(
        filter_kernel,
        out_shape=jax.ShapeDtypeStruct((64, 32, 128), jnp.float32),
        scratch_shapes=[pltpu.VMEM((64, 32, 128), jnp.float32)] + [pltpu.VMEM((64, 48, 128), jnp.float32)] * 2,
        compiler_params=pltpu.CompilerParams(vmem_limit_bytes=16 * MIB),
    )(received)
    return out.reshape(8, 256, 128)


def turn_kernel(in_ref, out_ref):
    turned = in_ref[0].T
    for yl in range(8):
        out_ref[:, yl * 256 : yl * 256 + 256] = turned[yl * 16 : yl * 16 + 16, :]


def turn(back, groups):
    return pl.pallas_call(
        turn_kernel,
        grid=(groups,),
        in_specs=[pl.BlockSpec((1, 256, 128), lambda i: (i, 0, 0))],
        out_specs=pl.BlockSpec((16, 2048), lambda i: (i, 0)),
        out_shape=jax.ShapeDtypeStruct((16 * groups, 2048), jnp.float32),
        compiler_params=pltpu.CompilerParams(vmem_limit_bytes=4 * MIB),
        cost_estimate=pl.CostEstimate(flops=groups * 500_000, bytes_accessed=groups * MIB // 4, transcendentals=0),
    )(back)


def ring(count, step):
    return [(i, (i + step) % count) for i in range(count)]


def gather_panel(own, field, xl):
    def right(block):
        return lax.ppermute(block, "z", ring(8, 1))

    def left(block):
        return lax.ppermute(block, "z", ring(8, -1))

    def swap(block):
        return lax.ppermute(block, "c", ring(2, 1))

    then = lax.optimization_barrier
    other, field = then((lax.ppermute(own, "xl", ring(2, 1)), field))
    pair = jnp.concatenate([jnp.where(xl == 0, own, other), jnp.where(xl == 0, other, own)], axis=0)
    right1, left1 = right(pair), left(pair)
    next_r, pair_s = then((right1, swap(pair)))
    right2, left2 = right(next_r), left(left1)
    next_r, right1_s = then((right2, swap(right1)))
    next_l, left1_s = then((left2, swap(left1)))
    right3, left3 = right(next_r), left(next_l)
    next_r, right2_s = then((right3, swap(right2)))
    next_l, left2_s = then((left3, swap(left2)))
    far = jnp.concatenate([right(next_r[:16]), left(next_l[16:])], axis=0)
    here = [pair, right1, left1, right2, left2, right3, left3, far]
    return here + [pair_s, right1_s, left1_s, right2_s, left2_s, swap(right3), swap(left3), swap(far)], field


OFFSETS = (0, -1, 1, -2, 2, -3, 3, 4)


def products_kernel(place_ref, *refs):
    blocks, (field_ref, home_ref, out_ref, panel_ref, acc, corner, sems) = refs[:16], refs[16:]
    z, core = place_ref[1], place_ref[2]
    copies = []
    for half in range(2):
        points = pl.ds(half * 1024, 1024)
        for flip in range(2):
            for k, offset in enumerate(OFFSETS):
                first = (((z + offset) & 7) * 2 + (core ^ flip)) * 16
                target = panel_ref.at[:, pl.ds(pl.multiple_of(first, 16), 16), points]
                copies.append(pltpu.make_async_copy(blocks[flip * 8 + k].at[:, :, points], target, sems.at[len(copies)]))
                copies[-1].start()
    long = pl.ds(pl.multiple_of((1 - core) * 128, 128), 128)
    short = pl.ds(pl.multiple_of(core * 128, 128), 128)
    acc[...] = jnp.zeros_like(acc)
    corner[...] = jnp.zeros_like(corner)

    def chunk(i, _):
        points = pl.ds(pl.multiple_of(i * 512, 512), 512)
        rows = jnp.concatenate([panel_ref[1, long, points], field_ref[:, points]], axis=0)
        acc[...] += dot_nt(rows, panel_ref[:, :, points].reshape(PANEL, 512))
        corner[...] += dot_nt(panel_ref[0, short, points], panel_ref[0, :, points])
        return 0

    for half in range(2):
        for copy in copies[half * 16 : half * 16 + 16]:
            copy.wait()
        if half:
            home = pltpu.make_async_copy(panel_ref, home_ref, sems.at[32])
            home.start()
        lax.fori_loop(half * 2, half * 2 + 2, chunk, 0)
    for s in range(8):
        rows = slice(s * 16, s * 16 + 16)
        out_ref[s, :, 0:384] = acc[rows, 0:384]
        out_ref[s, :, 384:512] = jnp.where(core == 0, acc[rows, 384:512], corner[rows, 128:256])
        out_ref[s, :, 512:640] = corner[rows, 0:128]
        out_ref[s, :, 640:1152] = acc[128 + s * 16 : 128 + s * 16 + 16, :]
    home.wait()


def products(place, blocks, field):
    panel, terms = pl.pallas_call(
        products_kernel,
        in_specs=[pl.BlockSpec(memory_space=pltpu.SMEM)]
        + [pl.BlockSpec(memory_space=pl.ANY)] * 16
        + [pl.BlockSpec(memory_space=pltpu.VMEM)],
        out_shape=(jax.ShapeDtypeStruct((2, 256, 2048), jnp.float32), jax.ShapeDtypeStruct((8, 16, 1152), jnp.float32)),
        out_specs=(pl.BlockSpec(memory_space=pl.ANY), pl.BlockSpec(memory_space=pltpu.VMEM)),
        scratch_shapes=[
            pltpu.VMEM((2, 256, 2048), jnp.float32),
            pltpu.VMEM((256, 512), jnp.float32),
            pltpu.VMEM((128, 256), jnp.float32),
            pltpu.SemaphoreType.DMA((33,)),
        ],
        compiler_params=pltpu.CompilerParams(vmem_limit_bytes=BIG * MIB),
    )(place, *(block.reshape(2, 16, 2048) for block in blocks), field)
    return panel.reshape(PANEL, 2048), terms


def total_of(terms):
    while len(terms) > 1:
        terms = [terms[i] + terms[i + 1] for i in range(0, len(terms), 2)]
    return terms[0]


def eliminate(block):
    rows = lax.broadcasted_iota(jnp.int32, (8, 128), 0)
    lanes = lax.broadcasted_iota(jnp.int32, (8, 128), 1)

    def spread_row(tile, i):
        return jnp.broadcast_to(tile[i : i + 1, :], (8, 128))

    def spread_lane(tile, j):
        return jnp.broadcast_to(tile[:, j : j + 1], (8, 128))

    left = [block[8 * t : 8 * t + 8, :] for t in range(16)]
    right = [jnp.where(lanes == rows + 8 * t, 1.0, 0.0).astype(jnp.float32) for t in range(16)]
    out = []
    for t0 in range(16):
        columns = [spread_lane(left[t0], 8 * t0 + j) for j in range(8)]
        corner = [[spread_row(columns[j], i) for j in range(i + 1)] for i in range(8)]
        row_l = [spread_row(left[t0], i) for i in range(8)]
        row_r = [spread_row(right[t0], i) for i in range(8)]
        inverse, factor = [None] * 8, [[None] * 8 for _ in range(8)]
        for j in range(8):
            inverse[j] = 1.0 / corner[j][j]
            for i in range(j + 1, 8):
                factor[i][j] = corner[i][j] * inverse[j]
            for i in range(j + 1, 8):
                for k in range(j + 1, i + 1):
                    corner[i][k] = corner[i][k] - factor[i][j] * corner[k][j]
                row_l[i] = row_l[i] - factor[i][j] * row_l[j]
                row_r[i] = row_r[i] - factor[i][j] * row_r[j]
        own, pivot = row_r[0], corner[0][0]
        for i in range(1, 8):
            own, pivot = jnp.where(rows == i, row_r[i], own), jnp.where(rows == i, corner[i][i], pivot)
        root = lax.rsqrt(pivot)
        root = root * (1.5 - 0.5 * pivot * root * root)
        out.append(own * root)
        if t0 == 15:
            break
        solved_l, solved_r = [None] * 8, [None] * 8
        for k in range(7, -1, -1):
            u, v = row_l[k] * inverse[k], row_r[k] * inverse[k]
            for i in range(7, k, -1):
                u, v = u - factor[i][k] * solved_l[i], v - factor[i][k] * solved_r[i]
            solved_l[k], solved_r[k] = u, v
        for t in range(t0 + 1, 16):
            weights = [spread_lane(left[t], 8 * t0 + j) for j in range(8)]
            left[t] = left[t] - total_of([weights[j] * solved_l[j] for j in range(8)])
            right[t] = right[t] - total_of([weights[j] * solved_r[j] for j in range(8)])
    return jnp.concatenate(out, axis=0)


def invert(pieces, core, work, inv_ref):
    for flip, ref in enumerate(pieces):
        owner = core ^ flip
        for s in range(8):
            tile = ref[s] * (1.0 / POINTS)
            work[pl.ds(pl.multiple_of((3 - owner) * 128 + s * 16, 16), 16), 0:384] = tile[:, 0:384]
            square = pl.multiple_of((3 - 2 * owner) * 128, 128)
            work[pl.ds(pl.multiple_of(square + s * 16, 16), 16), pl.ds(square, 128)] = tile[:, 384:512]
            work[pl.ds(pl.multiple_of(owner * 128 + s * 16, 16), 16), 0:128] = tile[:, 512:640]
    inv_ref[...] = jnp.zeros_like(inv_ref)

    def diagonal(k, _):
        here = pl.ds(pl.multiple_of(k * 128, 128), 128)
        corner = eliminate(work[here, here])
        for kk in range(4):

            @pl.when(k == kk)
            def _(kk=kk, corner=corner):
                low, high = kk * 128, kk * 128 + 128
                if kk:
                    inv_ref[low:high, :low] = dot_nn(corner, inv_ref[low:high, :low])
                inv_ref[low:high, low:high] = corner
                if high < PANEL:
                    panel = dot_nt(work[high:, low:high], corner)
                    work[high:, high:] -= dot_nt(panel, panel)
                    inv_ref[high:, :high] -= dot_nn(panel, inv_ref[low:high, :high])

        return 0

    lax.fori_loop(0, 4, diagonal, 0)


def update_kernel(place_ref, sums_ref, by_core_ref, panel_ref, field_ref, out_ref, *scratch):
    work, inverse, coupling, mixer = scratch
    xl, z, core = place_ref[0], place_ref[1], place_ref[2]

    @pl.when(pl.program_id(0) == 0)
    def _():
        invert((sums_ref, by_core_ref), core, work, inverse)
        for s in range(8):
            coupling[s * 16 : s * 16 + 16, :] = sums_ref[s, :, 640:1152] * (1.0 / POINTS)
        factor = inverse[...]
        mixer[...] = -dot_nn(dot_nt(coupling[...], factor), factor)
        own = xl * 16 + z * 2 + core
        mixer[0:16, :] = inverse[pl.ds(pl.multiple_of(own * 16, 16), 16), :]

    keep = lax.broadcasted_iota(jnp.int32, (128, 512), 0) >= 16
    moved = (dot_nn(mixer[...], panel_ref[...]) + jnp.where(keep, field_ref[...], 0.0)).T
    for low in range(2):
        for xp in range(4):
            for yh in range(2):
                first = low * 256 + xp * 64 + yh * 32
                out_ref[xp, yh, low] = moved[first : first + 32, :]


def update(place, sums, by_core, panel, field):
    out = pl.pallas_call(
        update_kernel,
        grid=(4,),
        in_specs=[
            pl.BlockSpec(memory_space=pltpu.SMEM),
            pl.BlockSpec((8, 16, 1152), lambda i: (0, 0, 0)),
            pl.BlockSpec((8, 16, 640), lambda i: (0, 0, 0)),
            pl.BlockSpec((PANEL, 512), lambda i: (0, i)),
            pl.BlockSpec((128, 512), lambda i: (0, i)),
        ],
        out_specs=pl.BlockSpec((4, 2, 2, 32, 128), lambda i: (0, 0, i, 0, 0)),
        out_shape=jax.ShapeDtypeStruct((4, 2, 8, 32, 128), jnp.float32),
        scratch_shapes=[pltpu.VMEM((PANEL, PANEL), jnp.float32)] * 2 + [pltpu.VMEM((128, PANEL), jnp.float32)] * 2,
        compiler_params=pltpu.CompilerParams(vmem_limit_bytes=52 * MIB),
    )(place, sums, by_core, panel, field)
    return out.reshape(4, 16, 32, 128)


def per_device(orbitals, potential):
    xl, z, core = lax.axis_index("xl"), lax.axis_index("z"), lax.axis_index("c")
    place = jnp.stack([xl, z, core]).astype(jnp.int32)
    received = lax.all_to_all(pack(orbitals, potential), SPACE, 0, 0, tiled=True)
    back = lax.all_to_all(chebyshev(received), SPACE, 0, 0, tiled=True)
    blocks, field = gather_panel(turn(back, 1), turn(back, 8), xl)
    panel, terms = products(place, blocks, field)
    mine = jnp.sum(lax.all_to_all(terms, SPACE, 0, 0, tiled=True), axis=0)
    sums = lax.all_to_all(jnp.broadcast_to(mine, (8, 16, 1152)), SPACE, 0, 0, tiled=True)
    by_core = lax.ppermute(sums[:, :, :640], "c", ring(2, 1))
    return update(place, sums, by_core, panel, field)


def solution(mesh):
    fine = Mesh(mesh.devices.reshape(4, 2, 2, 8, 2), ("y", "xh", "xl", "z", "c"))
    return jax.shard_map(
        per_device,
        mesh=fine,
        in_specs=(P(SPACE, None, None, ("xl", "z", "c")), P(SPACE, None, None)),
        out_specs=P(SPACE, None, None, ("xl", "z", "c")),
        check_vma=False,
    )
```

```python
import functools

import jax
import jax.numpy as jnp
from jax import lax
from jax.experimental import pallas as pl
from jax.experimental.pallas import tpu as pltpu
from jax.sharding import Mesh, PartitionSpec as P

PANEL = 512
C0, C1, C2, C3, C4 = (-205.0 / 72.0, 8.0 / 5.0, -1.0 / 5.0, 8.0 / 315.0, -1.0 / 560.0)
SHIFT_MID = 7.25
HALF_WIDTH = 4.75
POINTS = 16384.0
SPACE = ("y", "xh")
HI = lax.Precision.HIGHEST
MIB = 1024 * 1024
BIG = 56


def dot_nn(a, b):
    return lax.dot_general(a, b, (((1,), (0,)), ((), ())), precision=HI, preferred_element_type=jnp.float32)


def dot_nt(a, b):
    return lax.dot_general(a, b, (((1,), (1,)), ((), ())), precision=HI, preferred_element_type=jnp.float32)


def dot_tn(a, b):
    return lax.dot_general(a, b, (((0,), (0,)), ((), ())), precision=HI, preferred_element_type=jnp.float32)


def swap_groups(arrays):
    arrays = list(arrays)
    group = lax.broadcasted_iota(jnp.int32, arrays[0].shape, 1) // 16
    for bit in (1, 2, 4):
        high = (group & bit) != 0
        for i in range(8):
            if i & bit:
                continue
            a, d = arrays[i], arrays[i | bit]
            arrays[i] = jnp.where(high, pltpu.roll(d, 16 * bit, 1), a)
            arrays[i | bit] = jnp.where(high, d, pltpu.roll(a, 128 - 16 * bit, 1))
    return arrays


def pack_kernel(orb_ref, pot_ref, sent_ref, orb, pot, out_ref, sems):
    copies = [pltpu.make_async_copy(orb_ref.at[xp], orb.at[xp], sems.at[xp]) for xp in range(4)]
    copies.append(pltpu.make_async_copy(pot_ref, pot, sems.at[4]))
    for copy in copies:
        copy.start()

    def send(first, count):
        rows = pl.ds(first, count)
        copies.append(pltpu.make_async_copy(out_ref.at[:, rows, :], sent_ref.at[:, rows, :], sems.at[len(copies)]))
        copies[-1].start()

    copies[4].wait()
    packed = jnp.concatenate([pot[p] for p in range(4)], axis=1)
    for g in range(8):
        out_ref[g, 256:272, :] = packed
    send(256, 16)
    for xp in range(4):
        copies[xp].wait()
        for yh in range(2):
            parts = swap_groups([orb[xp, yh * 8 + yl] for yl in range(8)])
            for g in range(8):
                out_ref[g, xp * 64 + yh * 32 : xp * 64 + yh * 32 + 32, :] = parts[g]
        send(xp * 64, 64)
    for copy in copies[5:]:
        copy.wait()


def pack(orbitals, potential):
    return pl.pallas_call(
        pack_kernel,
        in_specs=[pl.BlockSpec(memory_space=pl.ANY)] * 2,
        out_specs=pl.BlockSpec(memory_space=pl.ANY),
        out_shape=jax.ShapeDtypeStruct((8, 272, 128), jnp.float32),
        scratch_shapes=[
            pltpu.VMEM((4, 16, 32, 128), jnp.float32),
            pltpu.VMEM((4, 16, 32), jnp.float32),
            pltpu.VMEM((8, 272, 128), jnp.float32),
            pltpu.SemaphoreType.DMA((10,)),
        ],
        compiler_params=pltpu.CompilerParams(vmem_limit_bytes=BIG * MIB),
    )(orbitals, potential)


def roll_y(pair, places, lane):
    shift = 16 * places % 128
    turned = [pltpu.roll(half, shift, 1) for half in pair]
    wraps = lane < shift if places > 0 else lane >= shift
    return [jnp.where(wraps, turned[1], turned[0]), jnp.where(wraps, turned[0], turned[1])]


def filter_kernel(in_ref, out_ref, weight, buf_a, buf_b):
    scale = 2.0 / HALF_WIDTH
    centre = (-1.5 * C0 - SHIFT_MID) * scale
    side = [-0.5 * c * scale for c in (C1, C2, C3, C4)]
    y_of = lax.broadcasted_iota(jnp.int32, (16, 256), 0)
    lane_y = lax.broadcasted_iota(jnp.int32, (16, 256), 1) // 16
    spread = jnp.where(y_of == lane_y, 1.0, 0.0).astype(jnp.float32)
    for s in range(8):
        wide = dot_tn(in_ref[s, 256:272, :], spread) * scale + centre
        for xp in range(4):
            for yh in range(2):
                weight[8 * s + 2 * xp + yh] = wide[xp * 32 : xp * 32 + 32, yh * 128 : yh * 128 + 128]
    lane = lax.broadcasted_iota(jnp.int32, (32, 128), 1)

    def put(ref, plane, value):
        ref[plane, 8:40, :] = value
        ref[plane, 4:8, :] = value[28:32, :]
        ref[plane, 40:44, :] = value[0:4, :]

    def take(plane, _):
        put(buf_b, plane, in_ref[plane // 8, pl.ds((plane % 8) * 32, 32), :])
        return 0

    def apply(ref, x):
        near = [ref[2 * x + yh, 8:40, :] for yh in range(2)]
        total = [weight[2 * x + yh] * near[yh] for yh in range(2)]
        for m in range(1, 5):
            up, down = 2 * ((x + m) & 31), 2 * ((x + 32 - m) & 31)
            for yh in range(2):
                along_x = ref[up + yh, 8:40, :] + ref[down + yh, 8:40, :]
                along_z = ref[2 * x + yh, 8 - m : 40 - m, :] + ref[2 * x + yh, 8 + m : 40 + m, :]
                total[yh] = total[yh] + side[m - 1] * (along_x + along_z)
        forth, back = roll_y(near, 1, lane), roll_y(near, -1, lane)
        ahead = [side[1] * back[yh] + side[2] * near[yh] + side[3] * forth[yh] for yh in range(2)]
        behind = [side[1] * forth[yh] + side[2] * near[yh] + side[3] * back[yh] for yh in range(2)]
        ahead, behind = roll_y(ahead, 3, lane), roll_y(behind, -3, lane)
        return [total[yh] + (side[0] * (forth[yh] + back[yh]) + (ahead[yh] + behind[yh])) for yh in range(2)]

    def first(x, _):
        for yh, total in enumerate(apply(buf_b, x)):
            put(buf_a, 2 * x + yh, 0.5 * total)
        return 0

    def second(x, _):
        for yh, total in enumerate(apply(buf_a, x)):
            put(buf_b, 2 * x + yh, total - buf_b[2 * x + yh, 8:40, :])
        return 0

    def third(x, _):
        for yh, total in enumerate(apply(buf_b, x)):
            put(buf_a, 2 * x + yh, total - buf_a[2 * x + yh, 8:40, :])
        return 0

    def fourth(x, _):
        for yh, total in enumerate(apply(buf_a, x)):
            out_ref[2 * x + yh] = total - buf_b[2 * x + yh, 8:40, :]
        return 0

    lax.fori_loop(0, 64, take, 0, unroll=4)
    for step in (first, second, third, fourth):
        lax.fori_loop(0, 32, step, 0, unroll=4)


def chebyshev(received):
    out = pl.pallas_call(
        filter_kernel,
        out_shape=jax.ShapeDtypeStruct((64, 32, 128), jnp.float32),
        scratch_shapes=[pltpu.VMEM((64, 32, 128), jnp.float32)] + [pltpu.VMEM((64, 48, 128), jnp.float32)] * 2,
        compiler_params=pltpu.CompilerParams(vmem_limit_bytes=16 * MIB),
    )(received)
    return out.reshape(8, 256, 128)


def turn_kernel(in_ref, out_ref):
    turned = in_ref[0].T
    for yl in range(8):
        out_ref[:, yl * 256 : yl * 256 + 256] = turned[yl * 16 : yl * 16 + 16, :]


def turn(back, groups):
    return pl.pallas_call(
        turn_kernel,
        grid=(groups,),
        in_specs=[pl.BlockSpec((1, 256, 128), lambda i: (i, 0, 0))],
        out_specs=pl.BlockSpec((16, 2048), lambda i: (i, 0)),
        out_shape=jax.ShapeDtypeStruct((16 * groups, 2048), jnp.float32),
        compiler_params=pltpu.CompilerParams(vmem_limit_bytes=4 * MIB),
        cost_estimate=pl.CostEstimate(flops=groups * 500_000, bytes_accessed=groups * MIB // 4, transcendentals=0),
    )(back)


def ring(count, step):
    return [(i, (i + step) % count) for i in range(count)]


def gather_panel(own, field, xl):
    def right(block):
        return lax.ppermute(block, "z", ring(8, 1))

    def left(block):
        return lax.ppermute(block, "z", ring(8, -1))

    def swap(block):
        return lax.ppermute(block, "c", ring(2, 1))

    then = lax.optimization_barrier
    other, field = then((lax.ppermute(own, "xl", ring(2, 1)), field))
    pair = jnp.concatenate([jnp.where(xl == 0, own, other), jnp.where(xl == 0, other, own)], axis=0)
    right1, left1 = right(pair), left(pair)
    next_r, pair_s = then((right1, swap(pair)))
    right2, left2 = right(next_r), left(left1)
    next_r, right1_s = then((right2, swap(right1)))
    next_l, left1_s = then((left2, swap(left1)))
    right3, left3 = right(next_r), left(next_l)
    next_r, right2_s = then((right3, swap(right2)))
    next_l, left2_s = then((left3, swap(left2)))
    far = jnp.concatenate([right(next_r[:16]), left(next_l[16:])], axis=0)
    here = [pair, right1, left1, right2, left2, right3, left3, far]
    return here + [pair_s, right1_s, left1_s, right2_s, left2_s, swap(right3), swap(left3), swap(far)], field


OFFSETS = (0, -1, 1, -2, 2, -3, 3, 4)


def products_kernel(place_ref, *refs):
    blocks, (field_ref, home_ref, out_ref, panel_ref, acc, corner, sems) = refs[:16], refs[16:]
    z, core = place_ref[1], place_ref[2]
    copies = []
    for half in range(2):
        points = pl.ds(half * 1024, 1024)
        for flip in range(2):
            for k, offset in enumerate(OFFSETS):
                first = (((z + offset) & 7) * 2 + (core ^ flip)) * 16
                target = panel_ref.at[:, pl.ds(pl.multiple_of(first, 16), 16), points]
                copies.append(pltpu.make_async_copy(blocks[flip * 8 + k].at[:, :, points], target, sems.at[len(copies)]))
                copies[-1].start()
    long = pl.ds(pl.multiple_of((1 - core) * 128, 128), 128)
    short = pl.ds(pl.multiple_of(core * 128, 128), 128)
    acc[...] = jnp.zeros_like(acc)
    corner[...] = jnp.zeros_like(corner)

    def chunk(i, _):
        points = pl.ds(pl.multiple_of(i * 512, 512), 512)
        rows = jnp.concatenate([panel_ref[1, long, points], field_ref[:, points]], axis=0)
        acc[...] += dot_nt(rows, panel_ref[:, :, points].reshape(PANEL, 512))
        corner[...] += dot_nt(panel_ref[0, short, points], panel_ref[0, :, points])
        return 0

    homes = []
    for half in range(2):
        for copy in copies[half * 16 : half * 16 + 16]:
            copy.wait()
        for part in range(8):
            place = (slice(None), pl.ds(part * 32, 32), pl.ds(half * 1024, 1024))
            homes.append(pltpu.make_async_copy(panel_ref.at[place], home_ref.at[place], sems.at[32 + len(homes)]))
            homes[-1].start()
        lax.fori_loop(half * 2, half * 2 + 2, chunk, 0)
    for s in range(8):
        rows = slice(s * 16, s * 16 + 16)
        out_ref[s, :, 0:384] = acc[rows, 0:384]
        out_ref[s, :, 384:512] = jnp.where(core == 0, acc[rows, 384:512], corner[rows, 128:256])
        out_ref[s, :, 512:640] = corner[rows, 0:128]
        out_ref[s, :, 640:1152] = acc[128 + s * 16 : 128 + s * 16 + 16, :]
    for copy in homes:
        copy.wait()


def products(place, blocks, field):
    panel, terms = pl.pallas_call(
        products_kernel,
        in_specs=[pl.BlockSpec(memory_space=pltpu.SMEM)]
        + [pl.BlockSpec(memory_space=pl.ANY)] * 16
        + [pl.BlockSpec(memory_space=pltpu.VMEM)],
        out_shape=(jax.ShapeDtypeStruct((2, 256, 2048), jnp.float32), jax.ShapeDtypeStruct((8, 16, 1152), jnp.float32)),
        out_specs=(pl.BlockSpec(memory_space=pl.ANY), pl.BlockSpec(memory_space=pltpu.VMEM)),
        scratch_shapes=[
            pltpu.VMEM((2, 256, 2048), jnp.float32),
            pltpu.VMEM((256, 512), jnp.float32),
            pltpu.VMEM((128, 256), jnp.float32),
            pltpu.SemaphoreType.DMA((48,)),
        ],
        compiler_params=pltpu.CompilerParams(vmem_limit_bytes=BIG * MIB),
    )(place, *(block.reshape(2, 16, 2048) for block in blocks), field)
    return panel.reshape(PANEL, 2048), terms


def total_of(terms):
    while len(terms) > 1:
        terms = [terms[i] + terms[i + 1] for i in range(0, len(terms), 2)]
    return terms[0]


def eliminate(block):
    rows = lax.broadcasted_iota(jnp.int32, (8, 128), 0)
    lanes = lax.broadcasted_iota(jnp.int32, (8, 128), 1)

    def spread_row(tile, i):
        return jnp.broadcast_to(tile[i : i + 1, :], (8, 128))

    def spread_lane(tile, j):
        return jnp.broadcast_to(tile[:, j : j + 1], (8, 128))

    left = [block[8 * t : 8 * t + 8, :] for t in range(16)]
    right = [jnp.where(lanes == rows + 8 * t, 1.0, 0.0).astype(jnp.float32) for t in range(16)]
    out = []
    for t0 in range(16):
        columns = [spread_lane(left[t0], 8 * t0 + j) for j in range(8)]
        corner = [[spread_row(columns[j], i) for j in range(i + 1)] for i in range(8)]
        row_l = [spread_row(left[t0], i) for i in range(8)]
        row_r = [spread_row(right[t0], i) for i in range(8)]
        inverse, factor = [None] * 8, [[None] * 8 for _ in range(8)]
        for j in range(8):
            inverse[j] = 1.0 / corner[j][j]
            for i in range(j + 1, 8):
                factor[i][j] = corner[i][j] * inverse[j]
            for i in range(j + 1, 8):
                for k in range(j + 1, i + 1):
                    corner[i][k] = corner[i][k] - factor[i][j] * corner[k][j]
                row_l[i] = row_l[i] - factor[i][j] * row_l[j]
                row_r[i] = row_r[i] - factor[i][j] * row_r[j]
        own, pivot = row_r[0], corner[0][0]
        for i in range(1, 8):
            own, pivot = jnp.where(rows == i, row_r[i], own), jnp.where(rows == i, corner[i][i], pivot)
        root = lax.rsqrt(pivot)
        root = root * (1.5 - 0.5 * pivot * root * root)
        out.append(own * root)
        if t0 == 15:
            break
        solved_l, solved_r = [None] * 8, [None] * 8
        for k in range(7, -1, -1):
            u, v = row_l[k] * inverse[k], row_r[k] * inverse[k]
            for i in range(7, k, -1):
                u, v = u - factor[i][k] * solved_l[i], v - factor[i][k] * solved_r[i]
            solved_l[k], solved_r[k] = u, v
        for t in range(t0 + 1, 16):
            weights = [spread_lane(left[t], 8 * t0 + j) for j in range(8)]
            left[t] = left[t] - total_of([weights[j] * solved_l[j] for j in range(8)])
            right[t] = right[t] - total_of([weights[j] * solved_r[j] for j in range(8)])
    return jnp.concatenate(out, axis=0)


def invert(pieces, core, work, inv_ref):
    for flip, ref in enumerate(pieces):
        owner = core ^ flip
        for s in range(8):
            tile = ref[s] * (1.0 / POINTS)
            work[pl.ds(pl.multiple_of((3 - owner) * 128 + s * 16, 16), 16), 0:384] = tile[:, 0:384]
            square = pl.multiple_of((3 - 2 * owner) * 128, 128)
            work[pl.ds(pl.multiple_of(square + s * 16, 16), 16), pl.ds(square, 128)] = tile[:, 384:512]
            work[pl.ds(pl.multiple_of(owner * 128 + s * 16, 16), 16), 0:128] = tile[:, 512:640]
    inv_ref[...] = jnp.zeros_like(inv_ref)

    def diagonal(k, _):
        here = pl.ds(pl.multiple_of(k * 128, 128), 128)
        corner = eliminate(work[here, here])
        for kk in range(4):

            @pl.when(k == kk)
            def _(kk=kk, corner=corner):
                low, high = kk * 128, kk * 128 + 128
                if kk:
                    inv_ref[low:high, :low] = dot_nn(corner, inv_ref[low:high, :low])
                inv_ref[low:high, low:high] = corner
                if high < PANEL:
                    panel = dot_nt(work[high:, low:high], corner)
                    work[high:, high:] -= dot_nt(panel, panel)
                    inv_ref[high:, :high] -= dot_nn(panel, inv_ref[low:high, :high])

        return 0

    lax.fori_loop(0, 4, diagonal, 0)


def update_kernel(place_ref, sums_ref, by_core_ref, panel_ref, field_ref, out_ref, *scratch):
    work, inverse, coupling, mixer, held, sems = scratch
    xl, z, core = place_ref[0], place_ref[1], place_ref[2]

    @pl.when(pl.program_id(0) == 0)
    def _():
        copies = []
        for part in range(8):
            rows = pl.ds(part * 64, 64)
            copies.append(pltpu.make_async_copy(panel_ref.at[rows, :], held.at[rows, :], sems.at[part]))
            copies[-1].start()
        invert((sums_ref, by_core_ref), core, work, inverse)
        for s in range(8):
            coupling[s * 16 : s * 16 + 16, :] = sums_ref[s, :, 640:1152] * (1.0 / POINTS)
        factor = inverse[...]
        mixer[...] = -dot_nn(dot_nt(coupling[...], factor), factor)
        own = xl * 16 + z * 2 + core
        mixer[0:16, :] = inverse[pl.ds(pl.multiple_of(own * 16, 16), 16), :]
        for copy in copies:
            copy.wait()

    keep = lax.broadcasted_iota(jnp.int32, (128, 512), 0) >= 16
    points = pl.ds(pl.multiple_of(pl.program_id(0) * 512, 512), 512)
    moved = (dot_nn(mixer[...], held[:, points]) + jnp.where(keep, field_ref[...], 0.0)).T
    for low in range(2):
        for xp in range(4):
            for yh in range(2):
                first = low * 256 + xp * 64 + yh * 32
                out_ref[xp, yh, low] = moved[first : first + 32, :]


def update(place, sums, by_core, panel, field):
    out = pl.pallas_call(
        update_kernel,
        grid=(4,),
        in_specs=[
            pl.BlockSpec(memory_space=pltpu.SMEM),
            pl.BlockSpec((8, 16, 1152), lambda i: (0, 0, 0)),
            pl.BlockSpec((8, 16, 640), lambda i: (0, 0, 0)),
            pl.BlockSpec(memory_space=pl.ANY),
            pl.BlockSpec((128, 512), lambda i: (0, i)),
        ],
        out_specs=pl.BlockSpec((4, 2, 2, 32, 128), lambda i: (0, 0, i, 0, 0)),
        out_shape=jax.ShapeDtypeStruct((4, 2, 8, 32, 128), jnp.float32),
        scratch_shapes=[pltpu.VMEM((PANEL, PANEL), jnp.float32)] * 2
        + [pltpu.VMEM((128, PANEL), jnp.float32)] * 2
        + [pltpu.VMEM((PANEL, 2048), jnp.float32), pltpu.SemaphoreType.DMA((8,))],
        compiler_params=pltpu.CompilerParams(vmem_limit_bytes=52 * MIB),
    )(place, sums, by_core, panel, field)
    return out.reshape(4, 16, 32, 128)


def per_device(orbitals, potential):
    xl, z, core = lax.axis_index("xl"), lax.axis_index("z"), lax.axis_index("c")
    place = jnp.stack([xl, z, core]).astype(jnp.int32)
    received = lax.all_to_all(pack(orbitals, potential), SPACE, 0, 0, tiled=True)
    back = lax.all_to_all(chebyshev(received), SPACE, 0, 0, tiled=True)
    blocks, field = gather_panel(turn(back, 1), turn(back, 8), xl)
    panel, terms = products(place, blocks, field)
    mine = jnp.sum(lax.all_to_all(terms, SPACE, 0, 0, tiled=True), axis=0)
    sums = lax.all_to_all(jnp.broadcast_to(mine, (8, 16, 1152)), SPACE, 0, 0, tiled=True)
    by_core = lax.ppermute(sums[:, :, :640], "c", ring(2, 1))
    return update(place, sums, by_core, panel, field)


def solution(mesh):
    fine = Mesh(mesh.devices.reshape(4, 2, 2, 8, 2), ("y", "xh", "xl", "z", "c"))
    return jax.shard_map(
        per_device,
        mesh=fine,
        in_specs=(P(SPACE, None, None, ("xl", "z", "c")), P(SPACE, None, None)),
        out_specs=P(SPACE, None, None, ("xl", "z", "c")),
        check_vma=False,
    )
```

```python
import functools

import jax
import jax.numpy as jnp
from jax import lax
from jax.experimental import pallas as pl
from jax.experimental.pallas import tpu as pltpu
from jax.sharding import Mesh, PartitionSpec as P

PANEL = 512
C0, C1, C2, C3, C4 = (-205.0 / 72.0, 8.0 / 5.0, -1.0 / 5.0, 8.0 / 315.0, -1.0 / 560.0)
SHIFT_MID = 7.25
HALF_WIDTH = 4.75
POINTS = 16384.0
SPACE = ("y", "xh")
HI = lax.Precision.HIGHEST
MIB = 1024 * 1024
BIG = 56


def dot_nn(a, b):
    return lax.dot_general(a, b, (((1,), (0,)), ((), ())), precision=HI, preferred_element_type=jnp.float32)


def dot_nt(a, b):
    return lax.dot_general(a, b, (((1,), (1,)), ((), ())), precision=HI, preferred_element_type=jnp.float32)


def dot_tn(a, b):
    return lax.dot_general(a, b, (((0,), (0,)), ((), ())), precision=HI, preferred_element_type=jnp.float32)


def swap_groups(arrays):
    arrays = list(arrays)
    group = lax.broadcasted_iota(jnp.int32, arrays[0].shape, 1) // 16
    for bit in (1, 2, 4):
        high = (group & bit) != 0
        for i in range(8):
            if i & bit:
                continue
            a, d = arrays[i], arrays[i | bit]
            arrays[i] = jnp.where(high, pltpu.roll(d, 16 * bit, 1), a)
            arrays[i | bit] = jnp.where(high, d, pltpu.roll(a, 128 - 16 * bit, 1))
    return arrays


def pack_kernel(orb_ref, pot_ref, sent_ref, orb, pot, out_ref, sems):
    copies = [pltpu.make_async_copy(orb_ref.at[xp], orb.at[xp], sems.at[xp]) for xp in range(4)]
    copies.append(pltpu.make_async_copy(pot_ref, pot, sems.at[4]))
    for copy in copies:
        copy.start()

    def send(first, count):
        rows = pl.ds(first, count)
        copies.append(pltpu.make_async_copy(out_ref.at[:, rows, :], sent_ref.at[:, rows, :], sems.at[len(copies)]))
        copies[-1].start()

    copies[4].wait()
    packed = jnp.concatenate([pot[p] for p in range(4)], axis=1)
    for g in range(8):
        out_ref[g, 256:272, :] = packed
    send(256, 16)
    for xp in range(4):
        copies[xp].wait()
        for yh in range(2):
            parts = swap_groups([orb[xp, yh * 8 + yl] for yl in range(8)])
            for g in range(8):
                out_ref[g, xp * 64 + yh * 32 : xp * 64 + yh * 32 + 32, :] = parts[g]
        send(xp * 64, 64)
    for copy in copies[5:]:
        copy.wait()


def pack(orbitals, potential):
    return pl.pallas_call(
        pack_kernel,
        in_specs=[pl.BlockSpec(memory_space=pl.ANY)] * 2,
        out_specs=pl.BlockSpec(memory_space=pl.ANY),
        out_shape=jax.ShapeDtypeStruct((8, 272, 128), jnp.float32),
        scratch_shapes=[
            pltpu.VMEM((4, 16, 32, 128), jnp.float32),
            pltpu.VMEM((4, 16, 32), jnp.float32),
            pltpu.VMEM((8, 272, 128), jnp.float32),
            pltpu.SemaphoreType.DMA((10,)),
        ],
        compiler_params=pltpu.CompilerParams(vmem_limit_bytes=BIG * MIB),
    )(orbitals, potential)


def roll_y(pair, places, lane):
    shift = 16 * places % 128
    turned = [pltpu.roll(half, shift, 1) for half in pair]
    wraps = lane < shift if places > 0 else lane >= shift
    return [jnp.where(wraps, turned[1], turned[0]), jnp.where(wraps, turned[0], turned[1])]


def filter_kernel(in_ref, out_ref, weight, buf_a, buf_b):
    scale = 2.0 / HALF_WIDTH
    centre = (-1.5 * C0 - SHIFT_MID) * scale
    side = [-0.5 * c * scale for c in (C1, C2, C3, C4)]
    y_of = lax.broadcasted_iota(jnp.int32, (16, 256), 0)
    lane_y = lax.broadcasted_iota(jnp.int32, (16, 256), 1) // 16
    spread = jnp.where(y_of == lane_y, 1.0, 0.0).astype(jnp.float32)
    for s in range(8):
        wide = dot_tn(in_ref[s, 256:272, :], spread) * scale + centre
        for xp in range(4):
            for yh in range(2):
                weight[8 * s + 2 * xp + yh] = wide[xp * 32 : xp * 32 + 32, yh * 128 : yh * 128 + 128]
    lane = lax.broadcasted_iota(jnp.int32, (32, 128), 1)

    def put(ref, plane, value):
        ref[plane, 8:40, :] = value
        ref[plane, 4:8, :] = value[28:32, :]
        ref[plane, 40:44, :] = value[0:4, :]

    def take(plane, _):
        put(buf_b, plane, in_ref[plane // 8, pl.ds((plane % 8) * 32, 32), :])
        return 0

    def apply(ref, x):
        near = [ref[2 * x + yh, 8:40, :] for yh in range(2)]
        total = [weight[2 * x + yh] * near[yh] for yh in range(2)]
        for m in range(1, 5):
            up, down = 2 * ((x + m) & 31), 2 * ((x + 32 - m) & 31)
            for yh in range(2):
                along_x = ref[up + yh, 8:40, :] + ref[down + yh, 8:40, :]
                along_z = ref[2 * x + yh, 8 - m : 40 - m, :] + ref[2 * x + yh, 8 + m : 40 + m, :]
                total[yh] = total[yh] + side[m - 1] * (along_x + along_z)
        forth, back = roll_y(near, 1, lane), roll_y(near, -1, lane)
        ahead = [side[1] * back[yh] + side[2] * near[yh] + side[3] * forth[yh] for yh in range(2)]
        behind = [side[1] * forth[yh] + side[2] * near[yh] + side[3] * back[yh] for yh in range(2)]
        ahead, behind = roll_y(ahead, 3, lane), roll_y(behind, -3, lane)
        return [total[yh] + (side[0] * (forth[yh] + back[yh]) + (ahead[yh] + behind[yh])) for yh in range(2)]

    def first(x, _):
        for yh, total in enumerate(apply(buf_b, x)):
            put(buf_a, 2 * x + yh, 0.5 * total)
        return 0

    def second(x, _):
        for yh, total in enumerate(apply(buf_a, x)):
            put(buf_b, 2 * x + yh, total - buf_b[2 * x + yh, 8:40, :])
        return 0

    def third(x, _):
        for yh, total in enumerate(apply(buf_b, x)):
            put(buf_a, 2 * x + yh, total - buf_a[2 * x + yh, 8:40, :])
        return 0

    def fourth(x, _):
        for yh, total in enumerate(apply(buf_a, x)):
            out_ref[2 * x + yh] = total - buf_b[2 * x + yh, 8:40, :]
        return 0

    lax.fori_loop(0, 64, take, 0, unroll=4)
    for step in (first, second, third, fourth):
        lax.fori_loop(0, 32, step, 0, unroll=4)


def chebyshev(received):
    out = pl.pallas_call(
        filter_kernel,
        out_shape=jax.ShapeDtypeStruct((64, 32, 128), jnp.float32),
        scratch_shapes=[pltpu.VMEM((64, 32, 128), jnp.float32)] + [pltpu.VMEM((64, 48, 128), jnp.float32)] * 2,
        compiler_params=pltpu.CompilerParams(vmem_limit_bytes=16 * MIB),
    )(received)
    return out.reshape(8, 256, 128)


def turn_kernel(in_ref, out_ref):
    turned = in_ref[0].T
    for yl in range(8):
        out_ref[:, yl * 256 : yl * 256 + 256] = turned[yl * 16 : yl * 16 + 16, :]


def turn(back, groups):
    return pl.pallas_call(
        turn_kernel,
        grid=(groups,),
        in_specs=[pl.BlockSpec((1, 256, 128), lambda i: (i, 0, 0))],
        out_specs=pl.BlockSpec((16, 2048), lambda i: (i, 0)),
        out_shape=jax.ShapeDtypeStruct((16 * groups, 2048), jnp.float32),
        compiler_params=pltpu.CompilerParams(vmem_limit_bytes=4 * MIB),
        cost_estimate=pl.CostEstimate(flops=groups * 500_000, bytes_accessed=groups * MIB // 4, transcendentals=0),
    )(back)


def ring(count, step):
    return [(i, (i + step) % count) for i in range(count)]


def gather_panel(own, field, xl):
    def right(block):
        return lax.ppermute(block, "z", ring(8, 1))

    def left(block):
        return lax.ppermute(block, "z", ring(8, -1))

    def swap(block):
        return lax.ppermute(block, "c", ring(2, 1))

    then = lax.optimization_barrier
    other, field = then((lax.ppermute(own, "xl", ring(2, 1)), field))
    pair = jnp.concatenate([jnp.where(xl == 0, own, other), jnp.where(xl == 0, other, own)], axis=0)
    right1, left1 = right(pair), left(pair)
    next_r, pair_s = then((right1, swap(pair)))
    right2, left2 = right(next_r), left(left1)
    next_r, right1_s = then((right2, swap(right1)))
    next_l, left1_s = then((left2, swap(left1)))
    right3, left3 = right(next_r), left(next_l)
    next_r, right2_s = then((right3, swap(right2)))
    next_l, left2_s = then((left3, swap(left2)))
    far = jnp.concatenate([right(next_r[:16]), left(next_l[16:])], axis=0)
    here = [pair, right1, left1, right2, left2, right3, left3, far]
    return here + [pair_s, right1_s, left1_s, right2_s, left2_s, swap(right3), swap(left3), swap(far)], field


OFFSETS = (0, -1, 1, -2, 2, -3, 3, 4)


def collect(blocks, z, core, panel_ref, sems, cut, points):
    copies = []
    for flip in range(2):
        for k, offset in enumerate(OFFSETS):
            first = (((z + offset) & 7) * 2 + (core ^ flip)) * 16
            target = panel_ref.at[:, pl.ds(pl.multiple_of(first, 16), 16), points]
            source = blocks[flip * 8 + k].at[:, :, points]
            copies.append(pltpu.make_async_copy(source, target, sems.at[cut * 16 + len(copies)]))
            copies[-1].start()
    return copies


def products_kernel(place_ref, *refs):
    blocks, (field_ref, out_ref, panel_ref, acc, corner, sems) = refs[:16], refs[16:]
    z, core = place_ref[1], place_ref[2]
    copies = [collect(blocks, z, core, panel_ref, sems, cut, pl.ds(cut * 512, 512)) for cut in range(4)]
    long = pl.ds(pl.multiple_of((1 - core) * 128, 128), 128)
    short = pl.ds(pl.multiple_of(core * 128, 128), 128)
    acc[...] = jnp.zeros_like(acc)
    corner[...] = jnp.zeros_like(corner)

    for cut in range(4):
        for copy in copies[cut]:
            copy.wait()
        points = pl.ds(cut * 512, 512)
        rows = jnp.concatenate([panel_ref[1, long, points], field_ref[:, points]], axis=0)
        acc[...] += dot_nt(rows, panel_ref[:, :, points].reshape(PANEL, 512))
        corner[...] += dot_nt(panel_ref[0, short, points], panel_ref[0, :, points])
    for s in range(8):
        rows = slice(s * 16, s * 16 + 16)
        out_ref[s, :, 0:384] = acc[rows, 0:384]
        out_ref[s, :, 384:512] = jnp.where(core == 0, acc[rows, 384:512], corner[rows, 128:256])
        out_ref[s, :, 512:640] = corner[rows, 0:128]
        out_ref[s, :, 640:1152] = acc[128 + s * 16 : 128 + s * 16 + 16, :]


def products(place, blocks, field):
    return pl.pallas_call(
        products_kernel,
        in_specs=[pl.BlockSpec(memory_space=pltpu.SMEM)]
        + [pl.BlockSpec(memory_space=pl.ANY)] * 16
        + [pl.BlockSpec(memory_space=pltpu.VMEM)],
        out_shape=jax.ShapeDtypeStruct((8, 16, 1152), jnp.float32),
        scratch_shapes=[
            pltpu.VMEM((2, 256, 2048), jnp.float32),
            pltpu.VMEM((256, 512), jnp.float32),
            pltpu.VMEM((128, 256), jnp.float32),
            pltpu.SemaphoreType.DMA((64,)),
        ],
        compiler_params=pltpu.CompilerParams(vmem_limit_bytes=BIG * MIB),
    )(place, *blocks, field)


def total_of(terms):
    while len(terms) > 1:
        terms = [terms[i] + terms[i + 1] for i in range(0, len(terms), 2)]
    return terms[0]


def eliminate(block):
    rows = lax.broadcasted_iota(jnp.int32, (8, 128), 0)
    lanes = lax.broadcasted_iota(jnp.int32, (8, 128), 1)

    def spread_row(tile, i):
        return jnp.broadcast_to(tile[i : i + 1, :], (8, 128))

    def spread_lane(tile, j):
        return jnp.broadcast_to(tile[:, j : j + 1], (8, 128))

    left = [block[8 * t : 8 * t + 8, :] for t in range(16)]
    right = [jnp.where(lanes == rows + 8 * t, 1.0, 0.0).astype(jnp.float32) for t in range(16)]
    out = []
    for t0 in range(16):
        columns = [spread_lane(left[t0], 8 * t0 + j) for j in range(8)]
        corner = [[spread_row(columns[j], i) for j in range(i + 1)] for i in range(8)]
        row_l = [spread_row(left[t0], i) for i in range(8)]
        row_r = [spread_row(right[t0], i) for i in range(8)]
        inverse, factor = [None] * 8, [[None] * 8 for _ in range(8)]
        for j in range(8):
            inverse[j] = 1.0 / corner[j][j]
            for i in range(j + 1, 8):
                factor[i][j] = corner[i][j] * inverse[j]
            for i in range(j + 1, 8):
                for k in range(j + 1, i + 1):
                    corner[i][k] = corner[i][k] - factor[i][j] * corner[k][j]
                row_l[i] = row_l[i] - factor[i][j] * row_l[j]
                row_r[i] = row_r[i] - factor[i][j] * row_r[j]
        own, pivot = row_r[0], corner[0][0]
        for i in range(1, 8):
            own, pivot = jnp.where(rows == i, row_r[i], own), jnp.where(rows == i, corner[i][i], pivot)
        root = lax.rsqrt(pivot)
        root = root * (1.5 - 0.5 * pivot * root * root)
        out.append(own * root)
        if t0 == 15:
            break
        solved_l, solved_r = [None] * 8, [None] * 8
        for k in range(7, -1, -1):
            u, v = row_l[k] * inverse[k], row_r[k] * inverse[k]
            for i in range(7, k, -1):
                u, v = u - factor[i][k] * solved_l[i], v - factor[i][k] * solved_r[i]
            solved_l[k], solved_r[k] = u, v
        for t in range(t0 + 1, 16):
            weights = [spread_lane(left[t], 8 * t0 + j) for j in range(8)]
            left[t] = left[t] - total_of([weights[j] * solved_l[j] for j in range(8)])
            right[t] = right[t] - total_of([weights[j] * solved_r[j] for j in range(8)])
    return jnp.concatenate(out, axis=0)


def invert(pieces, core, work, inv_ref):
    for flip, ref in enumerate(pieces):
        owner = core ^ flip
        for s in range(8):
            tile = ref[s] * (1.0 / POINTS)
            work[pl.ds(pl.multiple_of((3 - owner) * 128 + s * 16, 16), 16), 0:384] = tile[:, 0:384]
            square = pl.multiple_of((3 - 2 * owner) * 128, 128)
            work[pl.ds(pl.multiple_of(square + s * 16, 16), 16), pl.ds(square, 128)] = tile[:, 384:512]
            work[pl.ds(pl.multiple_of(owner * 128 + s * 16, 16), 16), 0:128] = tile[:, 512:640]
    inv_ref[...] = jnp.zeros_like(inv_ref)

    def diagonal(k, _):
        here = pl.ds(pl.multiple_of(k * 128, 128), 128)
        corner = eliminate(work[here, here])
        for kk in range(4):

            @pl.when(k == kk)
            def _(kk=kk, corner=corner):
                low, high = kk * 128, kk * 128 + 128
                if kk:
                    inv_ref[low:high, :low] = dot_nn(corner, inv_ref[low:high, :low])
                inv_ref[low:high, low:high] = corner
                if high < PANEL:
                    panel = dot_nt(work[high:, low:high], corner)
                    work[high:, high:] -= dot_nt(panel, panel)
                    inv_ref[high:, :high] -= dot_nn(panel, inv_ref[low:high, :high])

        return 0

    lax.fori_loop(0, 4, diagonal, 0)


def update_kernel(place_ref, sums_ref, by_core_ref, field_ref, *refs):
    blocks, (out_ref, work, inverse, coupling, mixer, held, sems) = refs[:16], refs[16:]
    xl, z, core = place_ref[0], place_ref[1], place_ref[2]

    @pl.when(pl.program_id(0) == 0)
    def _():
        copies = collect(blocks, z, core, held, sems, 0, pl.ds(0, 2048))
        invert((sums_ref, by_core_ref), core, work, inverse)
        for s in range(8):
            coupling[s * 16 : s * 16 + 16, :] = sums_ref[s, :, 640:1152] * (1.0 / POINTS)
        factor = inverse[...]
        mixer[...] = -dot_nn(dot_nt(coupling[...], factor), factor)
        own = xl * 16 + z * 2 + core
        mixer[0:16, :] = inverse[pl.ds(pl.multiple_of(own * 16, 16), 16), :]
        for copy in copies:
            copy.wait()

    keep = lax.broadcasted_iota(jnp.int32, (128, 512), 0) >= 16
    points = pl.ds(pl.multiple_of(pl.program_id(0) * 512, 512), 512)
    moved = (dot_nn(mixer[...], held[:, :, points].reshape(PANEL, 512)) + jnp.where(keep, field_ref[...], 0.0)).T
    for low in range(2):
        for xp in range(4):
            for yh in range(2):
                first = low * 256 + xp * 64 + yh * 32
                out_ref[xp, yh, low] = moved[first : first + 32, :]


def update(place, sums, by_core, field, blocks):
    out = pl.pallas_call(
        update_kernel,
        grid=(4,),
        in_specs=[
            pl.BlockSpec(memory_space=pltpu.SMEM),
            pl.BlockSpec((8, 16, 1152), lambda i: (0, 0, 0)),
            pl.BlockSpec((8, 16, 640), lambda i: (0, 0, 0)),
            pl.BlockSpec((128, 512), lambda i: (0, i)),
            *[pl.BlockSpec(memory_space=pl.ANY)] * 16,
        ],
        out_specs=pl.BlockSpec((4, 2, 2, 32, 128), lambda i: (0, 0, i, 0, 0)),
        out_shape=jax.ShapeDtypeStruct((4, 2, 8, 32, 128), jnp.float32),
        scratch_shapes=[pltpu.VMEM((PANEL, PANEL), jnp.float32)] * 2
        + [pltpu.VMEM((128, PANEL), jnp.float32)] * 2
        + [pltpu.VMEM((2, 256, 2048), jnp.float32), pltpu.SemaphoreType.DMA((16,))],
        compiler_params=pltpu.CompilerParams(vmem_limit_bytes=48 * MIB),
    )(place, sums, by_core, field, *blocks)
    return out.reshape(4, 16, 32, 128)


def per_device(orbitals, potential):
    xl, z, core = lax.axis_index("xl"), lax.axis_index("z"), lax.axis_index("c")
    place = jnp.stack([xl, z, core]).astype(jnp.int32)
    received = lax.all_to_all(pack(orbitals, potential), SPACE, 0, 0, tiled=True)
    back = lax.all_to_all(chebyshev(received), SPACE, 0, 0, tiled=True)
    blocks, field = gather_panel(turn(back, 1), turn(back, 8), xl)
    blocks = [block.reshape(2, 16, 2048) for block in blocks]
    terms = products(place, blocks, field)
    mine = jnp.sum(lax.all_to_all(terms, SPACE, 0, 0, tiled=True), axis=0)
    sums = lax.all_to_all(jnp.broadcast_to(mine, (8, 16, 1152)), SPACE, 0, 0, tiled=True)
    by_core = lax.ppermute(sums[:, :, :640], "c", ring(2, 1))
    return update(place, sums, by_core, field, blocks)


def solution(mesh):
    fine = Mesh(mesh.devices.reshape(4, 2, 2, 8, 2), ("y", "xh", "xl", "z", "c"))
    return jax.shard_map(
        per_device,
        mesh=fine,
        in_specs=(P(SPACE, None, None, ("xl", "z", "c")), P(SPACE, None, None)),
        out_specs=P(SPACE, None, None, ("xl", "z", "c")),
        check_vma=False,
    )
```

```python
import functools

import jax
import jax.numpy as jnp
from jax import lax
from jax.experimental import pallas as pl
from jax.experimental.pallas import tpu as pltpu
from jax.sharding import Mesh, PartitionSpec as P

PANEL = 512
C0, C1, C2, C3, C4 = (-205.0 / 72.0, 8.0 / 5.0, -1.0 / 5.0, 8.0 / 315.0, -1.0 / 560.0)
SHIFT_MID = 7.25
HALF_WIDTH = 4.75
POINTS = 16384.0
SPACE = ("y", "xh")
HI = lax.Precision.HIGHEST
MIB = 1024 * 1024
BIG = 56


def dot_nn(a, b):
    return lax.dot_general(a, b, (((1,), (0,)), ((), ())), precision=HI, preferred_element_type=jnp.float32)


def dot_nt(a, b):
    return lax.dot_general(a, b, (((1,), (1,)), ((), ())), precision=HI, preferred_element_type=jnp.float32)


def dot_tn(a, b):
    return lax.dot_general(a, b, (((0,), (0,)), ((), ())), precision=HI, preferred_element_type=jnp.float32)


def swap_groups(arrays):
    arrays = list(arrays)
    group = lax.broadcasted_iota(jnp.int32, arrays[0].shape, 1) // 16
    for bit in (1, 2, 4):
        high = (group & bit) != 0
        for i in range(8):
            if i & bit:
                continue
            a, d = arrays[i], arrays[i | bit]
            arrays[i] = jnp.where(high, pltpu.roll(d, 16 * bit, 1), a)
            arrays[i | bit] = jnp.where(high, d, pltpu.roll(a, 128 - 16 * bit, 1))
    return arrays


def pack_kernel(orb_ref, pot_ref, sent_ref, orb, pot, out_ref, sems):
    copies = [pltpu.make_async_copy(orb_ref.at[xp], orb.at[xp], sems.at[xp]) for xp in range(4)]
    copies.append(pltpu.make_async_copy(pot_ref, pot, sems.at[4]))
    for copy in copies:
        copy.start()

    def send(first, count):
        rows = pl.ds(first, count)
        copies.append(pltpu.make_async_copy(out_ref.at[:, rows, :], sent_ref.at[:, rows, :], sems.at[len(copies)]))
        copies[-1].start()

    copies[4].wait()
    packed = jnp.concatenate([pot[p] for p in range(4)], axis=1)
    for g in range(8):
        out_ref[g, 256:272, :] = packed
    send(256, 16)
    for xp in range(4):
        copies[xp].wait()
        for yh in range(2):
            parts = swap_groups([orb[xp, yh * 8 + yl] for yl in range(8)])
            for g in range(8):
                out_ref[g, xp * 64 + yh * 32 : xp * 64 + yh * 32 + 32, :] = parts[g]
        send(xp * 64, 64)
    for copy in copies[5:]:
        copy.wait()


def pack(orbitals, potential):
    return pl.pallas_call(
        pack_kernel,
        in_specs=[pl.BlockSpec(memory_space=pl.ANY)] * 2,
        out_specs=pl.BlockSpec(memory_space=pl.ANY),
        out_shape=jax.ShapeDtypeStruct((8, 272, 128), jnp.float32),
        scratch_shapes=[
            pltpu.VMEM((4, 16, 32, 128), jnp.float32),
            pltpu.VMEM((4, 16, 32), jnp.float32),
            pltpu.VMEM((8, 272, 128), jnp.float32),
            pltpu.SemaphoreType.DMA((10,)),
        ],
        compiler_params=pltpu.CompilerParams(vmem_limit_bytes=BIG * MIB),
    )(orbitals, potential)


def roll_y(pair, places, lane):
    shift = 16 * places % 128
    turned = [pltpu.roll(half, shift, 1) for half in pair]
    wraps = lane < shift if places > 0 else lane >= shift
    return [jnp.where(wraps, turned[1], turned[0]), jnp.where(wraps, turned[0], turned[1])]


def filter_kernel(in_ref, out_ref, weight, buf_a, buf_b):
    scale = 2.0 / HALF_WIDTH
    centre = (-1.5 * C0 - SHIFT_MID) * scale
    side = [-0.5 * c * scale for c in (C1, C2, C3, C4)]
    y_of = lax.broadcasted_iota(jnp.int32, (16, 256), 0)
    lane_y = lax.broadcasted_iota(jnp.int32, (16, 256), 1) // 16
    spread = jnp.where(y_of == lane_y, 1.0, 0.0).astype(jnp.float32)
    for s in range(8):
        wide = dot_tn(in_ref[s, 256:272, :], spread) * scale + centre
        for xp in range(4):
            for yh in range(2):
                weight[8 * s + 2 * xp + yh] = wide[xp * 32 : xp * 32 + 32, yh * 128 : yh * 128 + 128]
    lane = lax.broadcasted_iota(jnp.int32, (32, 128), 1)

    def put(ref, plane, value):
        ref[plane, 8:40, :] = value
        ref[plane, 4:8, :] = value[28:32, :]
        ref[plane, 40:44, :] = value[0:4, :]

    def take(plane, _):
        put(buf_b, plane, in_ref[plane // 8, pl.ds((plane % 8) * 32, 32), :])
        return 0

    def apply(ref, x):
        near = [ref[2 * x + yh, 8:40, :] for yh in range(2)]
        total = [weight[2 * x + yh] * near[yh] for yh in range(2)]
        for m in range(1, 5):
            up, down = 2 * ((x + m) & 31), 2 * ((x + 32 - m) & 31)
            for yh in range(2):
                along_x = ref[up + yh, 8:40, :] + ref[down + yh, 8:40, :]
                along_z = ref[2 * x + yh, 8 - m : 40 - m, :] + ref[2 * x + yh, 8 + m : 40 + m, :]
                total[yh] = total[yh] + side[m - 1] * (along_x + along_z)
        forth, back = roll_y(near, 1, lane), roll_y(near, -1, lane)
        ahead = [side[1] * back[yh] + side[2] * near[yh] + side[3] * forth[yh] for yh in range(2)]
        behind = [side[1] * forth[yh] + side[2] * near[yh] + side[3] * back[yh] for yh in range(2)]
        ahead, behind = roll_y(ahead, 3, lane), roll_y(behind, -3, lane)
        return [total[yh] + (side[0] * (forth[yh] + back[yh]) + (ahead[yh] + behind[yh])) for yh in range(2)]

    def first(x, _):
        for yh, total in enumerate(apply(buf_b, x)):
            put(buf_a, 2 * x + yh, 0.5 * total)
        return 0

    def second(x, _):
        for yh, total in enumerate(apply(buf_a, x)):
            put(buf_b, 2 * x + yh, total - buf_b[2 * x + yh, 8:40, :])
        return 0

    def third(x, _):
        for yh, total in enumerate(apply(buf_b, x)):
            put(buf_a, 2 * x + yh, total - buf_a[2 * x + yh, 8:40, :])
        return 0

    def fourth(x, _):
        for yh, total in enumerate(apply(buf_a, x)):
            out_ref[2 * x + yh] = total - buf_b[2 * x + yh, 8:40, :]
        return 0

    lax.fori_loop(0, 64, take, 0, unroll=4)
    for step in (first, second, third, fourth):
        lax.fori_loop(0, 32, step, 0, unroll=4)


def chebyshev(received):
    out = pl.pallas_call(
        filter_kernel,
        out_shape=jax.ShapeDtypeStruct((64, 32, 128), jnp.float32),
        scratch_shapes=[pltpu.VMEM((64, 32, 128), jnp.float32)] + [pltpu.VMEM((64, 48, 128), jnp.float32)] * 2,
        compiler_params=pltpu.CompilerParams(vmem_limit_bytes=16 * MIB),
    )(received)
    return out.reshape(8, 256, 128)


def turn_kernel(in_ref, out_ref):
    turned = in_ref[0].T
    for yl in range(8):
        out_ref[:, yl * 256 : yl * 256 + 256] = turned[yl * 16 : yl * 16 + 16, :]


def turn(back, groups):
    return pl.pallas_call(
        turn_kernel,
        grid=(groups,),
        in_specs=[pl.BlockSpec((1, 256, 128), lambda i: (i, 0, 0))],
        out_specs=pl.BlockSpec((16, 2048), lambda i: (i, 0)),
        out_shape=jax.ShapeDtypeStruct((16 * groups, 2048), jnp.float32),
        compiler_params=pltpu.CompilerParams(vmem_limit_bytes=4 * MIB),
        cost_estimate=pl.CostEstimate(flops=groups * 500_000, bytes_accessed=groups * MIB // 4, transcendentals=0),
    )(back)


def ring(count, step):
    return [(i, (i + step) % count) for i in range(count)]


def gather_panel(own, field, xl):
    def right(block):
        return lax.ppermute(block, "z", ring(8, 1))

    def left(block):
        return lax.ppermute(block, "z", ring(8, -1))

    def swap(block):
        return lax.ppermute(block, "c", ring(2, 1))

    then = lax.optimization_barrier
    other, field = then((lax.ppermute(own, "xl", ring(2, 1)), field))
    pair = jnp.concatenate([jnp.where(xl == 0, own, other), jnp.where(xl == 0, other, own)], axis=0)
    right1, left1 = right(pair), left(pair)
    next_r, pair_s = then((right1, swap(pair)))
    right2, left2 = right(next_r), left(left1)
    next_r, right1_s = then((right2, swap(right1)))
    next_l, left1_s = then((left2, swap(left1)))
    right3, left3 = right(next_r), left(next_l)
    next_r, right2_s = then((right3, swap(right2)))
    next_l, left2_s = then((left3, swap(left2)))
    far = jnp.concatenate([right(next_r[:16]), left(next_l[16:])], axis=0)
    here = [pair, right1, left1, right2, left2, right3, left3, far]
    return here + [pair_s, right1_s, left1_s, right2_s, left2_s, swap(right3), swap(left3), swap(far)], field


OFFSETS = (0, -1, 1, -2, 2, -3, 3, 4)


def products_kernel(place_ref, *refs):
    blocks, (field_ref, home_ref, out_ref, panel_ref, acc, corner, sems) = refs[:16], refs[16:]
    z, core = place_ref[1], place_ref[2]
    copies = []
    for half in range(2):
        points = pl.ds(half * 1024, 1024)
        for flip in range(2):
            for k, offset in enumerate(OFFSETS):
                first = (((z + offset) & 7) * 2 + (core ^ flip)) * 16
                target = panel_ref.at[:, pl.ds(pl.multiple_of(first, 16), 16), points]
                copies.append(pltpu.make_async_copy(blocks[flip * 8 + k].at[:, :, points], target, sems.at[len(copies)]))
                copies[-1].start()
    long = pl.ds(pl.multiple_of((1 - core) * 128, 128), 128)
    short = pl.ds(pl.multiple_of(core * 128, 128), 128)
    acc[...] = jnp.zeros_like(acc)
    corner[...] = jnp.zeros_like(corner)

    def chunk(i, _):
        points = pl.ds(pl.multiple_of(i * 512, 512), 512)
        rows = jnp.concatenate([panel_ref[1, long, points], field_ref[:, points]], axis=0)
        acc[:, 256:512] += dot_nt(rows, panel_ref[1, :, points])
        low = dot_nt(jnp.concatenate([rows, panel_ref[0, short, points]], axis=0), panel_ref[0, :, points])
        acc[:, 0:256] += low[0:256]
        corner[...] += low[256:384]
        return 0

    homes = []
    for half in range(2):
        for copy in copies[half * 16 : half * 16 + 16]:
            copy.wait()
        for part in range(8):
            place = (slice(None), pl.ds(part * 32, 32), pl.ds(half * 1024, 1024))
            homes.append(pltpu.make_async_copy(panel_ref.at[place], home_ref.at[place], sems.at[32 + len(homes)]))
            homes[-1].start()
        lax.fori_loop(half * 2, half * 2 + 2, chunk, 0)
    for s in range(8):
        rows = slice(s * 16, s * 16 + 16)
        out_ref[s, :, 0:384] = acc[rows, 0:384]
        out_ref[s, :, 384:512] = jnp.where(core == 0, acc[rows, 384:512], corner[rows, 128:256])
        out_ref[s, :, 512:640] = corner[rows, 0:128]
        out_ref[s, :, 640:1152] = acc[128 + s * 16 : 128 + s * 16 + 16, :]
    for copy in homes:
        copy.wait()


def products(place, blocks, field):
    panel, terms = pl.pallas_call(
        products_kernel,
        in_specs=[pl.BlockSpec(memory_space=pltpu.SMEM)]
        + [pl.BlockSpec(memory_space=pl.ANY)] * 16
        + [pl.BlockSpec(memory_space=pltpu.VMEM)],
        out_shape=(jax.ShapeDtypeStruct((2, 256, 2048), jnp.float32), jax.ShapeDtypeStruct((8, 16, 1152), jnp.float32)),
        out_specs=(pl.BlockSpec(memory_space=pl.ANY), pl.BlockSpec(memory_space=pltpu.VMEM)),
        scratch_shapes=[
            pltpu.VMEM((2, 256, 2048), jnp.float32),
            pltpu.VMEM((256, 512), jnp.float32),
            pltpu.VMEM((128, 256), jnp.float32),
            pltpu.SemaphoreType.DMA((48,)),
        ],
        compiler_params=pltpu.CompilerParams(vmem_limit_bytes=BIG * MIB),
    )(place, *(block.reshape(2, 16, 2048) for block in blocks), field)
    return panel.reshape(PANEL, 2048), terms


def total_of(terms):
    while len(terms) > 1:
        terms = [terms[i] + terms[i + 1] for i in range(0, len(terms), 2)]
    return terms[0]


def eliminate(block):
    rows = lax.broadcasted_iota(jnp.int32, (8, 128), 0)
    lanes = lax.broadcasted_iota(jnp.int32, (8, 128), 1)

    def spread_row(tile, i):
        return jnp.broadcast_to(tile[i : i + 1, :], (8, 128))

    def spread_lane(tile, j):
        return jnp.broadcast_to(tile[:, j : j + 1], (8, 128))

    left = [block[8 * t : 8 * t + 8, :] for t in range(16)]
    right = [jnp.where(lanes == rows + 8 * t, 1.0, 0.0).astype(jnp.float32) for t in range(16)]
    out = []
    for t0 in range(16):
        columns = [spread_lane(left[t0], 8 * t0 + j) for j in range(8)]
        corner = [[spread_row(columns[j], i) for j in range(i + 1)] for i in range(8)]
        row_l = [spread_row(left[t0], i) for i in range(8)]
        row_r = [spread_row(right[t0], i) for i in range(8)]
        inverse, factor = [None] * 8, [[None] * 8 for _ in range(8)]
        for j in range(8):
            inverse[j] = 1.0 / corner[j][j]
            for i in range(j + 1, 8):
                factor[i][j] = corner[i][j] * inverse[j]
            for i in range(j + 1, 8):
                for k in range(j + 1, i + 1):
                    corner[i][k] = corner[i][k] - factor[i][j] * corner[k][j]
                row_l[i] = row_l[i] - factor[i][j] * row_l[j]
                row_r[i] = row_r[i] - factor[i][j] * row_r[j]
        own, pivot = row_r[0], corner[0][0]
        for i in range(1, 8):
            own, pivot = jnp.where(rows == i, row_r[i], own), jnp.where(rows == i, corner[i][i], pivot)
        root = lax.rsqrt(pivot)
        root = root * (1.5 - 0.5 * pivot * root * root)
        out.append(own * root)
        if t0 == 15:
            break
        solved_l, solved_r = [None] * 8, [None] * 8
        for k in range(7, -1, -1):
            u, v = row_l[k] * inverse[k], row_r[k] * inverse[k]
            for i in range(7, k, -1):
                u, v = u - factor[i][k] * solved_l[i], v - factor[i][k] * solved_r[i]
            solved_l[k], solved_r[k] = u, v
        for t in range(t0 + 1, 16):
            weights = [spread_lane(left[t], 8 * t0 + j) for j in range(8)]
            left[t] = left[t] - total_of([weights[j] * solved_l[j] for j in range(8)])
            right[t] = right[t] - total_of([weights[j] * solved_r[j] for j in range(8)])
    return jnp.concatenate(out, axis=0)


def invert(pieces, core, work, inv_ref):
    for flip, ref in enumerate(pieces):
        owner = core ^ flip
        for s in range(8):
            tile = ref[s] * (1.0 / POINTS)
            work[pl.ds(pl.multiple_of((3 - owner) * 128 + s * 16, 16), 16), 0:384] = tile[:, 0:384]
            square = pl.multiple_of((3 - 2 * owner) * 128, 128)
            work[pl.ds(pl.multiple_of(square + s * 16, 16), 16), pl.ds(square, 128)] = tile[:, 384:512]
            work[pl.ds(pl.multiple_of(owner * 128 + s * 16, 16), 16), 0:128] = tile[:, 512:640]
    inv_ref[...] = jnp.zeros_like(inv_ref)

    def diagonal(k, _):
        here = pl.ds(pl.multiple_of(k * 128, 128), 128)
        corner = eliminate(work[here, here])
        for kk in range(4):

            @pl.when(k == kk)
            def _(kk=kk, corner=corner):
                low, high = kk * 128, kk * 128 + 128
                if kk:
                    inv_ref[low:high, :low] = dot_nn(corner, inv_ref[low:high, :low])
                inv_ref[low:high, low:high] = corner
                if high < PANEL:
                    panel = dot_nt(work[high:, low:high], corner)
                    work[high:, high:] -= dot_nt(panel, panel)
                    inv_ref[high:, :high] -= dot_nn(panel, inv_ref[low:high, :high])

        return 0

    lax.fori_loop(0, 4, diagonal, 0)


def update_kernel(place_ref, sums_ref, by_core_ref, panel_ref, field_ref, out_ref, *scratch):
    work, inverse, coupling, mixer, held, sems = scratch
    xl, z, core = place_ref[0], place_ref[1], place_ref[2]

    @pl.when(pl.program_id(0) == 0)
    def _():
        copies = []
        for part in range(8):
            rows = pl.ds(part * 64, 64)
            copies.append(pltpu.make_async_copy(panel_ref.at[rows, :], held.at[rows, :], sems.at[part]))
            copies[-1].start()
        invert((sums_ref, by_core_ref), core, work, inverse)
        for s in range(8):
            coupling[s * 16 : s * 16 + 16, :] = sums_ref[s, :, 640:1152] * (1.0 / POINTS)
        factor = inverse[...]
        mixer[...] = -dot_nn(dot_nt(coupling[...], factor), factor)
        own = xl * 16 + z * 2 + core
        mixer[0:16, :] = inverse[pl.ds(pl.multiple_of(own * 16, 16), 16), :]
        for copy in copies:
            copy.wait()

    keep = lax.broadcasted_iota(jnp.int32, (128, 512), 0) >= 16
    points = pl.ds(pl.multiple_of(pl.program_id(0) * 512, 512), 512)
    moved = (dot_nn(mixer[...], held[:, points]) + jnp.where(keep, field_ref[...], 0.0)).T
    for low in range(2):
        for xp in range(4):
            for yh in range(2):
                first = low * 256 + xp * 64 + yh * 32
                out_ref[xp, yh, low] = moved[first : first + 32, :]


def update(place, sums, by_core, panel, field):
    out = pl.pallas_call(
        update_kernel,
        grid=(4,),
        in_specs=[
            pl.BlockSpec(memory_space=pltpu.SMEM),
            pl.BlockSpec((8, 16, 1152), lambda i: (0, 0, 0)),
            pl.BlockSpec((8, 16, 640), lambda i: (0, 0, 0)),
            pl.BlockSpec(memory_space=pl.ANY),
            pl.BlockSpec((128, 512), lambda i: (0, i)),
        ],
        out_specs=pl.BlockSpec((4, 2, 2, 32, 128), lambda i: (0, 0, i, 0, 0)),
        out_shape=jax.ShapeDtypeStruct((4, 2, 8, 32, 128), jnp.float32),
        scratch_shapes=[pltpu.VMEM((PANEL, PANEL), jnp.float32)] * 2
        + [pltpu.VMEM((128, PANEL), jnp.float32)] * 2
        + [pltpu.VMEM((PANEL, 2048), jnp.float32), pltpu.SemaphoreType.DMA((8,))],
        compiler_params=pltpu.CompilerParams(vmem_limit_bytes=52 * MIB),
    )(place, sums, by_core, panel, field)
    return out.reshape(4, 16, 32, 128)


def per_device(orbitals, potential):
    xl, z, core = lax.axis_index("xl"), lax.axis_index("z"), lax.axis_index("c")
    place = jnp.stack([xl, z, core]).astype(jnp.int32)
    received = lax.all_to_all(pack(orbitals, potential), SPACE, 0, 0, tiled=True)
    back = lax.all_to_all(chebyshev(received), SPACE, 0, 0, tiled=True)
    blocks, field = gather_panel(turn(back, 1), turn(back, 8), xl)
    panel, terms = products(place, blocks, field)
    mine = jnp.sum(lax.all_to_all(terms, SPACE, 0, 0, tiled=True), axis=0)
    sums = lax.all_to_all(jnp.broadcast_to(mine, (8, 16, 1152)), SPACE, 0, 0, tiled=True)
    by_core = lax.ppermute(sums[:, :, :640], "c", ring(2, 1))
    return update(place, sums, by_core, panel, field)


def solution(mesh):
    fine = Mesh(mesh.devices.reshape(4, 2, 2, 8, 2), ("y", "xh", "xl", "z", "c"))
    return jax.shard_map(
        per_device,
        mesh=fine,
        in_specs=(P(SPACE, None, None, ("xl", "z", "c")), P(SPACE, None, None)),
        out_specs=P(SPACE, None, None, ("xl", "z", "c")),
        check_vma=False,
    )
```

```python
import functools

import jax
import jax.numpy as jnp
from jax import lax
from jax.experimental import pallas as pl
from jax.experimental.pallas import tpu as pltpu
from jax.sharding import Mesh, PartitionSpec as P

PANEL = 512
C0, C1, C2, C3, C4 = (-205.0 / 72.0, 8.0 / 5.0, -1.0 / 5.0, 8.0 / 315.0, -1.0 / 560.0)
SHIFT_MID = 7.25
HALF_WIDTH = 4.75
POINTS = 16384.0
SPACE = ("y", "xh")
HI = lax.Precision.HIGHEST
MIB = 1024 * 1024
BIG = 56


def dot_nn(a, b):
    return lax.dot_general(a, b, (((1,), (0,)), ((), ())), precision=HI, preferred_element_type=jnp.float32)


def dot_nt(a, b):
    return lax.dot_general(a, b, (((1,), (1,)), ((), ())), precision=HI, preferred_element_type=jnp.float32)


def dot_tn(a, b):
    return lax.dot_general(a, b, (((0,), (0,)), ((), ())), precision=HI, preferred_element_type=jnp.float32)


def swap_groups(arrays):
    arrays = list(arrays)
    group = lax.broadcasted_iota(jnp.int32, arrays[0].shape, 1) // 16
    for bit in (1, 2, 4):
        high = (group & bit) != 0
        for i in range(8):
            if i & bit:
                continue
            a, d = arrays[i], arrays[i | bit]
            arrays[i] = jnp.where(high, pltpu.roll(d, 16 * bit, 1), a)
            arrays[i | bit] = jnp.where(high, d, pltpu.roll(a, 128 - 16 * bit, 1))
    return arrays


def pack_kernel(orb_ref, pot_ref, sent_ref, orb, pot, out_ref, sems):
    copies = [pltpu.make_async_copy(orb_ref.at[xp], orb.at[xp], sems.at[xp]) for xp in range(4)]
    copies.append(pltpu.make_async_copy(pot_ref, pot, sems.at[4]))
    for copy in copies:
        copy.start()

    def send(first, count):
        rows = pl.ds(first, count)
        copies.append(pltpu.make_async_copy(out_ref.at[:, rows, :], sent_ref.at[:, rows, :], sems.at[len(copies)]))
        copies[-1].start()

    copies[4].wait()
    packed = jnp.concatenate([pot[p] for p in range(4)], axis=1)
    for g in range(8):
        out_ref[g, 256:272, :] = packed
    send(256, 16)
    for xp in range(4):
        copies[xp].wait()
        for yh in range(2):
            parts = swap_groups([orb[xp, yh * 8 + yl] for yl in range(8)])
            for g in range(8):
                out_ref[g, xp * 64 + yh * 32 : xp * 64 + yh * 32 + 32, :] = parts[g]
        send(xp * 64, 64)
    for copy in copies[5:]:
        copy.wait()


def pack(orbitals, potential):
    return pl.pallas_call(
        pack_kernel,
        in_specs=[pl.BlockSpec(memory_space=pl.ANY)] * 2,
        out_specs=pl.BlockSpec(memory_space=pl.ANY),
        out_shape=jax.ShapeDtypeStruct((8, 272, 128), jnp.float32),
        scratch_shapes=[
            pltpu.VMEM((4, 16, 32, 128), jnp.float32),
            pltpu.VMEM((4, 16, 32), jnp.float32),
            pltpu.VMEM((8, 272, 128), jnp.float32),
            pltpu.SemaphoreType.DMA((10,)),
        ],
        compiler_params=pltpu.CompilerParams(vmem_limit_bytes=BIG * MIB),
    )(orbitals, potential)


def roll_y(pair, places, lane):
    shift = 16 * places % 128
    turned = [pltpu.roll(half, shift, 1) for half in pair]
    wraps = lane < shift if places > 0 else lane >= shift
    return [jnp.where(wraps, turned[1], turned[0]), jnp.where(wraps, turned[0], turned[1])]


def filter_kernel(in_ref, out_ref, weight, buf_a, buf_b):
    scale = 2.0 / HALF_WIDTH
    centre = (-1.5 * C0 - SHIFT_MID) * scale
    side = [-0.5 * c * scale for c in (C1, C2, C3, C4)]
    y_of = lax.broadcasted_iota(jnp.int32, (16, 256), 0)
    lane_y = lax.broadcasted_iota(jnp.int32, (16, 256), 1) // 16
    spread = jnp.where(y_of == lane_y, 1.0, 0.0).astype(jnp.float32)
    for s in range(8):
        wide = dot_tn(in_ref[s, 256:272, :], spread) * scale + centre
        for xp in range(4):
            for yh in range(2):
                weight[8 * s + 2 * xp + yh] = wide[xp * 32 : xp * 32 + 32, yh * 128 : yh * 128 + 128]
    lane = lax.broadcasted_iota(jnp.int32, (32, 128), 1)

    def put(ref, plane, value):
        ref[plane, 8:40, :] = value
        ref[plane, 4:8, :] = value[28:32, :]
        ref[plane, 40:44, :] = value[0:4, :]

    def take(plane, _):
        put(buf_b, plane, in_ref[plane // 8, pl.ds((plane % 8) * 32, 32), :])
        return 0

    def apply(ref, x):
        near = [ref[2 * x + yh, 8:40, :] for yh in range(2)]
        total = [weight[2 * x + yh] * near[yh] for yh in range(2)]
        for m in range(1, 5):
            up, down = 2 * ((x + m) & 31), 2 * ((x + 32 - m) & 31)
            for yh in range(2):
                along_x = ref[up + yh, 8:40, :] + ref[down + yh, 8:40, :]
                along_z = ref[2 * x + yh, 8 - m : 40 - m, :] + ref[2 * x + yh, 8 + m : 40 + m, :]
                total[yh] = total[yh] + side[m - 1] * (along_x + along_z)
        forth, back = roll_y(near, 1, lane), roll_y(near, -1, lane)
        ahead = [side[1] * back[yh] + side[2] * near[yh] + side[3] * forth[yh] for yh in range(2)]
        behind = [side[1] * forth[yh] + side[2] * near[yh] + side[3] * back[yh] for yh in range(2)]
        ahead, behind = roll_y(ahead, 3, lane), roll_y(behind, -3, lane)
        return [total[yh] + (side[0] * (forth[yh] + back[yh]) + (ahead[yh] + behind[yh])) for yh in range(2)]

    def first(x, _):
        for yh, total in enumerate(apply(buf_b, x)):
            put(buf_a, 2 * x + yh, 0.5 * total)
        return 0

    def second(x, _):
        for yh, total in enumerate(apply(buf_a, x)):
            put(buf_b, 2 * x + yh, total - buf_b[2 * x + yh, 8:40, :])
        return 0

    def third(x, _):
        for yh, total in enumerate(apply(buf_b, x)):
            put(buf_a, 2 * x + yh, total - buf_a[2 * x + yh, 8:40, :])
        return 0

    def fourth(x, _):
        for yh, total in enumerate(apply(buf_a, x)):
            out_ref[2 * x + yh] = total - buf_b[2 * x + yh, 8:40, :]
        return 0

    lax.fori_loop(0, 64, take, 0, unroll=4)
    for step in (first, second, third, fourth):
        lax.fori_loop(0, 32, step, 0, unroll=4)


def chebyshev(received):
    out = pl.pallas_call(
        filter_kernel,
        out_shape=jax.ShapeDtypeStruct((64, 32, 128), jnp.float32),
        scratch_shapes=[pltpu.VMEM((64, 32, 128), jnp.float32)] + [pltpu.VMEM((64, 48, 128), jnp.float32)] * 2,
        compiler_params=pltpu.CompilerParams(vmem_limit_bytes=16 * MIB),
    )(received)
    return out.reshape(8, 256, 128)


def turn_kernel(in_ref, out_ref):
    turned = in_ref[0].T
    for yl in range(8):
        out_ref[:, yl * 256 : yl * 256 + 256] = turned[yl * 16 : yl * 16 + 16, :]


def turn(back, groups):
    return pl.pallas_call(
        turn_kernel,
        grid=(groups,),
        in_specs=[pl.BlockSpec((1, 256, 128), lambda i: (i, 0, 0))],
        out_specs=pl.BlockSpec((16, 2048), lambda i: (i, 0)),
        out_shape=jax.ShapeDtypeStruct((16 * groups, 2048), jnp.float32),
        compiler_params=pltpu.CompilerParams(vmem_limit_bytes=4 * MIB),
        cost_estimate=pl.CostEstimate(flops=groups * 500_000, bytes_accessed=groups * MIB // 4, transcendentals=0),
    )(back)


def ring(count, step):
    return [(i, (i + step) % count) for i in range(count)]


def gather_panel(own, field, xl):
    def right(block):
        return lax.ppermute(block, "z", ring(8, 1))

    def left(block):
        return lax.ppermute(block, "z", ring(8, -1))

    def swap(block):
        return lax.ppermute(block, "c", ring(2, 1))

    then = lax.optimization_barrier
    other, field = then((lax.ppermute(own, "xl", ring(2, 1)), field))
    pair = jnp.concatenate([jnp.where(xl == 0, own, other), jnp.where(xl == 0, other, own)], axis=0)
    right1, left1 = right(pair), left(pair)
    next_r, pair_s = then((right1, swap(pair)))
    right2, left2 = right(next_r), left(left1)
    next_r, right1_s = then((right2, swap(right1)))
    next_l, left1_s = then((left2, swap(left1)))
    right3, left3 = right(next_r), left(next_l)
    next_r, right2_s = then((right3, swap(right2)))
    next_l, left2_s = then((left3, swap(left2)))
    far = jnp.concatenate([right(next_r[:16]), left(next_l[16:])], axis=0)
    here = [pair, right1, left1, right2, left2, right3, left3, far]
    return here + [pair_s, right1_s, left1_s, right2_s, left2_s, swap(right3), swap(left3), swap(far)], field


OFFSETS = (0, -1, 1, -2, 2, -3, 3, 4)


def products_kernel(place_ref, *refs):
    blocks, (field_ref, home_ref, out_ref, panel_ref, acc, corner, sems) = refs[:16], refs[16:]
    z, core = place_ref[1], place_ref[2]
    copies = []
    for half in range(2):
        points = pl.ds(half * 1024, 1024)
        for flip in range(2):
            for k, offset in enumerate(OFFSETS):
                first = (((z + offset) & 7) * 2 + (core ^ flip)) * 16
                target = panel_ref.at[:, pl.ds(pl.multiple_of(first, 16), 16), points]
                copies.append(pltpu.make_async_copy(blocks[flip * 8 + k].at[:, :, points], target, sems.at[len(copies)]))
                copies[-1].start()
    long = pl.ds(pl.multiple_of((1 - core) * 128, 128), 128)
    short = pl.ds(pl.multiple_of(core * 128, 128), 128)
    acc[...] = jnp.zeros_like(acc)
    corner[...] = jnp.zeros_like(corner)

    def chunk(i, _):
        points = pl.ds(pl.multiple_of(i * 512, 512), 512)
        rows = jnp.concatenate([panel_ref[1, long, points], field_ref[:, points]], axis=0)
        acc[:, 256:512] += dot_nt(rows, panel_ref[1, :, points])
        low = dot_nt(jnp.concatenate([rows, panel_ref[0, short, points]], axis=0), panel_ref[0, :, points])
        acc[:, 0:256] += low[0:256]
        corner[...] += low[256:384]
        return 0

    homes = []
    for half in range(2):
        for copy in copies[half * 16 : half * 16 + 16]:
            copy.wait()
        for part in range(8):
            place = (slice(None), pl.ds(part * 32, 32), pl.ds(half * 1024, 1024))
            homes.append(pltpu.make_async_copy(panel_ref.at[place], home_ref.at[place], sems.at[32 + len(homes)]))
            homes[-1].start()
        lax.fori_loop(half * 2, half * 2 + 2, chunk, 0)
    for s in range(8):
        rows = slice(s * 16, s * 16 + 16)
        out_ref[s, :, 0:384] = acc[rows, 0:384]
        out_ref[s, :, 384:512] = jnp.where(core == 0, acc[rows, 384:512], corner[rows, 128:256])
        out_ref[s, :, 512:640] = corner[rows, 0:128]
        out_ref[s, :, 640:1152] = acc[128 + s * 16 : 128 + s * 16 + 16, :]
    for copy in homes:
        copy.wait()


def products(place, blocks, field):
    panel, terms = pl.pallas_call(
        products_kernel,
        in_specs=[pl.BlockSpec(memory_space=pltpu.SMEM)]
        + [pl.BlockSpec(memory_space=pl.ANY)] * 16
        + [pl.BlockSpec(memory_space=pltpu.VMEM)],
        out_shape=(jax.ShapeDtypeStruct((2, 256, 2048), jnp.float32), jax.ShapeDtypeStruct((8, 16, 1152), jnp.float32)),
        out_specs=(pl.BlockSpec(memory_space=pl.ANY), pl.BlockSpec(memory_space=pltpu.VMEM)),
        scratch_shapes=[
            pltpu.VMEM((2, 256, 2048), jnp.float32),
            pltpu.VMEM((256, 512), jnp.float32),
            pltpu.VMEM((128, 256), jnp.float32),
            pltpu.SemaphoreType.DMA((48,)),
        ],
        compiler_params=pltpu.CompilerParams(vmem_limit_bytes=BIG * MIB),
    )(place, *(block.reshape(2, 16, 2048) for block in blocks), field)
    return panel.reshape(PANEL, 2048), terms


def total_of(terms):
    while len(terms) > 1:
        terms = [terms[i] + terms[i + 1] for i in range(0, len(terms), 2)]
    return terms[0]


def eliminate(block):
    rows = lax.broadcasted_iota(jnp.int32, (8, 128), 0)
    lanes = lax.broadcasted_iota(jnp.int32, (8, 128), 1)

    def spread_row(tile, i):
        return jnp.broadcast_to(tile[i : i + 1, :], (8, 128))

    def spread_lane(tile, j):
        return jnp.broadcast_to(tile[:, j : j + 1], (8, 128))

    left = [block[8 * t : 8 * t + 8, :] for t in range(16)]
    right = [jnp.where(lanes == rows + 8 * t, 1.0, 0.0).astype(jnp.float32) for t in range(16)]
    out = []
    for t0 in range(16):
        columns = [spread_lane(left[t0], 8 * t0 + j) for j in range(8)]
        corner = [[spread_row(columns[j], i) for j in range(i + 1)] for i in range(8)]
        row_l = [spread_row(left[t0], i) for i in range(8)]
        row_r = [spread_row(right[t0], i) for i in range(8)]
        inverse, factor = [None] * 8, [[None] * 8 for _ in range(8)]
        for j in range(8):
            inverse[j] = 1.0 / corner[j][j]
            for i in range(j + 1, 8):
                factor[i][j] = corner[i][j] * inverse[j]
            for i in range(j + 1, 8):
                for k in range(j + 1, i + 1):
                    corner[i][k] = corner[i][k] - factor[i][j] * corner[k][j]
                row_l[i] = row_l[i] - factor[i][j] * row_l[j]
                row_r[i] = row_r[i] - factor[i][j] * row_r[j]
        own, pivot = row_r[0], corner[0][0]
        for i in range(1, 8):
            own, pivot = jnp.where(rows == i, row_r[i], own), jnp.where(rows == i, corner[i][i], pivot)
        root = lax.rsqrt(pivot)
        root = root * (1.5 - 0.5 * pivot * root * root)
        out.append(own * root)
        if t0 == 15:
            break
        solved_l, solved_r = [None] * 8, [None] * 8
        for k in range(7, -1, -1):
            u, v = row_l[k] * inverse[k], row_r[k] * inverse[k]
            for i in range(7, k, -1):
                u, v = u - factor[i][k] * solved_l[i], v - factor[i][k] * solved_r[i]
            solved_l[k], solved_r[k] = u, v
        for t in range(t0 + 1, 16):
            weights = [spread_lane(left[t], 8 * t0 + j) for j in range(8)]
            left[t] = left[t] - total_of([weights[j] * solved_l[j] for j in range(8)])
            right[t] = right[t] - total_of([weights[j] * solved_r[j] for j in range(8)])
    return jnp.concatenate(out, axis=0)


def invert(pieces, core, work, inv_ref):
    for flip, ref in enumerate(pieces):
        owner = core ^ flip
        for s in range(8):
            tile = ref[s] * (1.0 / POINTS)
            work[pl.ds(pl.multiple_of((3 - owner) * 128 + s * 16, 16), 16), 0:384] = tile[:, 0:384]
            square = pl.multiple_of((3 - 2 * owner) * 128, 128)
            work[pl.ds(pl.multiple_of(square + s * 16, 16), 16), pl.ds(square, 128)] = tile[:, 384:512]
            work[pl.ds(pl.multiple_of(owner * 128 + s * 16, 16), 16), 0:128] = tile[:, 512:640]
    inv_ref[...] = jnp.zeros_like(inv_ref)

    def diagonal(k, _):
        here = pl.ds(pl.multiple_of(k * 128, 128), 128)
        corner = eliminate(work[here, here])
        for kk in range(4):

            @pl.when(k == kk)
            def _(kk=kk, corner=corner):
                low, high = kk * 128, kk * 128 + 128
                if kk:
                    inv_ref[low:high, :low] = dot_nn(corner, inv_ref[low:high, :low])
                inv_ref[low:high, low:high] = corner
                if high < PANEL:
                    panel = dot_nt(work[high:, low:high], corner)
                    work[high:, high:] -= dot_nt(panel, panel)
                    inv_ref[high:, :high] -= dot_nn(panel, inv_ref[low:high, :high])

        return 0

    lax.fori_loop(0, 4, diagonal, 0)


def update_kernel(place_ref, sums_ref, by_core_ref, panel_ref, field_ref, out_ref, *scratch):
    work, inverse, coupling, mixer, held, sems = scratch
    xl, z, core = place_ref[0], place_ref[1], place_ref[2]

    @pl.when(pl.program_id(0) == 0)
    def _():
        copies = []
        for part in range(8):
            rows = pl.ds(part * 64, 64)
            copies.append(pltpu.make_async_copy(panel_ref.at[rows, :], held.at[rows, :], sems.at[part]))
            copies[-1].start()
        invert((sums_ref, by_core_ref), core, work, inverse)
        for s in range(8):
            coupling[s * 16 : s * 16 + 16, :] = sums_ref[s, :, 640:1152] * (1.0 / POINTS)
        factor = inverse[...]
        mixer[...] = -dot_nn(dot_nt(coupling[...], factor), factor)
        own = xl * 16 + z * 2 + core
        mixer[0:16, :] = inverse[pl.ds(pl.multiple_of(own * 16, 16), 16), :]
        for copy in copies:
            copy.wait()

    keep = lax.broadcasted_iota(jnp.int32, (128, 1024), 0) >= 16
    points = pl.ds(pl.multiple_of(pl.program_id(0) * 1024, 1024), 1024)
    moved = (dot_nn(mixer[...], held[:, points]) + jnp.where(keep, field_ref[...], 0.0)).T
    for low in range(4):
        for xp in range(4):
            for yh in range(2):
                first = low * 256 + xp * 64 + yh * 32
                out_ref[xp, yh, low] = moved[first : first + 32, :]


def update(place, sums, by_core, panel, field):
    out = pl.pallas_call(
        update_kernel,
        grid=(2,),
        in_specs=[
            pl.BlockSpec(memory_space=pltpu.SMEM),
            pl.BlockSpec((8, 16, 1152), lambda i: (0, 0, 0)),
            pl.BlockSpec((8, 16, 640), lambda i: (0, 0, 0)),
            pl.BlockSpec(memory_space=pl.ANY),
            pl.BlockSpec((128, 1024), lambda i: (0, i)),
        ],
        out_specs=pl.BlockSpec((4, 2, 4, 32, 128), lambda i: (0, 0, i, 0, 0)),
        out_shape=jax.ShapeDtypeStruct((4, 2, 8, 32, 128), jnp.float32),
        scratch_shapes=[pltpu.VMEM((PANEL, PANEL), jnp.float32)] * 2
        + [pltpu.VMEM((128, PANEL), jnp.float32)] * 2
        + [pltpu.VMEM((PANEL, 2048), jnp.float32), pltpu.SemaphoreType.DMA((8,))],
        compiler_params=pltpu.CompilerParams(vmem_limit_bytes=52 * MIB),
    )(place, sums, by_core, panel, field)
    return out.reshape(4, 16, 32, 128)


def per_device(orbitals, potential):
    xl, z, core = lax.axis_index("xl"), lax.axis_index("z"), lax.axis_index("c")
    place = jnp.stack([xl, z, core]).astype(jnp.int32)
    received = lax.all_to_all(pack(orbitals, potential), SPACE, 0, 0, tiled=True)
    back = lax.all_to_all(chebyshev(received), SPACE, 0, 0, tiled=True)
    blocks, field = gather_panel(turn(back, 1), turn(back, 8), xl)
    panel, terms = products(place, blocks, field)
    mine = jnp.sum(lax.all_to_all(terms, SPACE, 0, 0, tiled=True), axis=0)
    sums = lax.all_to_all(jnp.broadcast_to(mine, (8, 16, 1152)), SPACE, 0, 0, tiled=True)
    by_core = lax.ppermute(sums[:, :, :640], "c", ring(2, 1))
    return update(place, sums, by_core, panel, field)


def solution(mesh):
    fine = Mesh(mesh.devices.reshape(4, 2, 2, 8, 2), ("y", "xh", "xl", "z", "c"))
    return jax.shard_map(
        per_device,
        mesh=fine,
        in_specs=(P(SPACE, None, None, ("xl", "z", "c")), P(SPACE, None, None)),
        out_specs=P(SPACE, None, None, ("xl", "z", "c")),
        check_vma=False,
    )
```
